32 devices in a mesh: dev: 32 (over z, y, x, core).
Axes of the slice: x: 2, y: 2, z: 4, core: 2. Of those that a mesh axis runs over, the one named last changes fastest.
Arguments:
- tokens: bfloat16 [12288, 1024], P('dev'), may hold values from -6 to 6
- cotangent: bfloat16 [12288, 1024], P('dev'), may hold values from -6 to 6
- image_lengths: int32 [12], replicated, may hold values from 1 to 1370, 12288 in all
- ln1_gain: bfloat16 [1024], P('dev'), may hold values from 0.5 to 1.5
- ln1_bias: bfloat16 [1024], P('dev'), may hold values from -1.75 to 1.75
- qkv_weight: bfloat16 [1024, 3072], P('dev'), may hold values from -0.1875 to 0.1875
- qv_bias: bfloat16 [2048], P('dev'), may hold values from -1.75 to 1.75
- proj_weight: bfloat16 [1024, 1024], P('dev'), may hold values from -1 to 1
- proj_bias: bfloat16 [1024], P('dev'), may hold values from -1.75 to 1.75
- scale_attn: bfloat16 [1024], P('dev'), may hold values from 0.5 to 2
- ln2_gain: bfloat16 [1024], P('dev'), may hold values from 0.5 to 1.5
- ln2_bias: bfloat16 [1024], P('dev'), may hold values from -1.75 to 1.75
- fc1_weight: bfloat16 [1024, 4096], P('dev'), may hold values from -0.1875 to 0.1875
- fc1_bias: bfloat16 [4096], P('dev'), may hold values from -1.75 to 1.75
- fc2_weight: bfloat16 [4096, 1024], P('dev'), may hold values from -0.09375 to 0.09375
- fc2_bias: bfloat16 [1024], P('dev'), may hold values from -1.75 to 1.75
- scale_mlp: bfloat16 [1024], P('dev'), may hold values from 0.5 to 2
Outputs:
- block_out: bfloat16 [12288, 1024], P('dev')
- grad_tokens: bfloat16 [12288, 1024], P('dev')
- grad_ln1_gain: float32 [1024], P('dev')
- grad_ln1_bias: float32 [1024], P('dev')
- grad_qkv_weight: float32 [1024, 3072], P('dev')
- grad_qv_bias: float32 [2048], P('dev')
- grad_proj_weight: float32 [1024, 1024], P('dev')
- grad_proj_bias: float32 [1024], P('dev')
- grad_scale_attn: float32 [1024], P('dev')
- grad_ln2_gain: float32 [1024], P('dev')
- grad_ln2_bias: float32 [1024], P('dev')
- grad_fc1_weight: float32 [1024, 4096], P('dev')
- grad_fc1_bias: float32 [4096], P('dev')
- grad_fc2_weight: float32 [4096, 1024], P('dev')
- grad_fc2_bias: float32 [1024], P('dev')
- grad_scale_mlp: float32 [1024], P('dev')
The draws below stay inside these ranges and needn't reach their ends.
Inputs may be any that keep to these rules, and one draw needn't show every extreme that they name: `image_lengths`: they sum to 12288; the longest image has exactly 1370 tokens.
All inputs are finite; a program needn't handle non-finite values.
Results may differ from the reference program's by a relative error of at most 0.011.
Values may be sent and summed in bfloat16 or wider, within the bound.
No kernel may reach another device: no remote copies, remote signals or barrier semaphores. Data moves between devices by JAX's collectives and lax.ppermute only.
A program may use at most 192 MiB of HBM per device.

```python
import math
import jax
import jax.numpy as jnp
import numpy as np
from jax import lax

D = 1024
HEADS = 16
HD = 64
FF = 4096
SEQ = 1370
TOK_DEV = 384
TOKENS = 12288
IMAGES = 12


def strengthened(drawn, own_key, source, target, blocks, factor):
    def block_of(dim):
        return (jnp.arange(drawn.shape[dim]) // (drawn.shape[dim] // blocks)).reshape((-1,) + (1,) * (drawn.ndim - 1 - dim))

    one_side = jax.random.permutation(own_key, blocks)[block_of(target)]
    far = (block_of(target) + blocks // 2) % blocks
    return jnp.where((block_of(source) == one_side) | (block_of(source) == far), factor * drawn, drawn)


def shard_levels(stream_key, dims, cuts, least, top_value):
    def one(dim, parts):
        steps = jax.random.uniform(jax.random.fold_in(jax.random.fold_in(stream_key, 6), dim), (parts,), jnp.float32, least / len(cuts), top_value / len(cuts))
        return jnp.repeat(jnp.exp(steps), dims[dim] // parts).reshape((-1,) + (1,) * (len(dims) - dim - 1))

    factor_of = one(*cuts[0])
    for cut in cuts[1:]:
        factor_of = factor_of * one(*cut)
    return factor_of


def length_profile(amount, total, most, skew):
    loads = [(1 << 20) // math.isqrt(rank ** skew) + 1 for rank in range(2, amount + 1)]
    spare, given = total - most - (amount - 1), [1] * (amount - 1)
    while spare > 0:
        movable = [i for i in range(amount - 1) if given[i] < most]
        pool, budget = sum([loads[i] for i in movable]), spare
        for i in movable:
            addition = min(most - given[i], max(1, budget * loads[i] // pool), spare)
            given[i] = given[i] + addition
            spare = spare - addition
    return np.array([most] + given)


def uneven(own_key, amount, total, most, lean):
    if amount == 2:
        one = jax.random.randint(own_key, (), max(1, total - most), min(most, total - 1) + 1)
        return jnp.stack([one, total - one])
    tallies = jnp.asarray(length_profile(amount, total, most, lean), jnp.int32)
    couples = (amount - 1) // 2
    giver, sink = tallies[1:1 + 2 * couples:2], tallies[2:2 + 2 * couples:2]
    slack = jnp.minimum(giver - 1, most - sink)
    passed = jax.random.randint(jax.random.fold_in(own_key, 1), (couples,), 0, 1 << 20) % (slack + 1)
    tallies = tallies.at[1:1 + 2 * couples:2].set(giver - passed).at[2:2 + 2 * couples:2].set(sink + passed)
    return tallies[jax.random.permutation(jax.random.fold_in(own_key, 2), amount)]


def bell_draw(key, dims, width, most, pieces=(), kind=jnp.bfloat16):
    factor_of = shard_levels(key, dims, pieces, -0.22, 0.18) if pieces else 1.0
    array = jax.random.normal(key, dims, jnp.float32) * width * factor_of
    return jnp.minimum(jnp.maximum(array, -most), most).astype(kind)


def noise_with(stream_key, extent, width, most, split, heavy, held_as=jnp.bfloat16):
    entries = width * jax.random.normal(stream_key, extent, jnp.float32)
    if split:
        entries = entries * shard_levels(stream_key, extent, split, -0.22, 0.18)
    return jnp.clip(strengthened(entries, jax.random.fold_in(stream_key, 3), *heavy), -most, most).astype(held_as)


def setup_inputs(seed: int = 0) -> dict:
    streams_of = jax.random.split(jax.random.key(seed), 18)
    return {
        "tokens": bell_draw(streams_of[0], (TOKENS, D), 1.0, 6.0, ((0, 32),)),
        "cotangent": noise_with(streams_of[1], (TOKENS, D), 1.0, 6.0, ((0, 32),), (0, 1, 32, 2.75)),
        "image_lengths": uneven(streams_of[2], IMAGES, TOKENS, SEQ, 0).astype(jnp.int32),
        "ln1_gain": jnp.clip(1.0 + 0.1 * jax.random.normal(streams_of[3], (D,), jnp.float32), 0.5, 1.5).astype(jnp.bfloat16),
        "ln1_bias": bell_draw(streams_of[4], (D,), 0.3, 1.75, ((0, 32),)),
        "qkv_weight": bell_draw(streams_of[5], (D, 3 * D), D ** -0.5, 0.1875, ((0, 32),)),
        "qv_bias": bell_draw(streams_of[6], (2 * D,), 0.3, 1.75, ((0, 32),)),
        "proj_weight": bell_draw(streams_of[7], (D, D), (D // 32) ** -0.5, 1.0, ((0, 32),)),
        "proj_bias": bell_draw(streams_of[8], (D,), 0.3, 1.75, ((0, 32),)),
        "scale_attn": jnp.clip(jnp.exp(math.log(2.0) - 1.3862944 * jax.random.uniform(streams_of[9], (D,), jnp.float32) ** shard_levels(streams_of[9], (D,), ((0, 32),), -0.2, 0.2)), 0.5, 2.0).astype(jnp.bfloat16),
        "ln2_gain": jnp.clip(1.0 + 0.1 * jax.random.normal(streams_of[10], (D,), jnp.float32), 0.5, 1.5).astype(jnp.bfloat16),
        "ln2_bias": bell_draw(streams_of[11], (D,), 0.3, 1.75, ((0, 32),)),
        "fc1_weight": bell_draw(streams_of[12], (D, FF), D ** -0.5, 0.1875, ((0, 32),)),
        "fc1_bias": bell_draw(streams_of[13], (FF,), 0.3, 1.75, ((0, 32),)),
        "fc2_weight": bell_draw(streams_of[14], (FF, D), FF ** -0.5, 0.09375, ((0, 32),)),
        "fc2_bias": bell_draw(streams_of[15], (D,), 0.3, 1.75, ((0, 32),)),
        "scale_mlp": jnp.clip(jnp.exp(math.log(2.0) - 1.3862944 * jax.random.uniform(streams_of[16], (D,), jnp.float32) ** shard_levels(streams_of[16], (D,), ((0, 32),), -0.2, 0.2)), 0.5, 2.0).astype(jnp.bfloat16),
    }


@jax.custom_vjp
def low(v):
    return lax.optimization_barrier(v.astype(jnp.bfloat16)).astype(jnp.float32)

@jax.custom_vjp
def low_back(v):
    return v

def low_keep(v):
    return (low(v), None)

def low_pass(kept, grad):
    return (grad,)

def back_keep(v):
    return (v, None)

def back_low(kept, grad):
    return (low(grad),)
low.defvjp(low_keep, low_pass)
low_back.defvjp(back_keep, back_low)
eps = 1e-06

def both_ways(value):
    return low_back(low(value))

def matmul(left, right):
    return jnp.dot(left, right, precision=lax.Precision.HIGHEST, preferred_element_type=jnp.float32)

def layer_norm(value, gain, shift):
    centre = value - lax.optimization_barrier(jnp.mean(value, axis=-1, keepdims=True))
    spread = lax.optimization_barrier(jnp.mean(centre * centre, axis=-1, keepdims=True))
    return centre * lax.rsqrt(spread + eps) * gain + shift

def attend(query, key, value, image_of):
    block = TOK_DEV
    reach = (SEQ + block - 2) // block
    margin = reach * block
    window = (2 * reach + 1) * block
    key_pad = jnp.pad(key, ((margin, margin), (0, 0)))
    value_pad = jnp.pad(value, ((margin, margin), (0, 0)))
    ids_pad = jnp.pad(image_of, (margin, margin), constant_values=-1)

    def one_block(index):
        start = (index * block).astype(jnp.int32)
        q_rows = lax.dynamic_slice_in_dim(query, start, block, 0).reshape(block, HEADS, HD)
        k_rows = lax.dynamic_slice_in_dim(key_pad, start, window, 0).reshape(window, HEADS, HD)
        v_rows = lax.dynamic_slice_in_dim(value_pad, start, window, 0).reshape(window, HEADS, HD)
        q_ids = lax.dynamic_slice_in_dim(image_of, start, block, 0)
        k_ids = lax.dynamic_slice_in_dim(ids_pad, start, window, 0)
        scores = jnp.einsum('qhd,khd->hqk', q_rows, k_rows, precision=lax.Precision.HIGHEST) * 0.125
        scores = low_back(scores)
        same = q_ids[:, None] == k_ids[None, :]
        scores = jnp.where(same[None], scores, -1e+30)
        top = lax.optimization_barrier(jnp.max(scores, axis=-1, keepdims=True))
        expo = jnp.exp(scores - top)
        prob = low(expo / lax.optimization_barrier(jnp.sum(expo, axis=-1, keepdims=True)))
        out = jnp.einsum('hqk,khd->qhd', prob, v_rows, precision=lax.Precision.HIGHEST)
        return out.reshape(block, D)
    blocks = lax.map(jax.checkpoint(one_block), jnp.arange(TOKENS // block, dtype=jnp.int32))
    return blocks.reshape(TOKENS, D)

def reference(tokens, cotangent, image_lengths, ln1_gain, ln1_bias, qkv_weight, qv_bias, proj_weight, proj_bias, scale_attn, ln2_gain, ln2_bias, fc1_weight, fc1_bias, fc2_weight, fc2_bias, scale_mlp):
    ends = jnp.cumsum(image_lengths).astype(jnp.int32)
    places = jnp.arange(TOKENS, dtype=jnp.int32)
    image_of = lax.optimization_barrier(jnp.sum((places[:, None] >= ends[None, :]).astype(jnp.int32), axis=1)).astype(jnp.int32)

    def forward(x, g1, b1, w_qkv, b_qv, w_proj, b_proj, s_attn, g2, b2, w_fc1, b_fc1, w_fc2, b_fc2, s_mlp):
        norm1 = low(layer_norm(x, g1, b1))
        qkv = matmul(norm1, w_qkv)
        query = both_ways(qkv[:, :D] + b_qv[:D])
        key = both_ways(qkv[:, D:2 * D])
        value = both_ways(qkv[:, 2 * D:] + b_qv[D:])
        mixed = both_ways(attend(query, key, value, image_of))
        branch = low_back(matmul(mixed, w_proj)) + b_proj
        hidden = x + s_attn * branch
        norm2 = low(layer_norm(hidden, g2, b2))
        pre = low_back(matmul(norm2, w_fc1)) + b_fc1
        act = low(jax.nn.gelu(pre, approximate=False))
        mlp = low_back(matmul(act, w_fc2)) + b_fc2
        return hidden + s_mlp * mlp
    params = (tokens, ln1_gain, ln1_bias, qkv_weight, qv_bias, proj_weight, proj_bias, scale_attn, ln2_gain, ln2_bias, fc1_weight, fc1_bias, fc2_weight, fc2_bias, scale_mlp)
    params = tuple((item.astype(jnp.float32) for item in params))
    result, pullback = jax.vjp(forward, *params)
    grads = pullback(cotangent.astype(jnp.float32))
    return (result.astype(jnp.bfloat16), grads[0].astype(jnp.bfloat16), grads[1], grads[2], grads[3], grads[4], grads[5], grads[6], grads[7], grads[8], grads[9], grads[10], grads[11], grads[12], grads[13], grads[14])
```

```python
import jax
import jax.numpy as jnp
from jax import lax
from jax.sharding import PartitionSpec as P
from jax.experimental import pallas as pl
from jax.experimental.pallas import tpu as pltpu

BQ = 256
BK = 256
HD = 64
LOG2E = 1.4426950408889634
SCALE = 0.125
MASKED = -1e30
NT = (((1,), (1,)), ((), ()))


def rows_of(ref, block, size):
    return ref[pl.ds(pl.multiple_of(block * size, size), size), :]


def head_halves(block):
    first = lax.broadcasted_iota(jnp.int32, block.shape, 1) < HD
    zero = jnp.zeros_like(block)
    return jnp.where(first, block, zero), jnp.where(first, zero, block)


def transpose_into(target, source):
    for j in range(source.shape[0] // BK):
        part = source[j * BK : (j + 1) * BK, :].astype(jnp.float32)
        target[:, j * BK : (j + 1) * BK] = part.T.astype(target.dtype)


def forward_kernel(low, high, seg, q_ref, k_ref, v_ref, o_ref, lse_ref, v_t):
    step = pl.program_id(0)

    @pl.when(step == 0)
    def _():
        transpose_into(v_t, v_ref)

    q_heads = head_halves(q_ref[...])
    begin, end = seg[0:1, :], seg[1:2, :]
    place = lax.broadcasted_iota(jnp.int32, (BK, BQ), 0)

    def one_block(j, carry):
        keys = rows_of(k_ref, j, BK)
        at = place + j * BK
        valid = (at >= begin) & (at < end)
        out = []
        for h in range(2):
            top, total, acc = carry[h]
            s = lax.dot_general(keys, q_heads[h], NT, preferred_element_type=jnp.float32)
            s = jnp.where(valid, s * (SCALE * LOG2E), MASKED)
            new_top = jnp.maximum(top, jnp.max(s, axis=0, keepdims=True))
            p = jnp.exp2(s - new_top)
            fade = jnp.exp2(top - new_top)
            total = total * fade + jnp.sum(p, axis=0, keepdims=True)
            v_part = v_t[h * HD : (h + 1) * HD, pl.ds(pl.multiple_of(j * BK, BK), BK)]
            acc = acc * fade + jnp.dot(v_part, p.astype(jnp.bfloat16), preferred_element_type=jnp.float32)
            out.append((new_top, total, acc))
        return tuple(out)

    start = (
        jnp.full((1, BQ), MASKED, jnp.float32),
        jnp.zeros((1, BQ), jnp.float32),
        jnp.zeros((HD, BQ), jnp.float32),
    )
    done = lax.fori_loop(low[step], high[step], one_block, (start, start))
    outs = jnp.concatenate([acc / total for _, total, acc in done], axis=0)
    o_ref[...] = outs.T.astype(o_ref.dtype)
    for h in range(2):
        top, total, _ = done[h]
        lse_ref[h : h + 1, :] = top + jnp.log2(total)


def backward_kernel(
    low, high, seg, q_ref, k_ref, v_ref, o_ref, do_ref, lse_ref, dq_ref, mid_ref, edge_ref, k_t, dk, dv, dq_t
):
    step = pl.program_id(0)

    @pl.when(step == 0)
    def _():
        transpose_into(k_t, k_ref)
        dk[...] = jnp.zeros_like(dk)
        dv[...] = jnp.zeros_like(dv)

    q_heads = head_halves(q_ref[...])
    do_heads = head_halves(do_ref[...])
    q_both = jnp.concatenate(q_heads, axis=0)
    do_both = jnp.concatenate(do_heads, axis=0)
    prod = (do_ref[...].astype(jnp.float32) * o_ref[...].astype(jnp.float32)).T
    begin, end = seg[0:1, :], seg[1:2, :]
    place = lax.broadcasted_iota(jnp.int32, (BK, BQ), 0)
    centre = [jnp.sum(prod[h * HD : (h + 1) * HD], axis=0, keepdims=True) for h in range(2)]
    lse = [lse_ref[h : h + 1, :] for h in range(2)]
    dq_t[...] = jnp.zeros_like(dq_t)

    @pl.loop(low[step], high[step])
    def _(j):
        rows = pl.ds(pl.multiple_of(j * BK, BK), BK)
        keys, values = k_ref[rows, :], v_ref[rows, :]
        at = place + j * BK
        valid = (at >= begin) & (at < end)
        ps, dss = [], []
        for h in range(2):
            s = lax.dot_general(keys, q_heads[h], NT, preferred_element_type=jnp.float32)
            p = jnp.where(valid, jnp.exp2(s * (SCALE * LOG2E) - lse[h]), 0.0)
            dp = lax.dot_general(values, do_heads[h], NT, preferred_element_type=jnp.float32)
            ds = (p * (dp - centre[h])).astype(jnp.bfloat16)
            ps.append(p.astype(jnp.bfloat16))
            dss.append(ds)
            part = slice(h * HD, (h + 1) * HD)
            dq_t[part, :] += jnp.dot(k_t[part, rows], ds, preferred_element_type=jnp.float32)
        dv[rows, :] += jnp.dot(jnp.concatenate(ps, axis=1), do_both, preferred_element_type=jnp.float32)
        dk[rows, :] += jnp.dot(jnp.concatenate(dss, axis=1), q_both, preferred_element_type=jnp.float32)

    dq_ref[...] = (dq_t[...] * SCALE).T.astype(dq_ref.dtype)

    @pl.when(step == pl.num_programs(0) - 1)
    def _():
        halo = edge_ref.shape[1]
        span = mid_ref.shape[0]
        for j in range(dk.shape[0] // BK):
            part = slice(j * BK, (j + 1) * BK)
            both = jnp.concatenate([dk[part] * SCALE, dv[part]], axis=1)
            if j * BK < halo:
                edge_ref[0, part, :] = both.astype(edge_ref.dtype)
            elif j * BK < halo + span:
                mid_ref[j * BK - halo : (j + 1) * BK - halo, :] = both
            else:
                first = j * BK - halo - span
                edge_ref[1, first : first + BK, :] = both.astype(edge_ref.dtype)


def attention_forward(low, high, seg, q, k, v):
    span, width = q.shape
    window = k.shape[0]
    steps = span // BQ
    whole = pl.BlockSpec((window, width), lambda i, *_: (0, 0))
    rows = pl.BlockSpec((BQ, width), lambda i, *_: (i, 0))
    return pl.pallas_call(
        forward_kernel,
        out_shape=(
            jax.ShapeDtypeStruct((span, width), jnp.bfloat16),
            jax.ShapeDtypeStruct((8, span), jnp.float32),
        ),
        grid_spec=pltpu.PrefetchScalarGridSpec(
            num_scalar_prefetch=2,
            grid=(steps,),
            in_specs=[pl.BlockSpec((2, BQ), lambda i, *_: (0, i)), rows, whole, whole],
            out_specs=[rows, pl.BlockSpec((8, BQ), lambda i, *_: (0, i))],
            scratch_shapes=[pltpu.VMEM((width, window), jnp.bfloat16)],
        ),
        compiler_params=pltpu.CompilerParams(vmem_limit_bytes=40 << 20),
        cost_estimate=pl.CostEstimate(flops=16 * span * 1536 * 128, bytes_accessed=8 << 20, transcendentals=2 * span * 1536),
        name="attention_forward",
    )(low, high, seg, q, k, v)


def attention_backward(low, high, seg, q, k, v, o, do, lse, halo):
    span, width = q.shape
    window = k.shape[0]
    steps = span // BQ
    whole = pl.BlockSpec((window, width), lambda i, *_: (0, 0))
    rows = pl.BlockSpec((BQ, width), lambda i, *_: (i, 0))
    return pl.pallas_call(
        backward_kernel,
        out_shape=(
            jax.ShapeDtypeStruct((span, width), jnp.bfloat16),
            jax.ShapeDtypeStruct((span, 2 * width), jnp.float32),
            jax.ShapeDtypeStruct((2, halo, 2 * width), jnp.bfloat16),
        ),
        grid_spec=pltpu.PrefetchScalarGridSpec(
            num_scalar_prefetch=2,
            grid=(steps,),
            in_specs=[
                pl.BlockSpec((2, BQ), lambda i, *_: (0, i)), rows, whole, whole, rows, rows,
                pl.BlockSpec((8, BQ), lambda i, *_: (0, i)),
            ],
            out_specs=[
                rows,
                pl.BlockSpec((span, 2 * width), lambda i, *_: (0, 0)),
                pl.BlockSpec((2, halo, 2 * width), lambda i, *_: (0, 0, 0)),
            ],
            scratch_shapes=[
                pltpu.VMEM((width, window), jnp.bfloat16),
                pltpu.VMEM((window, width), jnp.float32),
                pltpu.VMEM((window, width), jnp.float32),
                pltpu.VMEM((width, BQ), jnp.float32),
            ],
        ),
        compiler_params=pltpu.CompilerParams(vmem_limit_bytes=48 << 20),
        cost_estimate=pl.CostEstimate(flops=40 * span * 1536 * 128, bytes_accessed=16 << 20, transcendentals=2 * span * 1536),
        name="attention_backward",
    )(low, high, seg, q, k, v, o, do, lse)


HEADS = 16
SEQ = 1370
GROUP = 8
EPS = 1e-06
F32, BF16 = jnp.float32, jnp.bfloat16


def mm(left, right):
    return jnp.dot(left, right, preferred_element_type=F32)


def mm_t(left, right):
    return jnp.einsum("tf,df->td", left, right, preferred_element_type=F32)


def t_mm(left, right):
    return jnp.einsum("td,tf->df", left, right, preferred_element_type=F32)


def normalised(value):
    centre = value - jnp.mean(value, axis=-1, keepdims=True)
    rstd = lax.rsqrt(jnp.mean(centre * centre, axis=-1, keepdims=True) + EPS)
    return centre * rstd, rstd


def norm_back(unit, rstd, grad):
    first = jnp.mean(grad, axis=-1, keepdims=True)
    second = jnp.mean(grad * unit, axis=-1, keepdims=True)
    return rstd * (grad - first - unit * second)


def gelu_parts(z):
    half = 0.5 * (1.0 + lax.erf(z * 0.7071067811865476))
    slope = half + z * (0.3989422804014327 * jnp.exp(-0.5 * z * z))
    return z * half, slope


def groups_of(count):
    return [list(range(first, first + GROUP)) for first in range(0, count, GROUP)]


def gathered(shard):
    return lax.all_gather(shard, "dev", axis=0, tiled=True)


def scattered(whole):
    return lax.psum_scatter(whole, "dev", scatter_dimension=0, tiled=True)


def pack(vectors, count):
    return jnp.concatenate([v.reshape(count, -1) for v in vectors], axis=1)


def unpack(packed, sizes):
    out, at = [], 0
    for size in sizes:
        out.append(packed[:, at : at + size].reshape(-1))
        at += size
    return out


def to_heads(parts, devices):
    rows = parts[0].shape[0]
    sent = jnp.stack([p.reshape(rows, GROUP, -1) for p in parts], axis=2)
    sent = sent.transpose(1, 0, 2, 3)
    back = lax.all_to_all(sent, "dev", 0, 0, axis_index_groups=groups_of(devices), tiled=True)
    return [back[:, :, i].reshape(GROUP * rows, -1) for i in range(len(parts))]


def to_tokens(parts, devices):
    rows = parts[0].shape[0] // GROUP
    sent = jnp.stack([p.reshape(GROUP, rows, -1) for p in parts], axis=2)
    back = lax.all_to_all(sent, "dev", 0, 0, axis_index_groups=groups_of(devices), tiled=True)
    return [back[:, :, i].transpose(1, 0, 2).reshape(rows, -1) for i in range(len(parts))]


def shifted(shard, by, devices):
    pairs = [(i, i + by) for i in range(devices) if 0 <= i + by < devices]
    return lax.ppermute(shard, "dev", pairs)


def body(
    tokens,
    cotangent,
    image_lengths,
    ln1_gain,
    ln1_bias,
    qkv_weight,
    qv_bias,
    proj_weight,
    proj_bias,
    scale_attn,
    ln2_gain,
    ln2_bias,
    fc1_weight,
    fc1_bias,
    fc2_weight,
    fc2_bias,
    scale_mlp,
):
    devices = lax.axis_size("dev")
    me = lax.axis_index("dev")
    rows, width = tokens.shape
    vectors = (
        ln1_gain, ln1_bias, qv_bias, proj_bias, scale_attn, ln2_gain, ln2_bias, fc1_bias, fc2_bias, scale_mlp,
    )
    sizes = [v.shape[0] for v in vectors]
    packed = gathered(pack(vectors, 1)).astype(F32)
    gain1, shift1, bias_qv, bias_proj, layer_attn, gain2, shift2, bias_fc1, bias_fc2, layer_mlp = unpack(packed, sizes)
    w_qkv = gathered(qkv_weight)
    w_proj = gathered(proj_weight)
    w_fc1 = gathered(fc1_weight)
    w_fc2 = gathered(fc2_weight)

    span = GROUP * rows
    halo = -(-(SEQ - 1) // BK) * BK
    base = (me // GROUP) * span - halo
    places = base + halo + jnp.arange(span, dtype=jnp.int32)
    ends = jnp.cumsum(image_lengths)
    before = ends[None, :] <= places[:, None]
    begin = jnp.max(jnp.where(before, ends[None, :], 0), axis=1)
    finish = jnp.min(jnp.where(before, devices * rows, ends[None, :]), axis=1)
    seg = jnp.stack([begin - base, finish - base]).astype(jnp.int32)
    low = seg[0, ::BQ] // BK
    high = -(-seg[1, BQ - 1 :: BQ] // BK)

    x = tokens.astype(F32)
    u1, rstd1 = normalised(x)
    n1 = (u1 * gain1 + shift1).astype(BF16)
    qkv = mm(n1, w_qkv)
    q_mine = (qkv[:, :width] + bias_qv[:width]).astype(BF16)
    k_mine = qkv[:, width : 2 * width].astype(BF16)
    v_mine = (qkv[:, 2 * width :] + bias_qv[width:]).astype(BF16)
    q, k, v = to_heads([q_mine, k_mine, v_mine], devices)
    kv = jnp.concatenate([k, v], axis=1)
    left = shifted(kv[span - halo :], GROUP, devices)
    right = shifted(kv[:halo], -GROUP, devices)
    window = jnp.concatenate([left, kv, right], axis=0)
    k_win, v_win = window[:, : q.shape[1]], window[:, q.shape[1] :]
    o_heads, lse = attention_forward(low, high, seg, q, k_win, v_win)
    (o,) = to_tokens([o_heads], devices)

    branch = mm(o, w_proj) + bias_proj
    y1 = x + layer_attn * branch
    u2, rstd2 = normalised(y1)
    n2 = (u2 * gain2 + shift2).astype(BF16)
    act, slope = gelu_parts(mm(n2, w_fc1) + bias_fc1)
    act = act.astype(BF16)
    mlp = mm(act, w_fc2) + bias_fc2
    block_out = (y1 + layer_mlp * mlp).astype(BF16)

    g = cotangent.astype(F32)
    d_scale_mlp = jnp.sum(g * mlp, axis=0)
    dm = layer_mlp * g
    d_fc2_bias = jnp.sum(dm, axis=0)
    dml = dm.astype(BF16)
    d_fc2 = t_mm(act, dml)
    dz = mm_t(dml, w_fc2) * slope
    d_fc1_bias = jnp.sum(dz, axis=0)
    dzl = dz.astype(BF16)
    d_fc1 = t_mm(n2, dzl)
    dn2 = mm_t(dzl, w_fc1)
    d_gain2 = jnp.sum(dn2 * u2, axis=0)
    d_shift2 = jnp.sum(dn2, axis=0)
    dy1 = g + norm_back(u2, rstd2, dn2 * gain2)
    d_scale_attn = jnp.sum(dy1 * branch, axis=0)
    db = layer_attn * dy1
    d_proj_bias = jnp.sum(db, axis=0)
    dbl = db.astype(BF16)
    d_proj = t_mm(o, dbl)
    do = mm_t(dbl, w_proj).astype(BF16)

    (do_heads,) = to_heads([do], devices)
    dq, mid, edge = attention_backward(low, high, seg, q, k_win, v_win, o_heads, do_heads, lse, halo)
    from_right = shifted(edge[0], -GROUP, devices).astype(F32)
    from_left = shifted(edge[1], GROUP, devices).astype(F32)
    rest = span - halo
    mid = mid + jnp.pad(from_left, ((0, rest), (0, 0))) + jnp.pad(from_right, ((rest, 0), (0, 0)))
    mid = mid.astype(BF16)
    half = dq.shape[1]
    dq, dk, dv = to_tokens([dq, mid[:, :half], mid[:, half:]], devices)
    dqkv = jnp.concatenate([dq, dk, dv], axis=1)
    d_qv_bias = jnp.concatenate([jnp.sum(dq.astype(F32), axis=0), jnp.sum(dv.astype(F32), axis=0)])
    d_qkv = t_mm(n1, dqkv)
    dn1 = mm_t(dqkv, w_qkv)
    d_gain1 = jnp.sum(dn1 * u1, axis=0)
    d_shift1 = jnp.sum(dn1, axis=0)
    grad_tokens = (dy1 + norm_back(u1, rstd1, dn1 * gain1)).astype(BF16)

    small = (
        d_gain1, d_shift1, d_qv_bias, d_proj_bias, d_scale_attn, d_gain2, d_shift2, d_fc1_bias, d_fc2_bias, d_scale_mlp,
    )
    small = scattered(pack(small, devices))
    s_gain1, s_shift1, s_qv, s_proj, s_attn, s_gain2, s_shift2, s_fc1, s_fc2, s_mlp = unpack(small, sizes)
    return (
        block_out,
        grad_tokens,
        s_gain1,
        s_shift1,
        scattered(d_qkv),
        s_qv,
        scattered(d_proj),
        s_proj,
        s_attn,
        s_gain2,
        s_shift2,
        scattered(d_fc1),
        s_fc1,
        scattered(d_fc2),
        s_fc2,
        s_mlp,
    )


def solution(mesh):
    matrix, vector = P("dev", None), P("dev")
    return jax.shard_map(
        body,
        mesh=mesh,
        in_specs=(
            matrix, matrix, P(), vector, vector, matrix, vector, matrix, vector, vector, vector, vector, matrix,
            vector, matrix, vector, vector,
        ),
        out_specs=(
            matrix, matrix, vector, vector, matrix, vector, matrix, vector, vector, vector, vector, matrix, vector,
            matrix, vector, vector,
        ),
        check_vma=False,
    )
```

```python
import jax
import jax.numpy as jnp
from jax import lax
from jax.sharding import PartitionSpec as P
from jax.experimental import pallas as pl
from jax.experimental.pallas import tpu as pltpu

BQ = 256
BK = 256
HD = 64
LOG2E = 1.4426950408889634
SCALE = 0.125
MASKED = -1e30
NT = (((1,), (1,)), ((), ()))


def rows_of(ref, block, size):
    return ref[pl.ds(pl.multiple_of(block * size, size), size), :]


def head_halves(block):
    first = lax.broadcasted_iota(jnp.int32, block.shape, 1) < HD
    zero = jnp.zeros_like(block)
    return jnp.where(first, block, zero), jnp.where(first, zero, block)


def transpose_into(target, source):
    for j in range(source.shape[0] // BK):
        part = source[j * BK : (j + 1) * BK, :].astype(jnp.float32)
        target[:, j * BK : (j + 1) * BK] = part.T.astype(target.dtype)


def forward_kernel(low, high, seg, q_ref, k_ref, v_ref, o_ref, lse_ref, v_t):
    step = pl.program_id(0)

    @pl.when(step == 0)
    def _():
        transpose_into(v_t, v_ref)

    q_heads = head_halves(q_ref[...])
    begin, end = seg[0:1, :], seg[1:2, :]
    place = lax.broadcasted_iota(jnp.int32, (BK, BQ), 0)

    def one_block(j, carry):
        keys = rows_of(k_ref, j, BK)
        at = place + j * BK
        valid = (at >= begin) & (at < end)
        out = []
        for h in range(2):
            top, total, acc = carry[h]
            s = lax.dot_general(keys, q_heads[h], NT, preferred_element_type=jnp.float32)
            s = jnp.where(valid, s * (SCALE * LOG2E), MASKED)
            new_top = jnp.maximum(top, jnp.max(s, axis=0, keepdims=True))
            p = jnp.exp2(s - new_top)
            fade = jnp.exp2(top - new_top)
            total = total * fade + jnp.sum(p, axis=0, keepdims=True)
            v_part = v_t[h * HD : (h + 1) * HD, pl.ds(pl.multiple_of(j * BK, BK), BK)]
            acc = acc * fade + jnp.dot(v_part, p.astype(jnp.bfloat16), preferred_element_type=jnp.float32)
            out.append((new_top, total, acc))
        return tuple(out)

    start = (
        jnp.full((1, BQ), MASKED, jnp.float32),
        jnp.zeros((1, BQ), jnp.float32),
        jnp.zeros((HD, BQ), jnp.float32),
    )
    done = lax.fori_loop(low[step], high[step], one_block, (start, start))
    outs = jnp.concatenate([acc / total for _, total, acc in done], axis=0)
    o_ref[...] = outs.T.astype(o_ref.dtype)
    for h in range(2):
        top, total, _ = done[h]
        lse_ref[h : h + 1, :] = top + jnp.log2(total)


def backward_kernel(
    low, high, seg, q_ref, k_ref, v_ref, o_ref, do_ref, lse_ref, dq_ref, mid_ref, edge_ref, k_t, dk, dv, dq_t
):
    step = pl.program_id(0)

    @pl.when(step == 0)
    def _():
        transpose_into(k_t, k_ref)
        dk[...] = jnp.zeros_like(dk)
        dv[...] = jnp.zeros_like(dv)

    q_heads = head_halves(q_ref[...])
    do_heads = head_halves(do_ref[...])
    q_both = jnp.concatenate(q_heads, axis=0)
    do_both = jnp.concatenate(do_heads, axis=0)
    prod = (do_ref[...].astype(jnp.float32) * o_ref[...].astype(jnp.float32)).T
    begin, end = seg[0:1, :], seg[1:2, :]
    place = lax.broadcasted_iota(jnp.int32, (BK, BQ), 0)
    centre = [jnp.sum(prod[h * HD : (h + 1) * HD], axis=0, keepdims=True) for h in range(2)]
    lse = [lse_ref[h : h + 1, :] for h in range(2)]
    dq_t[...] = jnp.zeros_like(dq_t)

    @pl.loop(low[step], high[step])
    def _(j):
        rows = pl.ds(pl.multiple_of(j * BK, BK), BK)
        keys, values = k_ref[rows, :], v_ref[rows, :]
        at = place + j * BK
        valid = (at >= begin) & (at < end)
        ps, dss = [], []
        for h in range(2):
            s = lax.dot_general(keys, q_heads[h], NT, preferred_element_type=jnp.float32)
            p = jnp.where(valid, jnp.exp2(s * (SCALE * LOG2E) - lse[h]), 0.0)
            dp = lax.dot_general(values, do_heads[h], NT, preferred_element_type=jnp.float32)
            ds = (p * (dp - centre[h])).astype(jnp.bfloat16)
            ps.append(p.astype(jnp.bfloat16))
            dss.append(ds)
            part = slice(h * HD, (h + 1) * HD)
            dq_t[part, :] += jnp.dot(k_t[part, rows], ds, preferred_element_type=jnp.float32)
        dv[rows, :] += jnp.dot(jnp.concatenate(ps, axis=1), do_both, preferred_element_type=jnp.float32)
        dk[rows, :] += jnp.dot(jnp.concatenate(dss, axis=1), q_both, preferred_element_type=jnp.float32)

    dq_ref[...] = (dq_t[...] * SCALE).T.astype(dq_ref.dtype)

    @pl.when(step == pl.num_programs(0) - 1)
    def _():
        halo = edge_ref.shape[1]
        span = mid_ref.shape[0]
        for j in range(dk.shape[0] // BK):
            part = slice(j * BK, (j + 1) * BK)
            both = jnp.concatenate([dk[part] * SCALE, dv[part]], axis=1)
            if j * BK < halo:
                edge_ref[0, part, :] = both.astype(edge_ref.dtype)
            elif j * BK < halo + span:
                mid_ref[j * BK - halo : (j + 1) * BK - halo, :] = both
            else:
                first = j * BK - halo - span
                edge_ref[1, first : first + BK, :] = both.astype(edge_ref.dtype)


def attention_forward(low, high, seg, q, k, v):
    span, width = q.shape
    window = k.shape[0]
    steps = span // BQ
    whole = pl.BlockSpec((window, width), lambda i, *_: (0, 0))
    rows = pl.BlockSpec((BQ, width), lambda i, *_: (i, 0))
    return pl.pallas_call(
        forward_kernel,
        out_shape=(
            jax.ShapeDtypeStruct((span, width), jnp.bfloat16),
            jax.ShapeDtypeStruct((8, span), jnp.float32),
        ),
        grid_spec=pltpu.PrefetchScalarGridSpec(
            num_scalar_prefetch=2,
            grid=(steps,),
            in_specs=[pl.BlockSpec((2, BQ), lambda i, *_: (0, i)), rows, whole, whole],
            out_specs=[rows, pl.BlockSpec((8, BQ), lambda i, *_: (0, i))],
            scratch_shapes=[pltpu.VMEM((width, window), jnp.bfloat16)],
        ),
        compiler_params=pltpu.CompilerParams(vmem_limit_bytes=40 << 20),
        cost_estimate=pl.CostEstimate(flops=16 * span * 1536 * 128, bytes_accessed=8 << 20, transcendentals=2 * span * 1536),
        name="attention_forward",
    )(low, high, seg, q, k, v)


def attention_backward(low, high, seg, q, k, v, o, do, lse, halo):
    span, width = q.shape
    window = k.shape[0]
    steps = span // BQ
    whole = pl.BlockSpec((window, width), lambda i, *_: (0, 0))
    rows = pl.BlockSpec((BQ, width), lambda i, *_: (i, 0))
    return pl.pallas_call(
        backward_kernel,
        out_shape=(
            jax.ShapeDtypeStruct((span, width), jnp.bfloat16),
            jax.ShapeDtypeStruct((span, 2 * width), jnp.float32),
            jax.ShapeDtypeStruct((2, halo, 2 * width), jnp.bfloat16),
        ),
        grid_spec=pltpu.PrefetchScalarGridSpec(
            num_scalar_prefetch=2,
            grid=(steps,),
            in_specs=[
                pl.BlockSpec((2, BQ), lambda i, *_: (0, i)), rows, whole, whole, rows, rows,
                pl.BlockSpec((8, BQ), lambda i, *_: (0, i)),
            ],
            out_specs=[
                rows,
                pl.BlockSpec((span, 2 * width), lambda i, *_: (0, 0)),
                pl.BlockSpec((2, halo, 2 * width), lambda i, *_: (0, 0, 0)),
            ],
            scratch_shapes=[
                pltpu.VMEM((width, window), jnp.bfloat16),
                pltpu.VMEM((window, width), jnp.float32),
                pltpu.VMEM((window, width), jnp.float32),
                pltpu.VMEM((width, BQ), jnp.float32),
            ],
        ),
        compiler_params=pltpu.CompilerParams(vmem_limit_bytes=48 << 20),
        cost_estimate=pl.CostEstimate(flops=40 * span * 1536 * 128, bytes_accessed=16 << 20, transcendentals=2 * span * 1536),
        name="attention_backward",
    )(low, high, seg, q, k, v, o, do, lse)


HEADS = 16
SEQ = 1370
GROUP = 8
EPS = 1e-06
F32, BF16 = jnp.float32, jnp.bfloat16


def mm(left, right):
    return jnp.dot(left, right, preferred_element_type=F32)


def mm_t(left, right):
    return jnp.einsum("tf,df->td", left, right, preferred_element_type=F32)


def t_mm(left, right):
    return jnp.einsum("td,tf->df", left, right, preferred_element_type=F32)


def normalised(value):
    centre = value - jnp.mean(value, axis=-1, keepdims=True)
    rstd = lax.rsqrt(jnp.mean(centre * centre, axis=-1, keepdims=True) + EPS)
    return centre * rstd, rstd


def norm_back(unit, rstd, grad):
    first = jnp.mean(grad, axis=-1, keepdims=True)
    second = jnp.mean(grad * unit, axis=-1, keepdims=True)
    return rstd * (grad - first - unit * second)


def gelu_parts(z):
    half = 0.5 * (1.0 + lax.erf(z * 0.7071067811865476))
    slope = half + z * (0.3989422804014327 * jnp.exp(-0.5 * z * z))
    return z * half, slope


def groups_of(count):
    return [list(range(first, first + GROUP)) for first in range(0, count, GROUP)]


def gathered(shard):
    return lax.all_gather(shard, "dev", axis=0, tiled=True)


def scattered(whole):
    return lax.psum_scatter(whole, "dev", scatter_dimension=0, tiled=True)


def pack(vectors, count):
    return jnp.concatenate([v.reshape(count, -1) for v in vectors], axis=1)


def unpack(packed, sizes):
    out, at = [], 0
    for size in sizes:
        out.append(packed[:, at : at + size].reshape(-1))
        at += size
    return out


def to_heads(parts, devices):
    rows = parts[0].shape[0]
    sent = jnp.stack([p.reshape(rows, GROUP, -1) for p in parts], axis=2)
    sent = sent.transpose(1, 0, 2, 3)
    back = lax.all_to_all(sent, "dev", 0, 0, axis_index_groups=groups_of(devices), tiled=True)
    return [back[:, :, i].reshape(GROUP * rows, -1) for i in range(len(parts))]


def to_tokens(parts, devices):
    rows = parts[0].shape[0] // GROUP
    sent = jnp.stack([p.reshape(GROUP, rows, -1) for p in parts], axis=2)
    back = lax.all_to_all(sent, "dev", 0, 0, axis_index_groups=groups_of(devices), tiled=True)
    return [back[:, :, i].transpose(1, 0, 2).reshape(rows, -1) for i in range(len(parts))]


def shifted(shard, by, devices):
    pairs = [(i, i + by) for i in range(devices) if 0 <= i + by < devices]
    return lax.ppermute(shard, "dev", pairs)


def take(stack, index, axis):
    return lax.dynamic_index_in_dim(stack, index, axis, keepdims=False)


def swapped(value, bit, devices):
    return lax.ppermute(value, "dev", [(i, i ^ bit) for i in range(devices)])


def column_groups(devices):
    return [list(range(first, devices, GROUP)) for first in range(GROUP)]


def across_planes(stack, devices):
    return lax.all_to_all(stack, "dev", 0, 0, axis_index_groups=column_groups(devices), tiled=True)


def assemble_kernel(bits, *refs):
    sources, (weight, vector), sem = refs[:4], refs[4:6], refs[6]
    y, x, c = bits[0], bits[1], bits[2]
    half = sources[0].shape[-1]
    copies = []
    for far in range(2):
        for i in range(2):
            for j in range(2):
                a = sources[far].at[i, j]
                b = sources[2 + far].at[j, i]
                target = weight.at[:, y ^ j, x ^ i, c ^ far]
                copies.append((a, target.at[:, :, :half]))
                copies.append((b.at[:, :, : weight.shape[-1] - half], target.at[:, :, half:]))
                copies.append((b.at[:, :, weight.shape[-1] - half :], vector.at[:, y ^ j, x ^ i, c ^ far]))
    started = [pltpu.make_async_copy(s, t, sem.at[n]) for n, (s, t) in enumerate(copies)]
    for copy in started:
        copy.start()
    for copy in started:
        copy.wait()


def position(me):
    return (me // 4) % 2, (me // 2) % 2, me % 2


def gather_by_axes(weight, extra, me, devices):
    planes, (rows, width) = devices // GROUP, weight.shape
    half = width // 2
    shard = jnp.concatenate([weight, extra], axis=1)
    stack = across_planes(jnp.broadcast_to(shard[None], (planes, *shard.shape)), devices)
    a, b = stack[..., :half], stack[..., half:]
    a = jnp.stack([a, swapped(a, 4, devices)])
    b = jnp.stack([b, swapped(b, 2, devices)])
    a = jnp.stack([a, swapped(a, 2, devices)])
    b = jnp.stack([b, swapped(b, 4, devices)])
    far_a, far_b = swapped(a, 1, devices), swapped(b, 1, devices)
    anywhere = pl.BlockSpec(memory_space=pl.ANY)
    out, vec = pl.pallas_call(
        assemble_kernel,
        out_shape=(
            jax.ShapeDtypeStruct((planes, 2, 2, 2, rows, width), weight.dtype),
            jax.ShapeDtypeStruct((planes, 2, 2, 2, rows, extra.shape[1]), weight.dtype),
        ),
        grid_spec=pltpu.PrefetchScalarGridSpec(
            num_scalar_prefetch=1,
            grid=(1,),
            in_specs=[anywhere] * 4,
            out_specs=[anywhere] * 2,
            scratch_shapes=[pltpu.SemaphoreType.DMA((24,))],
        ),
        cost_estimate=pl.CostEstimate(flops=0, bytes_accessed=4 * devices * rows * width, transcendentals=0),
        name="assemble",
    )(jnp.stack(position(me)).astype(jnp.int32), a, far_a, b, far_b)
    return out.reshape(devices * rows, width), vec.reshape(devices * rows, -1)


def grad_kernel(bits, a_ref, b_ref, keep_ref, send_ref, a_t):
    step = pl.program_id(0)
    per, rows, width = keep_ref.shape

    @pl.when(step == 0)
    def _():
        for j in range(a_ref.shape[1] // 128):
            part = a_ref[:, j * 128 : (j + 1) * 128].astype(F32).T.astype(BF16)
            for i in range(128 // rows):
                owner = j * (128 // rows) + i
                a_t[(owner % 2) ^ bits[2], owner // 2] = part[i * rows : (i + 1) * rows]

    columns = 512
    for side, out in enumerate((keep_ref, send_ref)):
        left = a_t[side, pl.ds(step * per, per)].reshape(per * rows, -1)
        for n in range(width // columns):
            at = slice(n * columns, (n + 1) * columns)
            out[:, :, at] = mm(left, b_ref[:, at]).reshape(per, rows, columns).astype(BF16)


def weight_grad(a, b, rows, me):
    tokens, height = a.shape
    width = b.shape[1]
    blocks = height // (2 * rows)
    per = 256 // rows
    out = jax.ShapeDtypeStruct((blocks, rows, width), BF16)
    tile = pl.BlockSpec((per, rows, width), lambda i, *_: (i, 0, 0))
    return pl.pallas_call(
        grad_kernel,
        out_shape=(out, out),
        grid_spec=pltpu.PrefetchScalarGridSpec(
            num_scalar_prefetch=1,
            grid=(blocks // per,),
            in_specs=[
                pl.BlockSpec((tokens, height), lambda i, *_: (0, 0)),
                pl.BlockSpec((tokens, width), lambda i, *_: (0, 0)),
            ],
            out_specs=[tile, tile],
            scratch_shapes=[pltpu.VMEM((2, blocks, rows, tokens), BF16)],
        ),
        compiler_params=pltpu.CompilerParams(vmem_limit_bytes=48 << 20),
        cost_estimate=pl.CostEstimate(
            flops=2 * tokens * height * width, bytes_accessed=2 * height * width + 2 * tokens * (height + width),
            transcendentals=0,
        ),
        name="weight_grad",
    )(jnp.stack(position(me)).astype(jnp.int32), a, b)


def scatter_by_axes(keep, send, me, devices):
    y, x, _ = position(me)
    blocks, rows, width = keep.shape
    half = width // 2
    got = swapped(send, 1, devices)
    shape = (devices // GROUP, 2, 2, rows, width)
    keep, got = keep.reshape(shape), got.reshape(shape)
    columns = (slice(0, half), slice(half, width))

    def first(part, index, axis):
        return take(keep[..., part], index, axis).astype(F32) + take(got[..., part], index, axis).astype(F32)

    a_got = swapped(first(columns[0], 1 - x, 2).astype(BF16), 2, devices)
    b_got = swapped(first(columns[1], 1 - y, 1).astype(BF16), 4, devices)
    a = (first(columns[0], x, 2) + a_got.astype(F32)).astype(BF16)
    b = (first(columns[1], y, 1) + b_got.astype(F32)).astype(BF16)
    a_more = swapped(take(a, 1 - y, 1), 4, devices)
    b_more = swapped(take(b, 1 - x, 1), 2, devices)
    a = take(a, y, 1).astype(F32) + a_more.astype(F32)
    b = take(b, x, 1).astype(F32) + b_more.astype(F32)
    planes = across_planes(jnp.concatenate([a, b], axis=2).astype(BF16), devices)
    return jnp.sum(planes.astype(F32), axis=0)


def pack_columns(vectors, rows):
    columns = jnp.concatenate([v.reshape(-1, rows).T for v in vectors], axis=1)
    return jnp.pad(columns, ((0, 0), (0, 128 - columns.shape[1])))


def unpack_columns(packed, sizes, rows):
    lines, out, at = packed[:, :16].T, [], 0
    for size in sizes:
        count = size // rows
        part = lines[at : at + count].reshape(count, -1, rows)
        out.append(part.transpose(1, 0, 2).reshape(-1))
        at += count
    return out


def body(
    tokens,
    cotangent,
    image_lengths,
    ln1_gain,
    ln1_bias,
    qkv_weight,
    qv_bias,
    proj_weight,
    proj_bias,
    scale_attn,
    ln2_gain,
    ln2_bias,
    fc1_weight,
    fc1_bias,
    fc2_weight,
    fc2_bias,
    scale_mlp,
):
    devices = lax.axis_size("dev")
    me = lax.axis_index("dev")
    rows, width = tokens.shape
    vectors = (
        ln1_gain, ln1_bias, qv_bias, proj_bias, scale_attn, ln2_gain, ln2_bias, fc1_bias, fc2_bias, scale_mlp,
    )
    sizes = [v.shape[0] for v in vectors]
    shard_rows = qkv_weight.shape[0]
    by_axes = shard_rows % 32 == 0
    if by_axes:
        w_qkv, packed = gather_by_axes(qkv_weight, pack_columns(vectors, shard_rows), me, devices)
        spread = unpack_columns(packed.astype(F32), sizes, shard_rows)
    else:
        w_qkv = gathered(qkv_weight)
        spread = unpack(gathered(pack(vectors, 1)).astype(F32), sizes)
    gain1, shift1, bias_qv, bias_proj, layer_attn, gain2, shift2, bias_fc1, bias_fc2, layer_mlp = spread

    def summed(a, b, rows):
        if by_axes:
            return scatter_by_axes(*weight_grad(a, b, rows, me), me, devices)
        return scattered(t_mm(a, b))

    w_proj = gathered(proj_weight)
    w_fc1 = gathered(fc1_weight)
    w_fc2 = gathered(fc2_weight)

    span = GROUP * rows
    halo = -(-(SEQ - 1) // BK) * BK
    base = (me // GROUP) * span - halo
    places = base + halo + jnp.arange(span, dtype=jnp.int32)
    ends = jnp.cumsum(image_lengths)
    before = ends[None, :] <= places[:, None]
    begin = jnp.max(jnp.where(before, ends[None, :], 0), axis=1)
    finish = jnp.min(jnp.where(before, devices * rows, ends[None, :]), axis=1)
    seg = jnp.stack([begin - base, finish - base]).astype(jnp.int32)
    low = seg[0, ::BQ] // BK
    high = -(-seg[1, BQ - 1 :: BQ] // BK)

    x = tokens.astype(F32)
    u1, rstd1 = normalised(x)
    n1 = (u1 * gain1 + shift1).astype(BF16)
    qkv = mm(n1, w_qkv)
    q_mine = (qkv[:, :width] + bias_qv[:width]).astype(BF16)
    k_mine = qkv[:, width : 2 * width].astype(BF16)
    v_mine = (qkv[:, 2 * width :] + bias_qv[width:]).astype(BF16)
    q, k, v = to_heads([q_mine, k_mine, v_mine], devices)
    kv = jnp.concatenate([k, v], axis=1)
    left = shifted(kv[span - halo :], GROUP, devices)
    right = shifted(kv[:halo], -GROUP, devices)
    window = jnp.concatenate([left, kv, right], axis=0)
    k_win, v_win = window[:, : q.shape[1]], window[:, q.shape[1] :]
    o_heads, lse = attention_forward(low, high, seg, q, k_win, v_win)
    (o,) = to_tokens([o_heads], devices)

    branch = mm(o, w_proj) + bias_proj
    y1 = x + layer_attn * branch
    u2, rstd2 = normalised(y1)
    n2 = (u2 * gain2 + shift2).astype(BF16)
    act, slope = gelu_parts(mm(n2, w_fc1) + bias_fc1)
    act = act.astype(BF16)
    mlp = mm(act, w_fc2) + bias_fc2
    block_out = (y1 + layer_mlp * mlp).astype(BF16)

    g = cotangent.astype(F32)
    d_scale_mlp = jnp.sum(g * mlp, axis=0)
    dm = layer_mlp * g
    d_fc2_bias = jnp.sum(dm, axis=0)
    dml = dm.astype(BF16)
    d_fc2 = summed(act, dml, fc2_weight.shape[0])
    dz = mm_t(dml, w_fc2) * slope
    d_fc1_bias = jnp.sum(dz, axis=0)
    dzl = dz.astype(BF16)
    d_fc1 = summed(n2, dzl, fc1_weight.shape[0])
    dn2 = mm_t(dzl, w_fc1)
    d_gain2 = jnp.sum(dn2 * u2, axis=0)
    d_shift2 = jnp.sum(dn2, axis=0)
    dy1 = g + norm_back(u2, rstd2, dn2 * gain2)
    d_scale_attn = jnp.sum(dy1 * branch, axis=0)
    db = layer_attn * dy1
    d_proj_bias = jnp.sum(db, axis=0)
    dbl = db.astype(BF16)
    d_proj = scattered(t_mm(o, dbl))
    do = mm_t(dbl, w_proj).astype(BF16)

    (do_heads,) = to_heads([do], devices)
    dq, mid, edge = attention_backward(low, high, seg, q, k_win, v_win, o_heads, do_heads, lse, halo)
    from_right = shifted(edge[0], -GROUP, devices).astype(F32)
    from_left = shifted(edge[1], GROUP, devices).astype(F32)
    rest = span - halo
    mid = mid + jnp.pad(from_left, ((0, rest), (0, 0))) + jnp.pad(from_right, ((rest, 0), (0, 0)))
    mid = mid.astype(BF16)
    half = dq.shape[1]
    dq, dk, dv = to_tokens([dq, mid[:, :half], mid[:, half:]], devices)
    dqkv = jnp.concatenate([dq, dk, dv], axis=1)
    d_qv_bias = jnp.concatenate([jnp.sum(dq.astype(F32), axis=0), jnp.sum(dv.astype(F32), axis=0)])
    d_qkv = summed(n1, dqkv, shard_rows)
    dn1 = mm_t(dqkv, w_qkv)
    d_gain1 = jnp.sum(dn1 * u1, axis=0)
    d_shift1 = jnp.sum(dn1, axis=0)
    grad_tokens = (dy1 + norm_back(u1, rstd1, dn1 * gain1)).astype(BF16)

    small = (
        d_gain1, d_shift1, d_qv_bias, d_proj_bias, d_scale_attn, d_gain2, d_shift2, d_fc1_bias, d_fc2_bias, d_scale_mlp,
    )
    small = lax.all_to_all(pack(small, devices), "dev", 0, 0, tiled=True)
    small = jnp.sum(small, axis=0, keepdims=True)
    s_gain1, s_shift1, s_qv, s_proj, s_attn, s_gain2, s_shift2, s_fc1, s_fc2, s_mlp = unpack(small, sizes)
    return (
        block_out,
        grad_tokens,
        s_gain1,
        s_shift1,
        d_qkv,
        s_qv,
        d_proj,
        s_proj,
        s_attn,
        s_gain2,
        s_shift2,
        d_fc1,
        s_fc1,
        d_fc2,
        s_fc2,
        s_mlp,
    )


def solution(mesh):
    matrix, vector = P("dev", None), P("dev")
    return jax.shard_map(
        body,
        mesh=mesh,
        in_specs=(
            matrix, matrix, P(), vector, vector, matrix, vector, matrix, vector, vector, vector, vector, matrix,
            vector, matrix, vector, vector,
        ),
        out_specs=(
            matrix, matrix, vector, vector, matrix, vector, matrix, vector, vector, vector, vector, matrix, vector,
            matrix, vector, vector,
        ),
        check_vma=False,
    )
```

```python
import jax
import jax.numpy as jnp
from jax import lax
from jax.sharding import PartitionSpec as P
from jax.experimental import pallas as pl
from jax.experimental.pallas import tpu as pltpu

BQ = 256
BK = 256
HD = 64
LOG2E = 1.4426950408889634
SCALE = 0.125
MASKED = -1e30
NT = (((1,), (1,)), ((), ()))


def rows_of(ref, block, size):
    return ref[pl.ds(pl.multiple_of(block * size, size), size), :]


def head_halves(block):
    first = lax.broadcasted_iota(jnp.int32, block.shape, 1) < HD
    zero = jnp.zeros_like(block)
    return jnp.where(first, block, zero), jnp.where(first, zero, block)


def transpose_into(target, source):
    for j in range(source.shape[0] // BK):
        part = source[j * BK : (j + 1) * BK, :].astype(jnp.float32)
        target[:, j * BK : (j + 1) * BK] = part.T.astype(target.dtype)


def forward_kernel(low, high, seg, q_ref, k_ref, v_ref, o_ref, lse_ref, v_t):
    step = pl.program_id(0)

    @pl.when(step == 0)
    def _():
        transpose_into(v_t, v_ref)

    q_heads = head_halves(q_ref[...])
    begin, end = seg[0:1, :], seg[1:2, :]
    place = lax.broadcasted_iota(jnp.int32, (BK, BQ), 0)

    def one_block(j, carry):
        keys = rows_of(k_ref, j, BK)
        at = place + j * BK
        valid = (at >= begin) & (at < end)
        out = []
        for h in range(2):
            top, total, acc = carry[h]
            s = lax.dot_general(keys, q_heads[h], NT, preferred_element_type=jnp.float32)
            s = jnp.where(valid, s * (SCALE * LOG2E), MASKED)
            new_top = jnp.maximum(top, jnp.max(s, axis=0, keepdims=True))
            p = jnp.exp2(s - new_top)
            fade = jnp.exp2(top - new_top)
            total = total * fade + jnp.sum(p, axis=0, keepdims=True)
            v_part = v_t[h * HD : (h + 1) * HD, pl.ds(pl.multiple_of(j * BK, BK), BK)]
            acc = acc * fade + jnp.dot(v_part, p.astype(jnp.bfloat16), preferred_element_type=jnp.float32)
            out.append((new_top, total, acc))
        return tuple(out)

    start = (
        jnp.full((1, BQ), MASKED, jnp.float32),
        jnp.zeros((1, BQ), jnp.float32),
        jnp.zeros((HD, BQ), jnp.float32),
    )
    done = lax.fori_loop(low[step], high[step], one_block, (start, start))
    outs = jnp.concatenate([acc / total for _, total, acc in done], axis=0)
    o_ref[...] = outs.T.astype(o_ref.dtype)
    for h in range(2):
        top, total, _ = done[h]
        lse_ref[h : h + 1, :] = top + jnp.log2(total)


def backward_kernel(
    low, high, seg, q_ref, k_ref, v_ref, o_ref, do_ref, lse_ref, dq_ref, mid_ref, edge_ref, k_t, dk, dv, dq_t
):
    step = pl.program_id(0)

    @pl.when(step == 0)
    def _():
        transpose_into(k_t, k_ref)
        dk[...] = jnp.zeros_like(dk)
        dv[...] = jnp.zeros_like(dv)

    q_heads = head_halves(q_ref[...])
    do_heads = head_halves(do_ref[...])
    q_both = jnp.concatenate(q_heads, axis=0)
    do_both = jnp.concatenate(do_heads, axis=0)
    prod = (do_ref[...].astype(jnp.float32) * o_ref[...].astype(jnp.float32)).T
    begin, end = seg[0:1, :], seg[1:2, :]
    place = lax.broadcasted_iota(jnp.int32, (BK, BQ), 0)
    centre = [jnp.sum(prod[h * HD : (h + 1) * HD], axis=0, keepdims=True) for h in range(2)]
    lse = [lse_ref[h : h + 1, :] for h in range(2)]
    dq_t[...] = jnp.zeros_like(dq_t)

    @pl.loop(low[step], high[step])
    def _(j):
        rows = pl.ds(pl.multiple_of(j * BK, BK), BK)
        keys, values = k_ref[rows, :], v_ref[rows, :]
        at = place + j * BK
        valid = (at >= begin) & (at < end)
        ps, dss = [], []
        for h in range(2):
            s = lax.dot_general(keys, q_heads[h], NT, preferred_element_type=jnp.float32)
            p = jnp.where(valid, jnp.exp2(s * (SCALE * LOG2E) - lse[h]), 0.0)
            dp = lax.dot_general(values, do_heads[h], NT, preferred_element_type=jnp.float32)
            ds = (p * (dp - centre[h])).astype(jnp.bfloat16)
            ps.append(p.astype(jnp.bfloat16))
            dss.append(ds)
            part = slice(h * HD, (h + 1) * HD)
            dq_t[part, :] += jnp.dot(k_t[part, rows], ds, preferred_element_type=jnp.float32)
        dv[rows, :] += jnp.dot(jnp.concatenate(ps, axis=1), do_both, preferred_element_type=jnp.float32)
        dk[rows, :] += jnp.dot(jnp.concatenate(dss, axis=1), q_both, preferred_element_type=jnp.float32)

    dq_ref[...] = (dq_t[...] * SCALE).T.astype(dq_ref.dtype)

    @pl.when(step == pl.num_programs(0) - 1)
    def _():
        halo = edge_ref.shape[1]
        span = mid_ref.shape[0]
        for j in range(dk.shape[0] // BK):
            part = slice(j * BK, (j + 1) * BK)
            both = jnp.concatenate([dk[part] * SCALE, dv[part]], axis=1)
            if j * BK < halo:
                edge_ref[0, part, :] = both.astype(edge_ref.dtype)
            elif j * BK < halo + span:
                mid_ref[j * BK - halo : (j + 1) * BK - halo, :] = both
            else:
                first = j * BK - halo - span
                edge_ref[1, first : first + BK, :] = both.astype(edge_ref.dtype)


def attention_forward(low, high, seg, q, k, v):
    span, width = q.shape
    window = k.shape[0]
    steps = span // BQ
    whole = pl.BlockSpec((window, width), lambda i, *_: (0, 0))
    rows = pl.BlockSpec((BQ, width), lambda i, *_: (i, 0))
    return pl.pallas_call(
        forward_kernel,
        out_shape=(
            jax.ShapeDtypeStruct((span, width), jnp.bfloat16),
            jax.ShapeDtypeStruct((8, span), jnp.float32),
        ),
        grid_spec=pltpu.PrefetchScalarGridSpec(
            num_scalar_prefetch=2,
            grid=(steps,),
            in_specs=[pl.BlockSpec((2, BQ), lambda i, *_: (0, i)), rows, whole, whole],
            out_specs=[rows, pl.BlockSpec((8, BQ), lambda i, *_: (0, i))],
            scratch_shapes=[pltpu.VMEM((width, window), jnp.bfloat16)],
        ),
        compiler_params=pltpu.CompilerParams(vmem_limit_bytes=40 << 20),
        cost_estimate=pl.CostEstimate(flops=16 * span * 1536 * 128, bytes_accessed=8 << 20, transcendentals=2 * span * 1536),
        name="attention_forward",
    )(low, high, seg, q, k, v)


def attention_backward(low, high, seg, q, k, v, o, do, lse, halo):
    span, width = q.shape
    window = k.shape[0]
    steps = span // BQ
    whole = pl.BlockSpec((window, width), lambda i, *_: (0, 0))
    rows = pl.BlockSpec((BQ, width), lambda i, *_: (i, 0))
    return pl.pallas_call(
        backward_kernel,
        out_shape=(
            jax.ShapeDtypeStruct((span, width), jnp.bfloat16),
            jax.ShapeDtypeStruct((span, 2 * width), jnp.float32),
            jax.ShapeDtypeStruct((2, halo, 2 * width), jnp.bfloat16),
        ),
        grid_spec=pltpu.PrefetchScalarGridSpec(
            num_scalar_prefetch=2,
            grid=(steps,),
            in_specs=[
                pl.BlockSpec((2, BQ), lambda i, *_: (0, i)), rows, whole, whole, rows, rows,
                pl.BlockSpec((8, BQ), lambda i, *_: (0, i)),
            ],
            out_specs=[
                rows,
                pl.BlockSpec((span, 2 * width), lambda i, *_: (0, 0)),
                pl.BlockSpec((2, halo, 2 * width), lambda i, *_: (0, 0, 0)),
            ],
            scratch_shapes=[
                pltpu.VMEM((width, window), jnp.bfloat16),
                pltpu.VMEM((window, width), jnp.float32),
                pltpu.VMEM((window, width), jnp.float32),
                pltpu.VMEM((width, BQ), jnp.float32),
            ],
        ),
        compiler_params=pltpu.CompilerParams(vmem_limit_bytes=48 << 20),
        cost_estimate=pl.CostEstimate(flops=40 * span * 1536 * 128, bytes_accessed=16 << 20, transcendentals=2 * span * 1536),
        name="attention_backward",
    )(low, high, seg, q, k, v, o, do, lse)


HEADS = 16
SEQ = 1370
GROUP = 8
EPS = 1e-06
F32, BF16 = jnp.float32, jnp.bfloat16


def mm(left, right):
    return jnp.dot(left, right, preferred_element_type=F32)


def mm_t(left, right):
    return jnp.einsum("tf,df->td", left, right, preferred_element_type=F32)


def t_mm(left, right):
    return jnp.einsum("td,tf->df", left, right, preferred_element_type=F32)


def normalised(value):
    centre = value - jnp.mean(value, axis=-1, keepdims=True)
    rstd = lax.rsqrt(jnp.mean(centre * centre, axis=-1, keepdims=True) + EPS)
    return centre * rstd, rstd


def norm_back(unit, rstd, grad):
    first = jnp.mean(grad, axis=-1, keepdims=True)
    second = jnp.mean(grad * unit, axis=-1, keepdims=True)
    return rstd * (grad - first - unit * second)


def gelu_parts(z):
    half = 0.5 * (1.0 + lax.erf(z * 0.7071067811865476))
    slope = half + z * (0.3989422804014327 * jnp.exp(-0.5 * z * z))
    return z * half, slope


def groups_of(count):
    return [list(range(first, first + GROUP)) for first in range(0, count, GROUP)]


def gathered(shard):
    return lax.all_gather(shard, "dev", axis=0, tiled=True)


def scattered(whole):
    return lax.psum_scatter(whole, "dev", scatter_dimension=0, tiled=True)


def pack(vectors, count):
    return jnp.concatenate([v.reshape(count, -1) for v in vectors], axis=1)


def unpack(packed, sizes):
    out, at = [], 0
    for size in sizes:
        out.append(packed[:, at : at + size].reshape(-1))
        at += size
    return out


def to_heads(parts, devices):
    rows = parts[0].shape[0]
    sent = jnp.stack([p.reshape(rows, GROUP, -1) for p in parts], axis=2)
    sent = sent.transpose(1, 0, 2, 3)
    back = lax.all_to_all(sent, "dev", 0, 0, axis_index_groups=groups_of(devices), tiled=True)
    return [back[:, :, i].reshape(GROUP * rows, -1) for i in range(len(parts))]


def to_tokens(parts, devices):
    rows = parts[0].shape[0] // GROUP
    sent = jnp.stack([p.reshape(GROUP, rows, -1) for p in parts], axis=2)
    back = lax.all_to_all(sent, "dev", 0, 0, axis_index_groups=groups_of(devices), tiled=True)
    return [back[:, :, i].transpose(1, 0, 2).reshape(rows, -1) for i in range(len(parts))]


def shifted(shard, by, devices):
    pairs = [(i, i + by) for i in range(devices) if 0 <= i + by < devices]
    return lax.ppermute(shard, "dev", pairs)


def take(stack, index, axis):
    return lax.dynamic_index_in_dim(stack, index, axis, keepdims=False)


def swapped(value, bit, devices):
    return lax.ppermute(value, "dev", [(i, i ^ bit) for i in range(devices)])


def across_planes(stack, devices):
    columns = [list(range(first, devices, GROUP)) for first in range(GROUP)]
    return lax.all_to_all(stack, "dev", 0, 0, axis_index_groups=columns, tiled=True)


def in_plane(stack, devices):
    return lax.all_to_all(stack, "dev", 0, 0, axis_index_groups=groups_of(devices), tiled=True)


def position(me):
    return (me // 4) % 2, (me // 2) % 2, me % 2


def qkv_kernel(bits, near_a, far_a, near_b, far_b, gain, shift, weight, bias, n1_ref, q_ref, k_ref, v_ref):
    far = pl.program_id(0) >= 4
    left = jnp.where(far, far_a[0, 0], near_a[0, 0])
    right = jnp.where(far, far_b[0, 0], near_b[0, 0])
    unit, _ = normalised(jnp.concatenate([left, right], axis=1).astype(F32))
    n1 = (unit * gain[...] + shift[...]).astype(BF16)
    n1_ref[...] = n1
    out = (mm(n1, weight[...]) + bias[...]).astype(BF16)
    third = out.shape[1] // 3
    q_ref[...] = out[:, :third]
    k_ref[...] = out[:, third : 2 * third]
    v_ref[...] = out[:, 2 * third :]


def plane_qkv(tokens, gain, shift, weight, bias, me, devices):
    rows, width = tokens.shape
    half, third = width // 2, weight.shape[1] // 3
    a, b = tokens[:, :half], tokens[:, half:]
    a = jnp.stack([a, swapped(a, 4, devices)])
    b = jnp.stack([b, swapped(b, 2, devices)])
    a = jnp.stack([a, swapped(a, 2, devices)])
    b = jnp.stack([b, swapped(b, 4, devices)])
    far_a, far_b = swapped(a, 1, devices), swapped(b, 1, devices)

    def near_at(s, swap):
        i, j = (s // 2) % 2, s % 2
        i, j = jnp.where(s < 4, i, 1), jnp.where(s < 4, j, 1)
        return (j, i, 0, 0) if swap else (i, j, 0, 0)

    def far_at(s, swap):
        i, j = (s // 2) % 2, s % 2
        i, j = jnp.where(s < 4, 0, i), jnp.where(s < 4, 0, j)
        return (j, i, 0, 0) if swap else (i, j, 0, 0)

    def place(s, bits):
        return ((bits[0] ^ (s % 2)) * 4 + (bits[1] ^ ((s // 2) % 2)) * 2 + (bits[2] ^ (s // 4)), 0)

    piece = (1, 1, rows, half)
    line = pl.BlockSpec((1, width), lambda s, bits: (0, 0))
    span = GROUP * rows
    return pl.pallas_call(
        qkv_kernel,
        out_shape=(
            jax.ShapeDtypeStruct((span, width), BF16),
            jax.ShapeDtypeStruct((span, third), BF16),
            jax.ShapeDtypeStruct((span, third), BF16),
            jax.ShapeDtypeStruct((span, third), BF16),
        ),
        grid_spec=pltpu.PrefetchScalarGridSpec(
            num_scalar_prefetch=1,
            grid=(GROUP,),
            in_specs=[
                pl.BlockSpec(piece, lambda s, bits: near_at(s, False)),
                pl.BlockSpec(piece, lambda s, bits: far_at(s, False)),
                pl.BlockSpec(piece, lambda s, bits: near_at(s, True)),
                pl.BlockSpec(piece, lambda s, bits: far_at(s, True)),
                line,
                line,
                pl.BlockSpec(weight.shape, lambda s, bits: (0, 0)),
                pl.BlockSpec((1, 3 * third), lambda s, bits: (0, 0)),
            ],
            out_specs=[pl.BlockSpec((rows, width), place)] + [pl.BlockSpec((rows, third), place)] * 3,
        ),
        compiler_params=pltpu.CompilerParams(vmem_limit_bytes=40 << 20),
        cost_estimate=pl.CostEstimate(flops=30 << 28, bytes_accessed=16 << 20, transcendentals=0),
        name="plane_qkv",
    )(
        jnp.stack(position(me)).astype(jnp.int32), a, far_a, b, far_b, gain[None], shift[None], weight, bias[None],
    )


def by_parity(transposed, parity, rows):
    blocks = transposed.reshape(-1, 2, rows, transposed.shape[1])
    even, odd = (blocks[:, s].reshape(-1, transposed.shape[1]) for s in range(2))
    return jnp.where(parity == 0, even, odd), jnp.where(parity == 0, odd, even)


def turned(value):
    return value.astype(F32).T.astype(BF16)


def mlp_kernel(
    bits, n2_ref, dml_ref, f1_ref, f2_ref, bias, mlp_ref, dn2_ref, db_ref, keep1, send1, keep2, send2, n2_t
):
    step = pl.program_id(0)
    rows = keep1.shape[1]

    @pl.when(step == 0)
    def _():
        mlp_ref[...] = jnp.zeros_like(mlp_ref)
        dn2_ref[...] = jnp.zeros_like(dn2_ref)
        n2_t[0], n2_t[1] = by_parity(turned(n2_ref[...]), bits[2], rows)

    n2, dml, f1, f2 = n2_ref[...], dml_ref[...], f1_ref[...], f2_ref[...]
    act, slope = gelu_parts(mm(n2, f1) + bias[...])
    act = act.astype(BF16)
    mlp_ref[...] += mm(act, f2)
    dz = lax.dot_general(dml, f2, NT, preferred_element_type=F32) * slope
    db_ref[...] = jnp.sum(dz, axis=0, keepdims=True)
    dz = dz.astype(BF16)
    dn2_ref[...] += lax.dot_general(dz, f1, NT, preferred_element_type=F32)
    for side, out in enumerate((keep1, send1)):
        out[...] = mm(n2_t[side], dz).astype(BF16).reshape(out.shape)
    for part, out in zip(by_parity(turned(act), bits[2], rows), (keep2, send2)):
        out[...] = mm(part, dml).astype(BF16).reshape(out.shape)


def mlp_all(n2, dml, big, bias, me, shard_rows):
    tokens, width = n2.shape
    hidden, owners = bias.shape[0], width // shard_rows
    size = width // 2
    steps = hidden // size
    whole = pl.BlockSpec((tokens, width), lambda s, bits: (0, 0))
    first = pl.BlockSpec((owners // 2, shard_rows, size), lambda s, bits: (0, 0, s))
    second = pl.BlockSpec((owners // 4, shard_rows, width), lambda s, bits: (s % 2, 0, s // 2))
    line = pl.BlockSpec((1, size), lambda s, bits: (0, s))
    grads = jax.ShapeDtypeStruct((owners // 2, shard_rows, hidden), BF16)
    total = jax.ShapeDtypeStruct((tokens, width), F32)
    blocks = hidden // width
    return pl.pallas_call(
        mlp_kernel,
        out_shape=(total, total, jax.ShapeDtypeStruct((1, hidden), F32), grads, grads, grads, grads),
        grid_spec=pltpu.PrefetchScalarGridSpec(
            num_scalar_prefetch=1,
            grid=(steps,),
            in_specs=[
                whole,
                whole,
                pl.BlockSpec((width, size), lambda s, bits: (0, s)),
                pl.BlockSpec((size, width), lambda s, bits: (s % 2, blocks + s // 2)),
                line,
            ],
            out_specs=[whole, whole, line, first, first, second, second],
            scratch_shapes=[pltpu.VMEM((2, width // 2, tokens), BF16)],
        ),
        compiler_params=pltpu.CompilerParams(vmem_limit_bytes=52 << 20),
        cost_estimate=pl.CostEstimate(
            flops=12 * tokens * width * hidden, bytes_accessed=8 * width * hidden, transcendentals=2 * tokens * hidden
        ),
        name="mlp_all",
    )(jnp.stack(position(me)).astype(jnp.int32), n2, dml, big, big, bias[None])


def grad_kernel(bits, a_ref, b_ref, keep_ref, send_ref):
    for part, out in zip(by_parity(turned(a_ref[...]), bits[2], keep_ref.shape[1]), (keep_ref, send_ref)):
        out[...] = mm(part, b_ref[...]).astype(BF16).reshape(out.shape)


def weight_grad(a, b, rows, me):
    out = jax.ShapeDtypeStruct((a.shape[1] // (2 * rows), rows, b.shape[1]), BF16)
    return pl.pallas_call(
        grad_kernel,
        out_shape=(out, out),
        grid_spec=pltpu.PrefetchScalarGridSpec(num_scalar_prefetch=1, grid=(1,)),
        compiler_params=pltpu.CompilerParams(vmem_limit_bytes=40 << 20),
        cost_estimate=pl.CostEstimate(
            flops=2 * a.size * b.shape[1], bytes_accessed=2 * (a.size + b.size + 2 * out.size), transcendentals=0
        ),
        name="weight_grad",
    )(jnp.stack(position(me)).astype(jnp.int32), a, b)


def body(
    tokens,
    cotangent,
    image_lengths,
    ln1_gain,
    ln1_bias,
    qkv_weight,
    qv_bias,
    proj_weight,
    proj_bias,
    scale_attn,
    ln2_gain,
    ln2_bias,
    fc1_weight,
    fc1_bias,
    fc2_weight,
    fc2_bias,
    scale_mlp,
):
    devices = lax.axis_size("dev")
    me = lax.axis_index("dev")
    rows, width = tokens.shape
    vectors = (
        ln1_gain, ln1_bias, qv_bias, proj_bias, scale_attn, ln2_gain, ln2_bias, fc1_bias, fc2_bias, scale_mlp,
    )
    sizes = [v.shape[0] for v in vectors]
    shard_rows, hidden = qkv_weight.shape[0], fc1_weight.shape[1]
    by_axes = shard_rows % 32 == 0
    blocks = hidden // width
    packed = pack(vectors, 1)
    packed = lax.all_to_all(jnp.broadcast_to(packed, (devices, packed.shape[1])), "dev", 0, 0, tiled=True)
    spread = unpack(packed.astype(F32), sizes)
    gain1, shift1, bias_qv, bias_proj, layer_attn, gain2, shift2, bias_fc1, bias_fc2, layer_mlp = spread
    slab = qkv_weight.reshape(shard_rows, 3, GROUP, -1).transpose(2, 0, 1, 3).reshape(GROUP, shard_rows, -1)
    slab = in_plane(slab, devices).reshape(1, GROUP * shard_rows, -1)
    slab = across_planes(jnp.broadcast_to(slab, (devices // GROUP, *slab.shape[1:])), devices)
    slab = slab.reshape(width, -1)
    if by_axes:
        first = fc1_weight.reshape(shard_rows, devices, blocks, shard_rows).transpose(0, 2, 1, 3)
        second = fc2_weight.reshape(blocks, shard_rows, width).transpose(1, 0, 2)
        big = jnp.concatenate(
            [first.reshape(shard_rows, hidden), second.reshape(shard_rows, hidden), proj_weight], axis=1
        )
        big = gathered(big)
        w_proj = big[:, 2 * hidden :]
    else:
        w_proj, big = gathered(proj_weight), gathered(fc1_weight)
        w_fc2 = gathered(fc2_weight)
    qkv_late, big = lax.optimization_barrier((qkv_weight, big))
    w_qkv = gathered(qkv_late)

    span = GROUP * rows
    halo = -(-(SEQ - 1) // BK) * BK
    base = (me // GROUP) * span - halo
    places = base + halo + jnp.arange(span, dtype=jnp.int32)
    ends = jnp.cumsum(image_lengths)
    before = ends[None, :] <= places[:, None]
    begin = jnp.max(jnp.where(before, ends[None, :], 0), axis=1)
    finish = jnp.min(jnp.where(before, devices * rows, ends[None, :]), axis=1)
    seg = jnp.stack([begin - base, finish - base]).astype(jnp.int32)
    low = seg[0, ::BQ] // BK
    high = -(-seg[1, BQ - 1 :: BQ] // BK)

    x = tokens.astype(F32)
    u1, rstd1 = normalised(x)
    heads_width = width // GROUP
    mine = (me % GROUP) * heads_width
    bias = jnp.concatenate(
        [
            lax.dynamic_slice(bias_qv, (mine,), (heads_width,)),
            jnp.zeros((heads_width,), F32),
            lax.dynamic_slice(bias_qv, (width + mine,), (heads_width,)),
        ]
    )
    n1, q, k, v = plane_qkv(tokens, gain1, shift1, slab, bias, me, devices)
    kv = jnp.concatenate([k, v], axis=1)
    left = shifted(kv[span - halo :], GROUP, devices)
    right = shifted(kv[:halo], -GROUP, devices)
    window = jnp.concatenate([left, kv, right], axis=0)
    k_win, v_win = window[:, : q.shape[1]], window[:, q.shape[1] :]
    o_heads, lse = attention_forward(low, high, seg, q, k_win, v_win)
    (o,) = to_tokens([o_heads], devices)

    branch = mm(o, w_proj) + bias_proj
    y1 = x + layer_attn * branch
    u2, rstd2 = normalised(y1)
    n2 = (u2 * gain2 + shift2).astype(BF16)
    g = cotangent.astype(F32)
    dm = layer_mlp * g
    d_fc2_bias = jnp.sum(dm, axis=0)
    dml = dm.astype(BF16)
    if by_axes:
        bias_hidden = bias_fc1.reshape(devices, blocks, shard_rows).transpose(1, 0, 2).reshape(-1)
        mlp, dn2, d_fc1_bias, keep1, send1, keep2, send2 = mlp_all(n2, dml, big, bias_hidden, me, shard_rows)
        d_fc1_bias = d_fc1_bias.reshape(blocks, devices, shard_rows).transpose(1, 0, 2).reshape(-1)
    else:
        act, slope = gelu_parts(mm(n2, big) + bias_fc1)
        act = act.astype(BF16)
        mlp = mm(act, w_fc2)
        dz = mm_t(dml, w_fc2) * slope
        d_fc1_bias = jnp.sum(dz, axis=0)
        dz = dz.astype(BF16)
        dn2 = mm_t(dz, big)
        d_fc1, d_fc2 = scattered(t_mm(n2, dz)), scattered(t_mm(act, dml))
    mlp = mlp + bias_fc2
    block_out = (y1 + layer_mlp * mlp).astype(BF16)
    d_scale_mlp = jnp.sum(g * mlp, axis=0)
    d_gain2 = jnp.sum(dn2 * u2, axis=0)
    d_shift2 = jnp.sum(dn2, axis=0)
    dy1 = g + norm_back(u2, rstd2, dn2 * gain2)
    d_scale_attn = jnp.sum(dy1 * branch, axis=0)
    db = layer_attn * dy1
    d_proj_bias = jnp.sum(db, axis=0)
    dbl = db.astype(BF16)
    do = mm_t(dbl, w_proj).astype(BF16)

    if by_axes:
        y, x, _ = position(me)
        keep3, send3 = weight_grad(o, dbl, shard_rows, me)
        got1, got2, got3 = (swapped(s, 1, devices) for s in (send1, send2, send3))
        do, got1, got2, got3 = lax.optimization_barrier((do, got1, got2, got3))
        view = (devices // GROUP, 2, 2, shard_rows)
        own1, own2, own3 = (s.reshape(*view, -1) for s in (keep1, keep2, keep3))
        got1, got2, got3 = (s.reshape(*view, -1) for s in (got1, got2, got3))
        cut = width // 2

        def part(index, axis, which):
            cols = slice(0, cut) if which == 0 else slice(cut, width)
            pairs = ((own1, got1), (own2, got2))[which], (own3[..., cols], got3[..., cols])
            both = [take(m, index, axis).astype(F32) + take(n, index, axis).astype(F32) for m, n in pairs]
            return jnp.concatenate(both, axis=-1).astype(BF16)

        out_a, out_b = part(1 - x, 2, 0), part(1 - y, 1, 1)
        do, out_a, out_b = lax.optimization_barrier((do, out_a, out_b))
        in_a, in_b = swapped(out_a, 2, devices), swapped(out_b, 4, devices)
    else:
        d_proj = scattered(t_mm(o, dbl))

    (do_heads,) = to_heads([do], devices)
    dq, mid, edge = attention_backward(low, high, seg, q, k_win, v_win, o_heads, do_heads, lse, halo)
    if by_axes:
        dq, mid, edge, in_a, in_b = lax.optimization_barrier((dq, mid, edge, in_a, in_b))
        sum_a = (part(x, 2, 0).astype(F32) + in_a.astype(F32)).astype(BF16)
        sum_b = (part(y, 1, 1).astype(F32) + in_b.astype(F32)).astype(BF16)
        in_a = swapped(take(sum_a, 1 - y, 1), 4, devices)
        in_b = swapped(take(sum_b, 1 - x, 1), 2, devices)
    from_right = shifted(edge[0], -GROUP, devices).astype(F32)
    from_left = shifted(edge[1], GROUP, devices).astype(F32)
    rest = span - halo
    mid = mid + jnp.pad(from_left, ((0, rest), (0, 0))) + jnp.pad(from_right, ((rest, 0), (0, 0)))
    mid = mid.astype(BF16)
    d_heads = jnp.concatenate([dq, mid], axis=1)
    if by_axes:
        d_heads, in_a, in_b = lax.optimization_barrier((d_heads, in_a, in_b))
        sum_a = take(sum_a, y, 1).astype(F32) + in_a.astype(F32)
        sum_b = take(sum_b, x, 1).astype(F32) + in_b.astype(F32)
        planes = across_planes(jnp.concatenate([sum_a, sum_b], axis=-1).astype(BF16), devices)
    dqkv = in_plane(d_heads.reshape(GROUP, rows, -1), devices).reshape(GROUP, rows, 3, -1)
    dqkv = dqkv.transpose(1, 2, 0, 3).reshape(rows, 3 * width)
    dq, dv = dqkv[:, :width], dqkv[:, 2 * width :]
    d_qkv = t_mm(n1, d_heads).astype(BF16).reshape(devices // GROUP, GROUP, shard_rows, -1)
    d_qkv = jnp.sum(across_planes(d_qkv, devices).astype(F32), axis=0)
    d_qkv = in_plane(d_qkv, devices).reshape(GROUP, shard_rows, 3, -1)
    d_qkv = d_qkv.transpose(1, 2, 0, 3).reshape(shard_rows, 3 * width)
    if by_axes:
        sums = jnp.sum(planes.astype(F32), axis=0)
        d_fc1 = sums[:, :hidden].reshape(shard_rows, blocks, devices, shard_rows).transpose(0, 2, 1, 3)
        d_fc1 = d_fc1.reshape(shard_rows, hidden)
        at = hidden + cut
        d_fc2 = sums[:, at : at + hidden].reshape(shard_rows, blocks, width).transpose(1, 0, 2)
        d_fc2 = d_fc2.reshape(blocks * shard_rows, width)
        d_proj = jnp.concatenate([sums[:, hidden:at], sums[:, at + hidden :]], axis=1)
    d_qv_bias = jnp.concatenate([jnp.sum(dq.astype(F32), axis=0), jnp.sum(dv.astype(F32), axis=0)])
    dn1 = mm_t(dqkv, w_qkv)
    d_gain1 = jnp.sum(dn1 * u1, axis=0)
    d_shift1 = jnp.sum(dn1, axis=0)
    grad_tokens = (dy1 + norm_back(u1, rstd1, dn1 * gain1)).astype(BF16)

    small = (
        d_gain1, d_shift1, d_qv_bias, d_proj_bias, d_scale_attn, d_gain2, d_shift2, d_fc1_bias, d_fc2_bias, d_scale_mlp,
    )
    small = lax.all_to_all(pack(small, devices), "dev", 0, 0, tiled=True)
    small = jnp.sum(small, axis=0, keepdims=True)
    s_gain1, s_shift1, s_qv, s_proj, s_attn, s_gain2, s_shift2, s_fc1, s_fc2, s_mlp = unpack(small, sizes)
    return (
        block_out,
        grad_tokens,
        s_gain1,
        s_shift1,
        d_qkv,
        s_qv,
        d_proj,
        s_proj,
        s_attn,
        s_gain2,
        s_shift2,
        d_fc1,
        s_fc1,
        d_fc2,
        s_fc2,
        s_mlp,
    )


def solution(mesh):
    matrix, vector = P("dev", None), P("dev")
    return jax.shard_map(
        body,
        mesh=mesh,
        in_specs=(
            matrix, matrix, P(), vector, vector, matrix, vector, matrix, vector, vector, vector, vector, matrix,
            vector, matrix, vector, vector,
        ),
        out_specs=(
            matrix, matrix, vector, vector, matrix, vector, matrix, vector, vector, vector, vector, matrix, vector,
            matrix, vector, vector,
        ),
        check_vma=False,
    )
```

```python
import functools

import jax
import jax.numpy as jnp
from jax import lax
from jax.experimental import pallas as pl
from jax.experimental.pallas import tpu as pltpu
from jax.sharding import PartitionSpec as P

BQ = 256
BK = 256
SLAB = 2 * BK
HD = 64
LOG2E = 1.4426950408889634
SCALE = 0.125
MASKED = -1e30
NT = (((1,), (1,)), ((), ()))


def head_halves(block):
    first = lax.broadcasted_iota(jnp.int32, block.shape, 1) < HD
    zero = jnp.zeros_like(block)
    return jnp.where(first, block, zero), jnp.where(first, zero, block)


def transpose_into(target, source, column):
    width = target.shape[0]
    for j in range(source.shape[0] // BK):
        part = source[j * BK : (j + 1) * BK, column : column + width].astype(jnp.float32)
        target[:, j * BK : (j + 1) * BK] = part.T.astype(target.dtype)


def slabs(low, high, first, last):
    low = jnp.clip(low, first, last) - first
    count = (jnp.clip(high, first, last) - first - low + 1) // 2
    return jnp.minimum(low, last - first - 2 * count), count


def slab_rows(start, t):
    return pl.ds(pl.multiple_of((start + 2 * t) * BK, BK), SLAB)


def forward_over(span, kv_ref, v_t, offset, q_heads, seg, carry):
    start, count = span
    width = q_heads[0].shape[1]
    begin, end = seg[0:1, :], seg[1:2, :]
    place = lax.broadcasted_iota(jnp.int32, (SLAB, BQ), 0) + offset

    def one_slab(t, carry):
        rows = slab_rows(start, t)
        keys = kv_ref[rows, :width]
        at = place + (start + 2 * t) * BK
        valid = (at >= begin) & (at < end)
        out = []
        for h in range(2):
            top, total, acc = carry[h]
            s = lax.dot_general(keys, q_heads[h], NT, preferred_element_type=jnp.float32)
            s = jnp.where(valid, s * (SCALE * LOG2E), MASKED)
            new_top = jnp.maximum(top, jnp.max(s, axis=0, keepdims=True))
            p = jnp.exp2(s - new_top)
            fade = jnp.exp2(top - new_top)
            total = total * fade + jnp.sum(p, axis=0, keepdims=True)
            v_part = v_t[h * HD : (h + 1) * HD, rows]
            acc = acc * fade + jnp.dot(v_part, p.astype(jnp.bfloat16), preferred_element_type=jnp.float32)
            out.append((new_top, total, acc))
        return tuple(out)

    return lax.fori_loop(0, count, one_slab, carry)


def forward_mid_kernel(low, high, seg, q_ref, kv_ref, acc_ref, stat_ref, v_t, *, edge):
    step = pl.program_id(0)

    @pl.when(step == 0)
    def _():
        transpose_into(v_t, kv_ref, q_ref.shape[1])

    start = (
        jnp.full((1, BQ), MASKED, jnp.float32),
        jnp.zeros((1, BQ), jnp.float32),
        jnp.zeros((HD, BQ), jnp.float32),
    )
    blocks = kv_ref.shape[0] // BK
    span = slabs(low[step], high[step], edge, edge + blocks)
    done = forward_over(span, kv_ref, v_t, edge * BK, head_halves(q_ref[...]), seg, (start, start))
    for h, (top, total, acc) in enumerate(done):
        stat_ref[2 * h : 2 * h + 1, :] = top
        stat_ref[2 * h + 1 : 2 * h + 2, :] = total
        acc_ref[h * HD : (h + 1) * HD, :] = acc


def forward_edge_kernel(
    low, high, seg, q_ref, left_ref, right_ref, acc_ref, stat_ref, o_ref, lse_ref, left_t, right_t, *, last
):
    step = pl.program_id(0)
    width = q_ref.shape[1]
    edge = left_ref.shape[0] // BK

    @pl.when(step == 0)
    def _():
        transpose_into(left_t, left_ref, width)
        transpose_into(right_t, right_ref, width)

    carry = tuple(
        (stat_ref[2 * h : 2 * h + 1, :], stat_ref[2 * h + 1 : 2 * h + 2, :], acc_ref[h * HD : (h + 1) * HD, :])
        for h in range(2)
    )
    q_heads = head_halves(q_ref[...])
    span = slabs(low[step], high[step], 0, edge)
    carry = forward_over(span, left_ref, left_t, 0, q_heads, seg, carry)
    span = slabs(low[step], high[step], last, last + edge)
    carry = forward_over(span, right_ref, right_t, last * BK, q_heads, seg, carry)
    o_ref[...] = jnp.concatenate([acc / total for _, total, acc in carry], axis=0).T.astype(o_ref.dtype)
    for h, (top, total, _) in enumerate(carry):
        lse_ref[h : h + 1, :] = top + jnp.log2(total)


def backward_setup(q_ref, do_ref, o_ref, lse_ref, heads):
    prod = (do_ref[...].astype(jnp.float32) * o_ref[...].astype(jnp.float32)).T
    q_heads, do_heads = head_halves(q_ref[...]), head_halves(do_ref[...])
    return [
        (
            h,
            q_heads[h],
            do_heads[h],
            jnp.sum(prod[h * HD : (h + 1) * HD], axis=0, keepdims=True),
            lse_ref[h : h + 1, :],
        )
        for h in heads
    ]


def backward_over(span, kv_ref, k_t, dkv, dq_t, offset, heads, seg):
    start, count = span
    width = dq_t.shape[0]
    begin, end = seg[0:1, :], seg[1:2, :]
    place = lax.broadcasted_iota(jnp.int32, (SLAB, BQ), 0) + offset
    q_all = jnp.concatenate([q for _, q, _, _, _ in heads], axis=0)
    do_all = jnp.concatenate([d for _, _, d, _, _ in heads], axis=0)

    @pl.loop(0, count)
    def _(t):
        rows = slab_rows(start, t)
        keys, values = kv_ref[rows, :width], kv_ref[rows, width:]
        at = place + (start + 2 * t) * BK
        valid = (at >= begin) & (at < end)
        ps, dss = [], []
        for h, q, do, centre, lse in heads:
            s = lax.dot_general(keys, q, NT, preferred_element_type=jnp.float32)
            p = jnp.where(valid, jnp.exp2(s * (SCALE * LOG2E) - lse), 0.0)
            dp = lax.dot_general(values, do, NT, preferred_element_type=jnp.float32)
            ds = (p * (dp - centre)).astype(jnp.bfloat16)
            ps.append(p.astype(jnp.bfloat16))
            dss.append(ds)
            part = slice(h * HD, (h + 1) * HD)
            dq_t[part, :] += jnp.dot(k_t[part, rows], ds, preferred_element_type=jnp.float32)
        dkv[rows, :width] += jnp.dot(jnp.concatenate(dss, axis=1), q_all, preferred_element_type=jnp.float32)
        dkv[rows, width:] += jnp.dot(jnp.concatenate(ps, axis=1), do_all, preferred_element_type=jnp.float32)


def backward_first_kernel(
    low, high, seg, q_ref, kv_ref, left_ref, right_ref, o_ref, do_ref, lse_ref, dq_t, mid_ref, edge_ref,
    left_t, right_t, k_t, dkv, *, last
):
    step = pl.program_id(0)
    width = q_ref.shape[1]
    edge = left_ref.shape[0] // BK

    @pl.when(step == 0)
    def _():
        transpose_into(left_t, left_ref, 0)
        transpose_into(right_t, right_ref, 0)
        transpose_into(k_t, kv_ref, 0)
        dkv[...] = jnp.zeros_like(dkv)
        mid_ref[...] = jnp.zeros_like(mid_ref)

    heads = backward_setup(q_ref, do_ref, o_ref, lse_ref, range(2))
    dq_t[...] = jnp.zeros_like(dq_t)
    span = slabs(low[step], high[step], 0, edge)
    backward_over(span, left_ref, left_t, dkv.at[0], dq_t, 0, heads, seg)
    span = slabs(low[step], high[step], last, last + edge)
    backward_over(span, right_ref, right_t, dkv.at[1], dq_t, last * BK, heads, seg)
    span = slabs(low[step], high[step], edge, last)
    backward_over(span, kv_ref, k_t, mid_ref, dq_t, edge * BK, heads[:1], seg)

    @pl.when(step == pl.num_programs(0) - 1)
    def _():
        mid_ref[:, :width] = mid_ref[:, :width] * SCALE
        for side in range(2):
            for j in range(edge):
                part = slice(j * BK, (j + 1) * BK)
                edge_ref[side, part, :width] = (dkv[side, part, :width] * SCALE).astype(edge_ref.dtype)
                edge_ref[side, part, width:] = dkv[side, part, width:].astype(edge_ref.dtype)


def backward_mid_kernel(
    low, high, seg, q_ref, kv_ref, o_ref, do_ref, lse_ref, part_ref, dq_ref, mid_ref, k_t, dq_t, *, edge
):
    step = pl.program_id(0)
    width = q_ref.shape[1]

    @pl.when(step == 0)
    def _():
        transpose_into(k_t, kv_ref, 0)
        mid_ref[...] = jnp.zeros_like(mid_ref)

    dq_t[...] = part_ref[...]
    blocks = kv_ref.shape[0] // BK
    span = slabs(low[step], high[step], edge, edge + blocks)
    heads = backward_setup(q_ref, do_ref, o_ref, lse_ref, [1])
    backward_over(span, kv_ref, k_t, mid_ref, dq_t, edge * BK, heads, seg)
    dq_ref[...] = (dq_t[...] * SCALE).T.astype(dq_ref.dtype)

    @pl.when(step == pl.num_programs(0) - 1)
    def _():
        mid_ref[:, :width] = mid_ref[:, :width] * SCALE


def whole_spec(array):
    return pl.BlockSpec(array.shape, lambda i, *_: (0,) * len(array.shape))


def attention_call(kernel, name, prefetch, inputs, in_kinds, outputs, out_kinds, scratch, work):
    span = prefetch[0].shape[0] * BQ

    def spec(array, kind):
        if kind == "r":
            return pl.BlockSpec((BQ, array.shape[1]), lambda i, *_: (i, 0))
        if kind == "c":
            return pl.BlockSpec((array.shape[0], BQ), lambda i, *_: (0, i))
        return whole_spec(array)

    return pl.pallas_call(
        kernel,
        out_shape=tuple(outputs),
        grid_spec=pltpu.PrefetchScalarGridSpec(
            num_scalar_prefetch=2,
            grid=(span // BQ,),
            in_specs=[spec(a, k) for a, k in zip(inputs, in_kinds)],
            out_specs=[spec(a, k) for a, k in zip(outputs, out_kinds)],
            scratch_shapes=scratch,
        ),
        compiler_params=pltpu.CompilerParams(vmem_limit_bytes=48 << 20),
        cost_estimate=pl.CostEstimate(flops=work << 30, bytes_accessed=8 << 20, transcendentals=span * 128),
        name=name,
    )(*prefetch, *inputs)


def shaped(*shape, dtype=jnp.float32):
    return jax.ShapeDtypeStruct(shape, dtype)


def forward_mid(prefetch, seg, q, kv, edge):
    span, width = q.shape
    return attention_call(
        functools.partial(forward_mid_kernel, edge=edge), "forward_mid", prefetch, [seg, q, kv], "crw",
        [shaped(width, span), shaped(8, span)], "cc", [pltpu.VMEM((width, span), jnp.bfloat16)], 3,
    )


def forward_edge(prefetch, seg, q, left, right, acc, stat):
    span, width = q.shape
    halo = pltpu.VMEM((width, left.shape[0]), jnp.bfloat16)
    return attention_call(
        functools.partial(forward_edge_kernel, last=(left.shape[0] + span) // BK), "forward_edge", prefetch,
        [seg, q, left, right, acc, stat], "crwwcc",
        [shaped(span, width, dtype=jnp.bfloat16), shaped(8, span)], "rc", [halo, halo], 3,
    )


def backward_first(prefetch, seg, q, kv, left, right, o, do, lse):
    span, width = q.shape
    halo = pltpu.VMEM((width, left.shape[0]), jnp.bfloat16)
    return attention_call(
        functools.partial(backward_first_kernel, last=(left.shape[0] + span) // BK), "backward_first", prefetch,
        [seg, q, kv, left, right, o, do, lse], "crwwwrrc",
        [shaped(width, span), shaped(*kv.shape), shaped(2, *left.shape, dtype=jnp.bfloat16)], "cww",
        [halo, halo, pltpu.VMEM((width, span), jnp.bfloat16), pltpu.VMEM((2, *left.shape), jnp.float32)], 3,
    )


def backward_second(prefetch, seg, q, kv, o, do, lse, part, edge):
    span, width = q.shape
    return attention_call(
        functools.partial(backward_mid_kernel, edge=edge), "backward_second", prefetch,
        [seg, q, kv, o, do, lse, part], "crwrrcc",
        [shaped(span, width, dtype=jnp.bfloat16), shaped(*kv.shape)], "rw",
        [pltpu.VMEM((width, span), jnp.bfloat16), pltpu.VMEM((width, BQ), jnp.float32)], 3,
    )


HEADS = 16
SEQ = 1370
GROUP = 8
EPS = 1e-06
F32, BF16 = jnp.float32, jnp.bfloat16


def mm(left, right):
    return jnp.dot(left, right, preferred_element_type=F32)


def mm_t(left, right):
    return jnp.einsum("tf,df->td", left, right, preferred_element_type=F32)


def t_mm(left, right):
    return jnp.einsum("td,tf->df", left, right, preferred_element_type=F32)


def normalised(value):
    centre = value - jnp.mean(value, axis=-1, keepdims=True)
    rstd = lax.rsqrt(jnp.mean(centre * centre, axis=-1, keepdims=True) + EPS)
    return centre * rstd, rstd


def norm_back(unit, rstd, grad):
    first = jnp.mean(grad, axis=-1, keepdims=True)
    second = jnp.mean(grad * unit, axis=-1, keepdims=True)
    return rstd * (grad - first - unit * second)


def gelu_parts(z):
    half = 0.5 * (1.0 + lax.erf(z * 0.7071067811865476))
    slope = half + z * (0.3989422804014327 * jnp.exp(-0.5 * z * z))
    return z * half, slope


def groups_of(count):
    return [list(range(first, first + GROUP)) for first in range(0, count, GROUP)]


def gathered(shard):
    return lax.all_gather(shard, "dev", axis=0, tiled=True)


def scattered(whole):
    return lax.psum_scatter(whole, "dev", scatter_dimension=0, tiled=True)


def pack(vectors, count):
    return jnp.concatenate([v.reshape(count, -1) for v in vectors], axis=1)


def unpack(packed, sizes):
    out, at = [], 0
    for size in sizes:
        out.append(packed[:, at : at + size].reshape(-1))
        at += size
    return out


def to_heads(parts, devices):
    rows = parts[0].shape[0]
    sent = jnp.stack([p.reshape(rows, GROUP, -1) for p in parts], axis=2)
    sent = sent.transpose(1, 0, 2, 3)
    back = lax.all_to_all(sent, "dev", 0, 0, axis_index_groups=groups_of(devices), tiled=True)
    return [back[:, :, i].reshape(GROUP * rows, -1) for i in range(len(parts))]


def to_tokens(parts, devices):
    rows = parts[0].shape[0] // GROUP
    sent = jnp.stack([p.reshape(GROUP, rows, -1) for p in parts], axis=2)
    back = lax.all_to_all(sent, "dev", 0, 0, axis_index_groups=groups_of(devices), tiled=True)
    return [back[:, :, i].transpose(1, 0, 2).reshape(rows, -1) for i in range(len(parts))]


def shifted(shard, by, devices):
    pairs = [(i, i + by) for i in range(devices) if 0 <= i + by < devices]
    return lax.ppermute(shard, "dev", pairs)


def take(stack, index, axis):
    return lax.dynamic_index_in_dim(stack, index, axis, keepdims=False)


def swapped(value, bit, devices):
    return lax.ppermute(value, "dev", [(i, i ^ bit) for i in range(devices)])


def in_plane(stack, devices):
    return lax.all_to_all(stack, "dev", 0, 0, axis_index_groups=groups_of(devices), tiled=True)


def position(me):
    return (me // 4) % 2, (me // 2) % 2, me % 2


def qkv_kernel(bits, near_a, far_a, near_b, far_b, gain, shift, weight, bias, n1_ref, q_ref, kv_ref):
    far = pl.program_id(0) >= 4
    left = jnp.where(far, far_a[0, 0], near_a[0, 0])
    right = jnp.where(far, far_b[0, 0], near_b[0, 0])
    unit, _ = normalised(jnp.concatenate([left, right], axis=1).astype(F32))
    n1 = (unit * gain[...] + shift[...]).astype(BF16)
    n1_ref[...] = n1
    out = (mm(n1, weight[...]) + bias[...]).astype(BF16)
    third = out.shape[1] // 3
    q_ref[...] = out[:, :third]
    kv_ref[...] = out[:, third:]


def plane_qkv(tokens, gain, shift, weight, bias, me, devices):
    rows, width = tokens.shape
    half, third = width // 2, weight.shape[1] // 3
    a, b = tokens[:, :half], tokens[:, half:]
    a = jnp.stack([a, swapped(a, 4, devices)])
    b = jnp.stack([b, swapped(b, 2, devices)])
    a = jnp.stack([a, swapped(a, 2, devices)])
    b = jnp.stack([b, swapped(b, 4, devices)])
    far_a, far_b = swapped(a, 1, devices), swapped(b, 1, devices)

    def near_at(s, swap):
        i, j = (s // 2) % 2, s % 2
        i, j = jnp.where(s < 4, i, 1), jnp.where(s < 4, j, 1)
        return (j, i, 0, 0) if swap else (i, j, 0, 0)

    def far_at(s, swap):
        i, j = (s // 2) % 2, s % 2
        i, j = jnp.where(s < 4, 0, i), jnp.where(s < 4, 0, j)
        return (j, i, 0, 0) if swap else (i, j, 0, 0)

    def place(s, bits):
        return ((bits[0] ^ (s % 2)) * 4 + (bits[1] ^ ((s // 2) % 2)) * 2 + (bits[2] ^ (s // 4)), 0)

    piece = (1, 1, rows, half)
    line = pl.BlockSpec((1, width), lambda s, bits: (0, 0))
    span = GROUP * rows
    return pl.pallas_call(
        qkv_kernel,
        out_shape=(
            jax.ShapeDtypeStruct((span, width), BF16),
            jax.ShapeDtypeStruct((span, third), BF16),
            jax.ShapeDtypeStruct((span, 2 * third), BF16),
        ),
        grid_spec=pltpu.PrefetchScalarGridSpec(
            num_scalar_prefetch=1,
            grid=(GROUP,),
            in_specs=[
                pl.BlockSpec(piece, lambda s, bits: near_at(s, False)),
                pl.BlockSpec(piece, lambda s, bits: far_at(s, False)),
                pl.BlockSpec(piece, lambda s, bits: near_at(s, True)),
                pl.BlockSpec(piece, lambda s, bits: far_at(s, True)),
                line,
                line,
                pl.BlockSpec(weight.shape, lambda s, bits: (0, 0)),
                pl.BlockSpec((1, 3 * third), lambda s, bits: (0, 0)),
            ],
            out_specs=[pl.BlockSpec((rows, columns), place) for columns in (width, third, 2 * third)],
        ),
        compiler_params=pltpu.CompilerParams(vmem_limit_bytes=40 << 20),
        cost_estimate=pl.CostEstimate(flops=5 << 30, bytes_accessed=16 << 20, transcendentals=0),
        name="plane_qkv",
    )(
        jnp.stack(position(me)).astype(jnp.int32), a, far_a, b, far_b, gain[None], shift[None], weight, bias[None],
    )


def from_planes(stack, me, devices):
    planes, mine = devices // GROUP, me // GROUP
    got = []
    for k in range(1, planes):
        piece = take(stack, (mine + k) % planes, 0)
        got.append(lax.ppermute(piece, "dev", [(i, (i + k * GROUP) % devices) for i in range(devices)]))
    return take(stack, mine, 0), got


def total_of(own, others):
    total = own.astype(F32)
    for other in others:
        total = total + other.astype(F32)
    return total


def pack_columns(vectors, rows):
    columns = jnp.concatenate([v.reshape(-1, rows).T for v in vectors], axis=1)
    return jnp.pad(columns, ((0, 0), (0, 128 - columns.shape[1])))


def unpack_columns(packed, sizes, rows):
    lines, out, at = packed[:, :16].T, [], 0
    for size in sizes:
        count = size // rows
        part = lines[at : at + count].reshape(count, -1, rows)
        out.append(part.transpose(1, 0, 2).reshape(-1))
        at += count
    return out


def by_parity(transposed, parity, rows):
    blocks = transposed.reshape(-1, 2, rows, transposed.shape[1])
    even, odd = (blocks[:, s].reshape(-1, transposed.shape[1]) for s in range(2))
    return jnp.where(parity == 0, even, odd), jnp.where(parity == 0, odd, even)


def turned(value):
    return value.astype(F32).T.astype(BF16)


def mlp_kernel(
    bits, n2_ref, dml_ref, f1_ref, f2_ref, bias, mlp_ref, dn2_ref, db_ref, keep1, send1, keep2, send2, n2_t
):
    step = pl.program_id(0)
    rows = keep1.shape[1]

    @pl.when(step == 0)
    def _():
        mlp_ref[...] = jnp.zeros_like(mlp_ref)
        dn2_ref[...] = jnp.zeros_like(dn2_ref)
        n2_t[0], n2_t[1] = by_parity(turned(n2_ref[...]), bits[2], rows)

    n2, dml, f1, f2 = n2_ref[...], dml_ref[...], f1_ref[...], f2_ref[...]
    act, slope = gelu_parts(mm(n2, f1) + bias[...])
    act = act.astype(BF16)
    mlp_ref[...] += mm(act, f2)
    dz = lax.dot_general(dml, f2, NT, preferred_element_type=F32) * slope
    db_ref[...] = jnp.sum(dz, axis=0, keepdims=True)
    dz = dz.astype(BF16)
    dn2_ref[...] += lax.dot_general(dz, f1, NT, preferred_element_type=F32)
    for side, out in enumerate((keep1, send1)):
        out[...] = mm(n2_t[side], dz).astype(BF16).reshape(out.shape)
    for part, out in zip(by_parity(turned(act), bits[2], rows), (keep2, send2)):
        out[...] = mm(part, dml).astype(BF16).reshape(out.shape)


def mlp_all(n2, dml, big, bias, me, shard_rows):
    tokens, width = n2.shape
    hidden, owners = bias.shape[0], width // shard_rows
    size = width // 2
    steps = hidden // size
    whole = pl.BlockSpec((tokens, width), lambda s, bits: (0, 0))
    first = pl.BlockSpec((owners // 2, shard_rows, size), lambda s, bits: (0, 0, s))
    second = pl.BlockSpec((owners // 4, shard_rows, width), lambda s, bits: (s % 2, 0, s // 2))
    line = pl.BlockSpec((1, size), lambda s, bits: (0, s))
    grads = jax.ShapeDtypeStruct((owners // 2, shard_rows, hidden), BF16)
    total = jax.ShapeDtypeStruct((tokens, width), F32)
    blocks = hidden // width
    return pl.pallas_call(
        mlp_kernel,
        out_shape=(total, total, jax.ShapeDtypeStruct((1, hidden), F32), grads, grads, grads, grads),
        grid_spec=pltpu.PrefetchScalarGridSpec(
            num_scalar_prefetch=1,
            grid=(steps,),
            in_specs=[
                whole,
                whole,
                pl.BlockSpec((width, size), lambda s, bits: (0, s)),
                pl.BlockSpec((size, width), lambda s, bits: (s % 2, blocks + s // 2)),
                line,
            ],
            out_specs=[whole, whole, line, first, first, second, second],
            scratch_shapes=[pltpu.VMEM((2, width // 2, tokens), BF16)],
        ),
        compiler_params=pltpu.CompilerParams(vmem_limit_bytes=52 << 20),
        cost_estimate=pl.CostEstimate(
            flops=4 * tokens * width * hidden, bytes_accessed=8 * width * hidden, transcendentals=2 * tokens * hidden
        ),
        name="mlp_all",
    )(jnp.stack(position(me)).astype(jnp.int32), n2, dml, big, big, bias[None])


def grad_kernel(bits, a_ref, b_ref, keep_ref, send_ref):
    for part, out in zip(by_parity(turned(a_ref[...]), bits[2], keep_ref.shape[1]), (keep_ref, send_ref)):
        out[...] = mm(part, b_ref[...]).astype(BF16).reshape(out.shape)


def weight_grad(a, b, rows, me):
    out = jax.ShapeDtypeStruct((a.shape[1] // (2 * rows), rows, b.shape[1]), BF16)
    return pl.pallas_call(
        grad_kernel,
        out_shape=(out, out),
        grid_spec=pltpu.PrefetchScalarGridSpec(num_scalar_prefetch=1, grid=(1,)),
        compiler_params=pltpu.CompilerParams(vmem_limit_bytes=40 << 20),
        cost_estimate=pl.CostEstimate(
            flops=2 * a.size * b.shape[1], bytes_accessed=2 * (a.size + b.size + 2 * out.size), transcendentals=0
        ),
        name="weight_grad",
    )(jnp.stack(position(me)).astype(jnp.int32), a, b)


def body(
    tokens,
    cotangent,
    image_lengths,
    ln1_gain,
    ln1_bias,
    qkv_weight,
    qv_bias,
    proj_weight,
    proj_bias,
    scale_attn,
    ln2_gain,
    ln2_bias,
    fc1_weight,
    fc1_bias,
    fc2_weight,
    fc2_bias,
    scale_mlp,
):
    devices = lax.axis_size("dev")
    me = lax.axis_index("dev")
    rows, width = tokens.shape
    vectors = (
        ln1_gain, ln1_bias, qv_bias, proj_bias, scale_attn, ln2_gain, ln2_bias, fc1_bias, fc2_bias, scale_mlp,
    )
    sizes = [v.shape[0] for v in vectors]
    shard_rows, hidden = qkv_weight.shape[0], fc1_weight.shape[1]
    by_axes = shard_rows % 32 == 0
    blocks = hidden // width
    slab = qkv_weight.reshape(shard_rows, 3, GROUP, -1).transpose(2, 0, 1, 3).reshape(GROUP, shard_rows, -1)
    packed = jnp.broadcast_to(pack_columns(vectors, shard_rows), (GROUP, shard_rows, 128))
    slab = jnp.concatenate([slab, packed], axis=2)
    slab = jnp.broadcast_to(slab[None], (devices // GROUP, *slab.shape)).reshape(devices, shard_rows, -1)
    slab = lax.all_to_all(slab, "dev", 0, 0, tiled=True).reshape(width, -1)
    packed, slab = slab[:, -128:], slab[:, :-128]
    spread = unpack_columns(packed.astype(F32), sizes, shard_rows)
    gain1, shift1, bias_qv, bias_proj, layer_attn, gain2, shift2, bias_fc1, bias_fc2, layer_mlp = spread
    if by_axes:
        first = fc1_weight.reshape(shard_rows, devices, blocks, shard_rows).transpose(0, 2, 1, 3)
        second = fc2_weight.reshape(blocks, shard_rows, width).transpose(1, 0, 2)
        big = jnp.concatenate(
            [first.reshape(shard_rows, hidden), second.reshape(shard_rows, hidden), proj_weight], axis=1
        )
        big = gathered(big)
        w_proj = big[:, 2 * hidden :]
    else:
        w_proj, big = gathered(proj_weight), gathered(fc1_weight)
        w_fc2 = gathered(fc2_weight)
    qkv_late, packed = lax.optimization_barrier((qkv_weight, packed))
    w_qkv = gathered(qkv_late)

    span = GROUP * rows
    halo = -(-(SEQ - 1) // BK) * BK
    base = (me // GROUP) * span - halo
    places = base + halo + jnp.arange(span, dtype=jnp.int32)
    ends = jnp.cumsum(image_lengths)
    before = ends[None, :] <= places[:, None]
    begin = jnp.max(jnp.where(before, ends[None, :], 0), axis=1)
    finish = jnp.min(jnp.where(before, devices * rows, ends[None, :]), axis=1)
    seg = jnp.stack([begin - base, finish - base]).astype(jnp.int32)
    low = seg[0, ::BQ] // BK
    high = -(-seg[1, BQ - 1 :: BQ] // BK)

    x = tokens.astype(F32)
    u1, rstd1 = normalised(x)
    heads_width = width // GROUP
    mine = (me % GROUP) * heads_width
    bias = jnp.concatenate(
        [
            lax.dynamic_slice(bias_qv, (mine,), (heads_width,)),
            jnp.zeros((heads_width,), F32),
            lax.dynamic_slice(bias_qv, (width + mine,), (heads_width,)),
        ]
    )
    n1, q, kv = plane_qkv(tokens, gain1, shift1, slab, bias, me, devices)
    prefetch, edge_blocks = (low, high), halo // BK
    left = shifted(kv[span - halo :], GROUP, devices)
    right = shifted(kv[:halo], -GROUP, devices)
    acc, stat = forward_mid(prefetch, seg, q, kv, edge_blocks)
    acc, stat, left, right = lax.optimization_barrier((acc, stat, left, right))
    o_heads, lse = forward_edge(prefetch, seg, q, left, right, acc, stat)
    (o,) = to_tokens([o_heads], devices)

    branch = mm(o, w_proj) + bias_proj
    y1 = x + layer_attn * branch
    u2, rstd2 = normalised(y1)
    n2 = (u2 * gain2 + shift2).astype(BF16)
    g = cotangent.astype(F32)
    dm = layer_mlp * g
    d_fc2_bias = jnp.sum(dm, axis=0)
    dml = dm.astype(BF16)
    if by_axes:
        bias_hidden = bias_fc1.reshape(devices, blocks, shard_rows).transpose(1, 0, 2).reshape(-1)
        mlp, dn2, d_fc1_bias, keep1, send1, keep2, send2 = mlp_all(n2, dml, big, bias_hidden, me, shard_rows)
        d_fc1_bias = d_fc1_bias.reshape(blocks, devices, shard_rows).transpose(1, 0, 2).reshape(-1)
    else:
        act, slope = gelu_parts(mm(n2, big) + bias_fc1)
        act = act.astype(BF16)
        mlp = mm(act, w_fc2)
        dz = mm_t(dml, w_fc2) * slope
        d_fc1_bias = jnp.sum(dz, axis=0)
        dz = dz.astype(BF16)
        dn2 = mm_t(dz, big)
        d_fc1, d_fc2 = scattered(t_mm(n2, dz)), scattered(t_mm(act, dml))
    mlp = mlp + bias_fc2
    block_out = (y1 + layer_mlp * mlp).astype(BF16)
    d_scale_mlp = jnp.sum(g * mlp, axis=0)
    d_gain2 = jnp.sum(dn2 * u2, axis=0)
    d_shift2 = jnp.sum(dn2, axis=0)
    dy1 = g + norm_back(u2, rstd2, dn2 * gain2)
    d_scale_attn = jnp.sum(dy1 * branch, axis=0)
    db = layer_attn * dy1
    d_proj_bias = jnp.sum(db, axis=0)
    dbl = db.astype(BF16)
    do = mm_t(dbl, w_proj).astype(BF16)

    if by_axes:
        y, x, _ = position(me)
        keep3, send3 = weight_grad(o, dbl, shard_rows, me)
        got1, got2, got3 = (swapped(s, 1, devices) for s in (send1, send2, send3))
        do, got1, got2, got3 = lax.optimization_barrier((do, got1, got2, got3))
        view = (devices // GROUP, 2, 2, shard_rows)
        own1, own2, own3 = (s.reshape(*view, -1) for s in (keep1, keep2, keep3))
        got1, got2, got3 = (s.reshape(*view, -1) for s in (got1, got2, got3))
        cut = width // 2

        def part(index, axis, which):
            cols = slice(0, cut) if which == 0 else slice(cut, width)
            pairs = ((own1, got1), (own2, got2))[which], (own3[..., cols], got3[..., cols])
            both = [take(m, index, axis).astype(F32) + take(n, index, axis).astype(F32) for m, n in pairs]
            return jnp.concatenate(both, axis=-1).astype(BF16)

        out_a, out_b = part(1 - x, 2, 0), part(1 - y, 1, 1)
    else:
        d_proj = scattered(t_mm(o, dbl))

    (do_heads,) = to_heads([do], devices)
    if by_axes:
        do_heads, out_a, out_b = lax.optimization_barrier((do_heads, out_a, out_b))
        in_a, in_b = swapped(out_a, 2, devices), swapped(out_b, 4, devices)
    part_dq, mid0, edge = backward_first(prefetch, seg, q, kv, left, right, o_heads, do_heads, lse)
    if by_axes:
        part_dq, in_a, in_b, w_qkv = lax.optimization_barrier((part_dq, in_a, in_b, w_qkv))
        sum_a = (part(x, 2, 0).astype(F32) + in_a.astype(F32)).astype(BF16)
        sum_b = (part(y, 1, 1).astype(F32) + in_b.astype(F32)).astype(BF16)
        out_a, out_b = take(sum_a, 1 - y, 1), take(sum_b, 1 - x, 1)
        part_dq, out_a, out_b = lax.optimization_barrier((part_dq, out_a, out_b))
        in_a, in_b = swapped(out_a, 4, devices), swapped(out_b, 2, devices)
    from_right = shifted(edge[0], -GROUP, devices)
    from_left = shifted(edge[1], GROUP, devices)
    dq, mid1 = backward_second(prefetch, seg, q, kv, o_heads, do_heads, lse, part_dq, edge_blocks)
    dq, mid1, from_left, from_right = lax.optimization_barrier((dq, mid1, from_left, from_right))
    if by_axes:
        dq, in_a, in_b = lax.optimization_barrier((dq, in_a, in_b))
    rest = span - halo
    mid = mid0 + mid1 + jnp.pad(from_left.astype(F32), ((0, rest), (0, 0)))
    mid = mid + jnp.pad(from_right.astype(F32), ((rest, 0), (0, 0)))
    mid = mid.astype(BF16)
    d_heads = jnp.concatenate([dq, mid], axis=1)
    if by_axes:
        d_heads, in_a, in_b = lax.optimization_barrier((d_heads, in_a, in_b))
        sum_a = take(sum_a, y, 1).astype(F32) + in_a.astype(F32)
        sum_b = take(sum_b, x, 1).astype(F32) + in_b.astype(F32)
        d_heads, sums = lax.optimization_barrier((d_heads, jnp.concatenate([sum_a, sum_b], axis=-1).astype(BF16)))
        own_sums, sums = from_planes(sums, me, devices)
    dqkv = in_plane(d_heads.reshape(GROUP, rows, -1), devices).reshape(GROUP, rows, 3, -1)
    if by_axes:
        dqkv, sums = lax.optimization_barrier((dqkv, sums))
    dqkv = dqkv.transpose(1, 2, 0, 3).reshape(rows, 3 * width)
    dq, dv = dqkv[:, :width], dqkv[:, 2 * width :]
    d_qkv = t_mm(n1, d_heads).astype(BF16).reshape(devices // GROUP, GROUP, shard_rows, -1)
    d_qkv = total_of(*from_planes(d_qkv, me, devices))
    d_qkv = in_plane(d_qkv, devices).reshape(GROUP, shard_rows, 3, -1)
    d_qkv = d_qkv.transpose(1, 2, 0, 3).reshape(shard_rows, 3 * width)
    if by_axes:
        sums = total_of(own_sums, sums)
        d_fc1 = sums[:, :hidden].reshape(shard_rows, blocks, devices, shard_rows).transpose(0, 2, 1, 3)
        d_fc1 = d_fc1.reshape(shard_rows, hidden)
        at = hidden + cut
        d_fc2 = sums[:, at : at + hidden].reshape(shard_rows, blocks, width).transpose(1, 0, 2)
        d_fc2 = d_fc2.reshape(blocks * shard_rows, width)
        d_proj = jnp.concatenate([sums[:, hidden:at], sums[:, at + hidden :]], axis=1)
    d_qv_bias = jnp.concatenate([jnp.sum(dq.astype(F32), axis=0), jnp.sum(dv.astype(F32), axis=0)])
    dn1 = mm_t(dqkv, w_qkv)
    d_gain1 = jnp.sum(dn1 * u1, axis=0)
    d_shift1 = jnp.sum(dn1, axis=0)
    grad_tokens = (dy1 + norm_back(u1, rstd1, dn1 * gain1)).astype(BF16)

    small = (
        d_gain1, d_shift1, d_qv_bias, d_proj_bias, d_scale_attn, d_gain2, d_shift2, d_fc1_bias, d_fc2_bias, d_scale_mlp,
    )
    small = lax.all_to_all(pack(small, devices), "dev", 0, 0, tiled=True)
    small = jnp.sum(small, axis=0, keepdims=True)
    s_gain1, s_shift1, s_qv, s_proj, s_attn, s_gain2, s_shift2, s_fc1, s_fc2, s_mlp = unpack(small, sizes)
    return (
        block_out,
        grad_tokens,
        s_gain1,
        s_shift1,
        d_qkv,
        s_qv,
        d_proj,
        s_proj,
        s_attn,
        s_gain2,
        s_shift2,
        d_fc1,
        s_fc1,
        d_fc2,
        s_fc2,
        s_mlp,
    )


def solution(mesh):
    matrix, vector = P("dev", None), P("dev")
    return jax.shard_map(
        body,
        mesh=mesh,
        in_specs=(
            matrix, matrix, P(), vector, vector, matrix, vector, matrix, vector, vector, vector, vector, matrix,
            vector, matrix, vector, vector,
        ),
        out_specs=(
            matrix, matrix, vector, vector, matrix, vector, matrix, vector, vector, vector, vector, matrix, vector,
            matrix, vector, vector,
        ),
        check_vma=False,
    )
```

```python
import functools

import jax
import jax.numpy as jnp
from jax import lax
from jax.experimental import pallas as pl
from jax.experimental.pallas import tpu as pltpu
from jax.sharding import PartitionSpec as P

BQ = 256
BK = 256
SLAB = 2 * BK
HD = 64
LOG2E = 1.4426950408889634
SCALE = 0.125
MASKED = -1e30
NT = (((1,), (1,)), ((), ()))


def head_halves(block):
    first = lax.broadcasted_iota(jnp.int32, block.shape, 1) < HD
    zero = jnp.zeros_like(block)
    return jnp.where(first, block, zero), jnp.where(first, zero, block)


def transpose_into(target, source, column):
    width = target.shape[0]
    for j in range(source.shape[0] // BK):
        part = source[j * BK : (j + 1) * BK, column : column + width].astype(jnp.float32)
        target[:, j * BK : (j + 1) * BK] = part.T.astype(target.dtype)


def slabs(low, high, first, last):
    low = jnp.clip(low, first, last) - first
    count = (jnp.clip(high, first, last) - first - low + 1) // 2
    return jnp.minimum(low, last - first - 2 * count), count


def slab_rows(start, t):
    return pl.ds(pl.multiple_of((start + 2 * t) * BK, BK), SLAB)


def forward_over(span, kv_ref, v_t, offset, q_heads, seg, carry):
    start, count = span
    width = q_heads[0].shape[1]
    begin, end = seg[0:1, :], seg[1:2, :]
    place = lax.broadcasted_iota(jnp.int32, (SLAB, BQ), 0) + offset

    def one_slab(t, carry):
        rows = slab_rows(start, t)
        keys = kv_ref[rows, :width]
        at = place + (start + 2 * t) * BK
        valid = (at >= begin) & (at < end)
        out = []
        for h in range(2):
            top, total, acc = carry[h]
            s = lax.dot_general(keys, q_heads[h], NT, preferred_element_type=jnp.float32)
            s = jnp.where(valid, s * (SCALE * LOG2E), MASKED)
            new_top = jnp.maximum(top, jnp.max(s, axis=0, keepdims=True))
            p = jnp.exp2(s - new_top)
            fade = jnp.exp2(top - new_top)
            total = total * fade + jnp.sum(p, axis=0, keepdims=True)
            v_part = v_t[h * HD : (h + 1) * HD, rows]
            acc = acc * fade + jnp.dot(v_part, p.astype(jnp.bfloat16), preferred_element_type=jnp.float32)
            out.append((new_top, total, acc))
        return tuple(out)

    return lax.fori_loop(0, count, one_slab, carry)


def forward_mid_kernel(low, high, seg, q_ref, kv_ref, acc_ref, stat_ref, v_t, *, edge):
    step = pl.program_id(0)

    @pl.when(step == 0)
    def _():
        transpose_into(v_t, kv_ref, q_ref.shape[1])

    start = (
        jnp.full((1, BQ), MASKED, jnp.float32),
        jnp.zeros((1, BQ), jnp.float32),
        jnp.zeros((HD, BQ), jnp.float32),
    )
    blocks = kv_ref.shape[0] // BK
    span = slabs(low[step], high[step], edge, edge + blocks)
    done = forward_over(span, kv_ref, v_t, edge * BK, head_halves(q_ref[...]), seg, (start, start))
    for h, (top, total, acc) in enumerate(done):
        stat_ref[2 * h : 2 * h + 1, :] = top
        stat_ref[2 * h + 1 : 2 * h + 2, :] = total
        acc_ref[h * HD : (h + 1) * HD, :] = acc


def forward_edge_kernel(
    low, high, seg, q_ref, left_ref, right_ref, acc_ref, stat_ref, o_ref, lse_ref, left_t, right_t, *, last
):
    step = pl.program_id(0)
    width = q_ref.shape[1]
    edge = left_ref.shape[0] // BK

    @pl.when(step == 0)
    def _():
        transpose_into(left_t, left_ref, width)
        transpose_into(right_t, right_ref, width)

    carry = tuple(
        (stat_ref[2 * h : 2 * h + 1, :], stat_ref[2 * h + 1 : 2 * h + 2, :], acc_ref[h * HD : (h + 1) * HD, :])
        for h in range(2)
    )
    q_heads = head_halves(q_ref[...])
    span = slabs(low[step], high[step], 0, edge)
    carry = forward_over(span, left_ref, left_t, 0, q_heads, seg, carry)
    span = slabs(low[step], high[step], last, last + edge)
    carry = forward_over(span, right_ref, right_t, last * BK, q_heads, seg, carry)
    o_ref[...] = jnp.concatenate([acc / total for _, total, acc in carry], axis=0).T.astype(o_ref.dtype)
    for h, (top, total, _) in enumerate(carry):
        lse_ref[h : h + 1, :] = top + jnp.log2(total)


def backward_setup(q_ref, do_ref, o_ref, lse_ref, heads):
    prod = (do_ref[...].astype(jnp.float32) * o_ref[...].astype(jnp.float32)).T
    q_heads, do_heads = head_halves(q_ref[...]), head_halves(do_ref[...])
    return [
        (
            h,
            q_heads[h],
            do_heads[h],
            jnp.sum(prod[h * HD : (h + 1) * HD], axis=0, keepdims=True),
            lse_ref[h : h + 1, :],
        )
        for h in heads
    ]


def backward_over(span, kv_ref, k_t, dkv, dq_t, offset, heads, seg):
    start, count = span
    width = dq_t.shape[0]
    begin, end = seg[0:1, :], seg[1:2, :]
    place = lax.broadcasted_iota(jnp.int32, (SLAB, BQ), 0) + offset
    q_all = jnp.concatenate([q for _, q, _, _, _ in heads], axis=0)
    do_all = jnp.concatenate([d for _, _, d, _, _ in heads], axis=0)

    @pl.loop(0, count)
    def _(t):
        rows = slab_rows(start, t)
        keys, values = kv_ref[rows, :width], kv_ref[rows, width:]
        at = place + (start + 2 * t) * BK
        valid = (at >= begin) & (at < end)
        ps, dss = [], []
        for h, q, do, centre, lse in heads:
            s = lax.dot_general(keys, q, NT, preferred_element_type=jnp.float32)
            p = jnp.where(valid, jnp.exp2(s * (SCALE * LOG2E) - lse), 0.0)
            dp = lax.dot_general(values, do, NT, preferred_element_type=jnp.float32)
            ds = (p * (dp - centre)).astype(jnp.bfloat16)
            ps.append(p.astype(jnp.bfloat16))
            dss.append(ds)
            part = slice(h * HD, (h + 1) * HD)
            dq_t[part, :] += jnp.dot(k_t[part, rows], ds, preferred_element_type=jnp.float32)
        dkv[rows, :width] += jnp.dot(jnp.concatenate(dss, axis=1), q_all, preferred_element_type=jnp.float32)
        dkv[rows, width:] += jnp.dot(jnp.concatenate(ps, axis=1), do_all, preferred_element_type=jnp.float32)


def backward_first_kernel(
    low, high, seg, q_ref, kv_ref, left_ref, right_ref, o_ref, do_ref, lse_ref, dq_t, mid_ref, edge_ref,
    left_t, right_t, k_t, dkv, *, last
):
    step = pl.program_id(0)
    width = q_ref.shape[1]
    edge = left_ref.shape[0] // BK

    @pl.when(step == 0)
    def _():
        transpose_into(left_t, left_ref, 0)
        transpose_into(right_t, right_ref, 0)
        transpose_into(k_t, kv_ref, 0)
        dkv[...] = jnp.zeros_like(dkv)
        mid_ref[...] = jnp.zeros_like(mid_ref)

    heads = backward_setup(q_ref, do_ref, o_ref, lse_ref, range(2))
    dq_t[...] = jnp.zeros_like(dq_t)
    span = slabs(low[step], high[step], 0, edge)
    backward_over(span, left_ref, left_t, dkv.at[0], dq_t, 0, heads, seg)
    span = slabs(low[step], high[step], last, last + edge)
    backward_over(span, right_ref, right_t, dkv.at[1], dq_t, last * BK, heads, seg)
    span = slabs(low[step], high[step], edge, last)
    backward_over(span, kv_ref, k_t, mid_ref, dq_t, edge * BK, heads[:1], seg)

    @pl.when(step == pl.num_programs(0) - 1)
    def _():
        mid_ref[:, :width] = mid_ref[:, :width] * SCALE
        for side in range(2):
            for j in range(edge):
                part = slice(j * BK, (j + 1) * BK)
                edge_ref[side, part, :width] = (dkv[side, part, :width] * SCALE).astype(edge_ref.dtype)
                edge_ref[side, part, width:] = dkv[side, part, width:].astype(edge_ref.dtype)


def backward_mid_kernel(
    low, high, seg, q_ref, kv_ref, o_ref, do_ref, lse_ref, part_ref, dq_ref, mid_ref, k_t, dq_t, *, edge
):
    step = pl.program_id(0)
    width = q_ref.shape[1]

    @pl.when(step == 0)
    def _():
        transpose_into(k_t, kv_ref, 0)
        mid_ref[...] = jnp.zeros_like(mid_ref)

    dq_t[...] = part_ref[...]
    blocks = kv_ref.shape[0] // BK
    span = slabs(low[step], high[step], edge, edge + blocks)
    heads = backward_setup(q_ref, do_ref, o_ref, lse_ref, [1])
    backward_over(span, kv_ref, k_t, mid_ref, dq_t, edge * BK, heads, seg)
    dq_ref[...] = (dq_t[...] * SCALE).T.astype(dq_ref.dtype)

    @pl.when(step == pl.num_programs(0) - 1)
    def _():
        mid_ref[:, :width] = mid_ref[:, :width] * SCALE


def whole_spec(array):
    return pl.BlockSpec(array.shape, lambda i, *_: (0,) * len(array.shape))


def attention_call(kernel, name, prefetch, inputs, in_kinds, outputs, out_kinds, scratch, work):
    span = prefetch[0].shape[0] * BQ

    def spec(array, kind):
        if kind == "r":
            return pl.BlockSpec((BQ, array.shape[1]), lambda i, *_: (i, 0))
        if kind == "c":
            return pl.BlockSpec((array.shape[0], BQ), lambda i, *_: (0, i))
        return whole_spec(array)

    return pl.pallas_call(
        kernel,
        out_shape=tuple(outputs),
        grid_spec=pltpu.PrefetchScalarGridSpec(
            num_scalar_prefetch=2,
            grid=(span // BQ,),
            in_specs=[spec(a, k) for a, k in zip(inputs, in_kinds)],
            out_specs=[spec(a, k) for a, k in zip(outputs, out_kinds)],
            scratch_shapes=scratch,
        ),
        compiler_params=pltpu.CompilerParams(vmem_limit_bytes=48 << 20),
        cost_estimate=pl.CostEstimate(flops=work << 30, bytes_accessed=8 << 20, transcendentals=span * 128),
        name=name,
    )(*prefetch, *inputs)


def shaped(*shape, dtype=jnp.float32):
    return jax.ShapeDtypeStruct(shape, dtype)


def forward_mid(prefetch, seg, q, kv, edge):
    span, width = q.shape
    return attention_call(
        functools.partial(forward_mid_kernel, edge=edge), "forward_mid", prefetch, [seg, q, kv], "crw",
        [shaped(width, span), shaped(8, span)], "cc", [pltpu.VMEM((width, span), jnp.bfloat16)], 3,
    )


def forward_edge(prefetch, seg, q, left, right, acc, stat):
    span, width = q.shape
    halo = pltpu.VMEM((width, left.shape[0]), jnp.bfloat16)
    return attention_call(
        functools.partial(forward_edge_kernel, last=(left.shape[0] + span) // BK), "forward_edge", prefetch,
        [seg, q, left, right, acc, stat], "crwwcc",
        [shaped(span, width, dtype=jnp.bfloat16), shaped(8, span)], "rc", [halo, halo], 3,
    )


def backward_first(prefetch, seg, q, kv, left, right, o, do, lse):
    span, width = q.shape
    halo = pltpu.VMEM((width, left.shape[0]), jnp.bfloat16)
    return attention_call(
        functools.partial(backward_first_kernel, last=(left.shape[0] + span) // BK), "backward_first", prefetch,
        [seg, q, kv, left, right, o, do, lse], "crwwwrrc",
        [shaped(width, span), shaped(*kv.shape), shaped(2, *left.shape, dtype=jnp.bfloat16)], "cww",
        [halo, halo, pltpu.VMEM((width, span), jnp.bfloat16), pltpu.VMEM((2, *left.shape), jnp.float32)], 3,
    )


def backward_second(prefetch, seg, q, kv, o, do, lse, part, edge):
    span, width = q.shape
    return attention_call(
        functools.partial(backward_mid_kernel, edge=edge), "backward_second", prefetch,
        [seg, q, kv, o, do, lse, part], "crwrrcc",
        [shaped(span, width, dtype=jnp.bfloat16), shaped(*kv.shape)], "rw",
        [pltpu.VMEM((width, span), jnp.bfloat16), pltpu.VMEM((width, BQ), jnp.float32)], 3,
    )


HEADS = 16
SEQ = 1370
GROUP = 8
EPS = 1e-06
F32, BF16 = jnp.float32, jnp.bfloat16


def mm(left, right):
    return jnp.dot(left, right, preferred_element_type=F32)


def mm_t(left, right):
    return jnp.einsum("tf,df->td", left, right, preferred_element_type=F32)


def t_mm(left, right):
    return jnp.einsum("td,tf->df", left, right, preferred_element_type=F32)


def normalised(value):
    centre = value - jnp.mean(value, axis=-1, keepdims=True)
    rstd = lax.rsqrt(jnp.mean(centre * centre, axis=-1, keepdims=True) + EPS)
    return centre * rstd, rstd


def norm_back(unit, rstd, grad):
    first = jnp.mean(grad, axis=-1, keepdims=True)
    second = jnp.mean(grad * unit, axis=-1, keepdims=True)
    return rstd * (grad - first - unit * second)


def gelu_parts(z):
    half = 0.5 * (1.0 + lax.erf(z * 0.7071067811865476))
    slope = half + z * (0.3989422804014327 * jnp.exp(-0.5 * z * z))
    return z * half, slope


def groups_of(count):
    return [list(range(first, first + GROUP)) for first in range(0, count, GROUP)]


def gathered(shard):
    return lax.all_gather(shard, "dev", axis=0, tiled=True)


def scattered(whole):
    return lax.psum_scatter(whole, "dev", scatter_dimension=0, tiled=True)


def pack(vectors, count):
    return jnp.concatenate([v.reshape(count, -1) for v in vectors], axis=1)


def unpack(packed, sizes):
    out, at = [], 0
    for size in sizes:
        out.append(packed[:, at : at + size].reshape(-1))
        at += size
    return out


def to_heads(parts, devices):
    rows = parts[0].shape[0]
    sent = jnp.stack([p.reshape(rows, GROUP, -1) for p in parts], axis=2)
    sent = sent.transpose(1, 0, 2, 3)
    back = lax.all_to_all(sent, "dev", 0, 0, axis_index_groups=groups_of(devices), tiled=True)
    return [back[:, :, i].reshape(GROUP * rows, -1) for i in range(len(parts))]


def to_tokens(parts, devices):
    rows = parts[0].shape[0] // GROUP
    sent = jnp.stack([p.reshape(GROUP, rows, -1) for p in parts], axis=2)
    back = lax.all_to_all(sent, "dev", 0, 0, axis_index_groups=groups_of(devices), tiled=True)
    return [back[:, :, i].transpose(1, 0, 2).reshape(rows, -1) for i in range(len(parts))]


def shifted(shard, by, devices):
    pairs = [(i, i + by) for i in range(devices) if 0 <= i + by < devices]
    return lax.ppermute(shard, "dev", pairs)


def take(stack, index, axis):
    return lax.dynamic_index_in_dim(stack, index, axis, keepdims=False)


def swapped(value, bit, devices):
    return lax.ppermute(value, "dev", [(i, i ^ bit) for i in range(devices)])


def in_plane(stack, devices):
    return lax.all_to_all(stack, "dev", 0, 0, axis_index_groups=groups_of(devices), tiled=True)


def position(me):
    return (me // 4) % 2, (me // 2) % 2, me % 2


def qkv_kernel(bits, near_a, far_a, near_b, far_b, slab, n1_ref, q_ref, kv_ref, lines, bias, *, rows):
    step = pl.program_id(0)
    third = q_ref.shape[1]
    width = slab.shape[0]

    @pl.when(step == 0)
    def _():
        lines[...] = slab[:, 3 * third :].astype(F32).T
        group = bits[3]
        unit = lax.broadcasted_iota(jnp.int32, (width, third), 0)
        place = lax.broadcasted_iota(jnp.int32, (width, third), 1)
        some = lines[0:16, :].astype(BF16)
        bias[...] = jnp.zeros_like(bias)
        for part, first in ((0, 0), (2, width // 2)):
            total = jnp.zeros((1, third), F32)
            for column in range(2):
                at = first + group * (third // 2) + (place // (2 * rows)) * rows + place % rows
                chosen = (unit == at) & ((place // rows) % 2 == column)
                total = total + mm(some, jnp.where(chosen, 1.0, 0.0).astype(BF16))[2 + column : 3 + column]
            bias[0:1, part * third : (part + 1) * third] = total

    far = step >= 4
    left = jnp.where(far, far_a[0, 0], near_a[0, 0])
    right = jnp.where(far, far_b[0, 0], near_b[0, 0])
    unit, _ = normalised(jnp.concatenate([left, right], axis=1).astype(F32))
    n1 = (unit * lines[0:1, :] + lines[1:2, :]).astype(BF16)
    n1_ref[...] = n1
    out = (mm(n1, slab[:, : 3 * third]) + bias[0:1, :]).astype(BF16)
    q_ref[...] = out[:, :third]
    kv_ref[...] = out[:, third:]


def plane_qkv(tokens, slab, me, devices):
    rows, width = tokens.shape
    half, third = width // 2, (slab.shape[1] - 128) // 3
    a, b = tokens[:, :half], tokens[:, half:]
    a = jnp.stack([a, swapped(a, 4, devices)])
    b = jnp.stack([b, swapped(b, 2, devices)])
    a = jnp.stack([a, swapped(a, 2, devices)])
    b = jnp.stack([b, swapped(b, 4, devices)])
    far_a, far_b = swapped(a, 1, devices), swapped(b, 1, devices)

    def near_at(s, swap):
        i, j = (s // 2) % 2, s % 2
        i, j = jnp.where(s < 4, i, 1), jnp.where(s < 4, j, 1)
        return (j, i, 0, 0) if swap else (i, j, 0, 0)

    def far_at(s, swap):
        i, j = (s // 2) % 2, s % 2
        i, j = jnp.where(s < 4, 0, i), jnp.where(s < 4, 0, j)
        return (j, i, 0, 0) if swap else (i, j, 0, 0)

    def place(s, bits):
        return ((bits[0] ^ (s % 2)) * 4 + (bits[1] ^ ((s // 2) % 2)) * 2 + (bits[2] ^ (s // 4)), 0)

    piece = (1, 1, rows, half)
    span = GROUP * rows
    return pl.pallas_call(
        functools.partial(qkv_kernel, rows=width // devices),
        out_shape=(
            jax.ShapeDtypeStruct((span, width), BF16),
            jax.ShapeDtypeStruct((span, third), BF16),
            jax.ShapeDtypeStruct((span, 2 * third), BF16),
        ),
        grid_spec=pltpu.PrefetchScalarGridSpec(
            num_scalar_prefetch=1,
            grid=(GROUP,),
            in_specs=[
                pl.BlockSpec(piece, lambda s, bits: near_at(s, False)),
                pl.BlockSpec(piece, lambda s, bits: far_at(s, False)),
                pl.BlockSpec(piece, lambda s, bits: near_at(s, True)),
                pl.BlockSpec(piece, lambda s, bits: far_at(s, True)),
                pl.BlockSpec(slab.shape, lambda s, bits: (0, 0)),
            ],
            out_specs=[pl.BlockSpec((rows, columns), place) for columns in (width, third, 2 * third)],
            scratch_shapes=[pltpu.VMEM((128, width), F32), pltpu.VMEM((8, 3 * third), F32)],
        ),
        compiler_params=pltpu.CompilerParams(vmem_limit_bytes=40 << 20),
        cost_estimate=pl.CostEstimate(flops=5 << 30, bytes_accessed=16 << 20, transcendentals=0),
        name="plane_qkv",
    )(
        jnp.stack([*position(me), me % GROUP]).astype(jnp.int32), a, far_a, b, far_b, slab,
    )


def from_planes(stack, me, devices):
    planes, mine = devices // GROUP, me // GROUP
    got = []
    for k in range(1, planes):
        piece = take(stack, (mine + k) % planes, 0)
        got.append(lax.ppermute(piece, "dev", [(i, (i + k * GROUP) % devices) for i in range(devices)]))
    return take(stack, mine, 0), got


def total_of(own, others):
    total = own.astype(F32)
    for other in others:
        total = total + other.astype(F32)
    return total


def pack_columns(vectors, rows):
    columns = jnp.concatenate([v.reshape(-1, rows).T for v in vectors], axis=1)
    return jnp.pad(columns, ((0, 0), (0, 128 - columns.shape[1])))


def unpack_columns(packed, sizes, rows):
    lines, out, at = packed[:, :16].T, [], 0
    for size in sizes:
        count = size // rows
        part = lines[at : at + count].reshape(count, -1, rows)
        out.append(part.transpose(1, 0, 2).reshape(-1))
        at += count
    return out


def by_parity(transposed, parity, rows):
    blocks = transposed.reshape(-1, 2, rows, transposed.shape[1])
    even, odd = (blocks[:, s].reshape(-1, transposed.shape[1]) for s in range(2))
    return jnp.where(parity == 0, even, odd), jnp.where(parity == 0, odd, even)


def turned(value):
    return value.astype(F32).T.astype(BF16)


def mlp_kernel(
    bits, n2_ref, dml_ref, f1_ref, f2_ref, bias, mlp_ref, dn2_ref, db_ref, keep1, send1, keep2, send2, n2_t
):
    step = pl.program_id(0)
    rows = keep1.shape[1]

    @pl.when(step == 0)
    def _():
        mlp_ref[...] = jnp.zeros_like(mlp_ref)
        dn2_ref[...] = jnp.zeros_like(dn2_ref)
        n2_t[0], n2_t[1] = by_parity(turned(n2_ref[...]), bits[2], rows)

    n2, dml, f1, f2 = n2_ref[...], dml_ref[...], f1_ref[...], f2_ref[...]
    act, slope = gelu_parts(mm(n2, f1) + bias[...])
    act = act.astype(BF16)
    mlp_ref[...] += mm(act, f2)
    dz = lax.dot_general(dml, f2, NT, preferred_element_type=F32) * slope
    db_ref[...] = jnp.sum(dz, axis=0, keepdims=True)
    dz = dz.astype(BF16)
    dn2_ref[...] += lax.dot_general(dz, f1, NT, preferred_element_type=F32)
    for side, out in enumerate((keep1, send1)):
        out[...] = mm(n2_t[side], dz).astype(BF16).reshape(out.shape)
    for part, out in zip(by_parity(turned(act), bits[2], rows), (keep2, send2)):
        out[...] = mm(part, dml).astype(BF16).reshape(out.shape)


def mlp_all(n2, dml, big, bias, me, shard_rows):
    tokens, width = n2.shape
    hidden, owners = bias.shape[0], width // shard_rows
    size = width // 2
    steps = hidden // size
    whole = pl.BlockSpec((tokens, width), lambda s, bits: (0, 0))
    first = pl.BlockSpec((owners // 2, shard_rows, size), lambda s, bits: (0, 0, s))
    second = pl.BlockSpec((owners // 4, shard_rows, width), lambda s, bits: (s % 2, 0, s // 2))
    line = pl.BlockSpec((1, size), lambda s, bits: (0, s))
    grads = jax.ShapeDtypeStruct((owners // 2, shard_rows, hidden), BF16)
    total = jax.ShapeDtypeStruct((tokens, width), F32)
    blocks = hidden // width
    return pl.pallas_call(
        mlp_kernel,
        out_shape=(total, total, jax.ShapeDtypeStruct((1, hidden), F32), grads, grads, grads, grads),
        grid_spec=pltpu.PrefetchScalarGridSpec(
            num_scalar_prefetch=1,
            grid=(steps,),
            in_specs=[
                whole,
                whole,
                pl.BlockSpec((width, size), lambda s, bits: (0, s)),
                pl.BlockSpec((size, width), lambda s, bits: (s % 2, blocks + s // 2)),
                line,
            ],
            out_specs=[whole, whole, line, first, first, second, second],
            scratch_shapes=[pltpu.VMEM((2, width // 2, tokens), BF16)],
        ),
        compiler_params=pltpu.CompilerParams(vmem_limit_bytes=52 << 20),
        cost_estimate=pl.CostEstimate(
            flops=4 * tokens * width * hidden, bytes_accessed=8 * width * hidden, transcendentals=2 * tokens * hidden
        ),
        name="mlp_all",
    )(jnp.stack(position(me)).astype(jnp.int32), n2, dml, big, big, bias[None])


def grad_kernel(bits, a_ref, b_ref, keep_ref, send_ref):
    for part, out in zip(by_parity(turned(a_ref[...]), bits[2], keep_ref.shape[1]), (keep_ref, send_ref)):
        out[...] = mm(part, b_ref[...]).astype(BF16).reshape(out.shape)


def weight_grad(a, b, rows, me):
    out = jax.ShapeDtypeStruct((a.shape[1] // (2 * rows), rows, b.shape[1]), BF16)
    return pl.pallas_call(
        grad_kernel,
        out_shape=(out, out),
        grid_spec=pltpu.PrefetchScalarGridSpec(num_scalar_prefetch=1, grid=(1,)),
        compiler_params=pltpu.CompilerParams(vmem_limit_bytes=40 << 20),
        cost_estimate=pl.CostEstimate(
            flops=2 * a.size * b.shape[1], bytes_accessed=2 * (a.size + b.size + 2 * out.size), transcendentals=0
        ),
        name="weight_grad",
    )(jnp.stack(position(me)).astype(jnp.int32), a, b)


def after_mlp_kernel(
    bits, mlp, dn2, x_ref, branch, g_ref, o_ref, w_proj, vec, block_out, dy1_ref, sums, do_ref, keep, send
):
    layer_attn, gain2, layer_mlp, bias = (vec[i : i + 1, :] for i in range(4))
    g, out = g_ref[...].astype(F32), mlp[...] + bias
    y1 = x_ref[...].astype(F32) + layer_attn * branch[...]
    unit, rstd = normalised(y1)
    block_out[...] = (y1 + layer_mlp * out).astype(BF16)
    dy1 = g + norm_back(unit, rstd, dn2[...] * gain2)
    dy1_ref[...] = dy1
    db = layer_attn * dy1
    totals = (g * out, layer_mlp * g, dn2[...] * unit, dn2[...], dy1 * branch[...], db)
    for i, total in enumerate(totals):
        sums[i : i + 1, :] = jnp.sum(total, axis=0, keepdims=True)
    dbl = db.astype(BF16)
    do = lax.dot_general(dbl, w_proj[...], NT, preferred_element_type=F32).astype(BF16)
    columns = do_ref.shape[2]
    for j in range(do_ref.shape[0]):
        do_ref[j] = do[:, j * columns : (j + 1) * columns]
    for part, to in zip(by_parity(turned(o_ref[...]), bits[2], keep.shape[1]), (keep, send)):
        to[...] = mm(part, dbl).astype(BF16).reshape(to.shape)


def after_mlp(mlp, dn2, x, branch, g, o, big, vec, me, shard_rows):
    tokens, width = mlp.shape
    owners = width // shard_rows
    grads = shaped(owners // 2, shard_rows, width, dtype=BF16)
    outs = (
        shaped(tokens, width, dtype=BF16), shaped(tokens, width), shaped(8, width),
        shaped(GROUP, tokens, width // GROUP, dtype=BF16), grads, grads,
    )
    last = big.shape[1] // width - 1
    return pl.pallas_call(
        after_mlp_kernel,
        out_shape=outs,
        grid_spec=pltpu.PrefetchScalarGridSpec(
            num_scalar_prefetch=1,
            grid=(1,),
            in_specs=[whole_spec(a) for a in (mlp, dn2, x, branch, g, o)]
            + [pl.BlockSpec((width, width), lambda i, *_: (0, last)), whole_spec(vec)],
            out_specs=[whole_spec(a) for a in outs],
        ),
        compiler_params=pltpu.CompilerParams(vmem_limit_bytes=52 << 20),
        cost_estimate=pl.CostEstimate(flops=4 * tokens * width * width, bytes_accessed=20 << 20, transcendentals=0),
        name="after_mlp",
    )(jnp.stack(position(me)).astype(jnp.int32), mlp, dn2, x, branch, g, o, big, vec)


def add_kernel(bits, *refs, terms):
    outs = refs[terms * 2 * (len(refs) // (2 * terms + 1)) :]
    refs = refs[: terms * 2 * len(outs)]
    for n, out in enumerate(outs):
        wide, narrow = (
            [r[...].astype(F32).reshape(r.shape[-2:]) for r in refs[(2 * n + i) * terms : (2 * n + i + 1) * terms]]
            for i in range(2)
        )
        out[...] = jnp.concatenate([sum(wide), sum(narrow)], axis=1).astype(BF16).reshape(out.shape)


def added(operands, indices, grid, out_shape, out_index, me, name):
    flat, specs = [], []
    for sides, places in zip(operands, indices):
        for arrays, at in zip(sides, places):
            for (array, block), index in zip(arrays, at):
                flat.append(array)
                specs.append(pl.BlockSpec(block, index))
    terms = len(operands[0][0])
    outs = [shaped(*out_shape, dtype=BF16)] * len(operands)
    block = (1,) * (len(out_shape) - 2) + out_shape[-2:]
    return pl.pallas_call(
        functools.partial(add_kernel, terms=terms),
        out_shape=tuple(outs),
        grid_spec=pltpu.PrefetchScalarGridSpec(
            num_scalar_prefetch=1,
            grid=grid,
            in_specs=specs,
            out_specs=[pl.BlockSpec(block, out_index)] * len(outs),
        ),
        compiler_params=pltpu.CompilerParams(vmem_limit_bytes=40 << 20),
        cost_estimate=pl.CostEstimate(flops=0, bytes_accessed=16 << 20, transcendentals=0),
        name=name,
    )(jnp.stack(position(me)).astype(jnp.int32), *flat)


def first_sends(pairs, me):
    (one, two, small) = pairs
    planes, _, _, rows, width = one[0].shape
    cut = small[0].shape[-1] // 2
    wide, narrow = (1, 1, 1, rows, width), (1, 1, 1, rows, cut)

    def at_a(column):
        return lambda z, t, bits: (z, t, 1 - bits[1], 0, column)

    def at_b(column):
        return lambda z, t, bits: (z, 1 - bits[0], t, 0, column)

    operands = [
        ([(m, wide) for m in one], [(m, narrow) for m in small]),
        ([(m, wide) for m in two], [(m, narrow) for m in small]),
    ]
    indices = [([at_a(0)] * 2, [at_a(0)] * 2), ([at_b(0)] * 2, [at_b(1)] * 2)]
    shape = (planes, 2, rows, width + cut)
    return added(operands, indices, (planes, 2), shape, lambda z, t, bits: (z, t, 0, 0), me, "first_sends")


def second_sums(pairs, in_a, in_b, me):
    (one, two, small) = pairs
    planes, _, _, rows, width = one[0].shape
    cut = small[0].shape[-1] // 2
    wide, narrow = (1, 1, 1, rows, width), (1, 1, 1, rows, cut)
    wide_in, narrow_in = (1, 1, rows, width), (1, 1, rows, cut)
    operands, indices = [], []
    for sides, got, axis in ((one, in_a, 0), (two, in_b, 1)):
        for keep in (0, 1):
            def other(bits, axis=axis, keep=keep):
                return bits[axis] if keep else 1 - bits[axis]

            def at(column, axis=axis, other=other):
                if axis == 0:
                    return lambda z, bits: (z, other(bits), bits[1], 0, column)
                return lambda z, bits: (z, bits[0], other(bits), 0, column)

            def arrived(column, other=other):
                return lambda z, bits: (z, other(bits), 0, column)

            operands.append(
                ([(m, wide) for m in sides] + [(got, wide_in)], [(m, narrow) for m in small] + [(got, narrow_in)])
            )
            indices.append(
                ([at(0)] * 2 + [arrived(0)], [at(axis)] * 2 + [arrived(width // cut)])
            )
    shape = (planes, rows, width + cut)
    return added(operands, indices, (planes,), shape, lambda z, bits: (z, 0, 0), me, "second_sums")


def body(
    tokens,
    cotangent,
    image_lengths,
    ln1_gain,
    ln1_bias,
    qkv_weight,
    qv_bias,
    proj_weight,
    proj_bias,
    scale_attn,
    ln2_gain,
    ln2_bias,
    fc1_weight,
    fc1_bias,
    fc2_weight,
    fc2_bias,
    scale_mlp,
):
    devices = lax.axis_size("dev")
    me = lax.axis_index("dev")
    rows, width = tokens.shape
    vectors = (
        ln1_gain, ln1_bias, qv_bias, proj_bias, scale_attn, ln2_gain, ln2_bias, fc1_bias, fc2_bias, scale_mlp,
    )
    sizes = [v.shape[0] for v in vectors]
    shard_rows, hidden = qkv_weight.shape[0], fc1_weight.shape[1]
    by_axes = shard_rows % 32 == 0
    blocks = hidden // width
    slab = qkv_weight.reshape(shard_rows, 3, GROUP, -1).transpose(2, 0, 1, 3).reshape(GROUP, shard_rows, -1)
    packed = jnp.broadcast_to(pack_columns(vectors, shard_rows), (GROUP, shard_rows, 128))
    slab = jnp.concatenate([slab, packed], axis=2)
    slab = jnp.broadcast_to(slab[None], (devices // GROUP, *slab.shape)).reshape(devices, shard_rows, -1)
    slab = lax.all_to_all(slab, "dev", 0, 0, tiled=True).reshape(width, -1)
    packed = slab[:, -128:]
    spread = unpack_columns(packed.astype(F32), sizes, shard_rows)
    gain1, shift1, bias_qv, bias_proj, layer_attn, gain2, shift2, bias_fc1, bias_fc2, layer_mlp = spread
    if by_axes:
        first = fc1_weight.reshape(shard_rows, devices, blocks, shard_rows).transpose(0, 2, 1, 3)
        second = fc2_weight.reshape(blocks, shard_rows, width).transpose(1, 0, 2)
        big = jnp.concatenate(
            [first.reshape(shard_rows, hidden), second.reshape(shard_rows, hidden), proj_weight], axis=1
        )
        big = gathered(big)
        w_proj = big[:, 2 * hidden :]
    else:
        w_proj, big = gathered(proj_weight), gathered(fc1_weight)
        w_fc2 = gathered(fc2_weight)
    qkv_late = qkv_weight.reshape(shard_rows, 3, GROUP, -1).transpose(0, 2, 1, 3).reshape(shard_rows, -1)
    qkv_late, packed = lax.optimization_barrier((qkv_late, packed))
    w_qkv = gathered(qkv_late)

    span = GROUP * rows
    halo = -(-(SEQ - 1) // BK) * BK
    base = (me // GROUP) * span - halo
    places = base + halo + jnp.arange(span, dtype=jnp.int32)
    ends = jnp.cumsum(image_lengths)
    before = ends[None, :] <= places[:, None]
    begin = jnp.max(jnp.where(before, ends[None, :], 0), axis=1)
    finish = jnp.min(jnp.where(before, devices * rows, ends[None, :]), axis=1)
    seg = jnp.stack([begin - base, finish - base]).astype(jnp.int32)
    low = seg[0, ::BQ] // BK
    high = -(-seg[1, BQ - 1 :: BQ] // BK)

    x = tokens.astype(F32)
    u1, rstd1 = normalised(x)
    n1, q, kv = plane_qkv(tokens, slab, me, devices)
    prefetch, edge_blocks = (low, high), halo // BK
    left = shifted(kv[span - halo :], GROUP, devices)
    right = shifted(kv[:halo], -GROUP, devices)
    acc, stat = forward_mid(prefetch, seg, q, kv, edge_blocks)
    acc, stat, left, right = lax.optimization_barrier((acc, stat, left, right))
    o_heads, lse = forward_edge(prefetch, seg, q, left, right, acc, stat)
    (o,) = to_tokens([o_heads], devices)

    branch = mm(o, w_proj) + bias_proj
    y1 = x + layer_attn * branch
    u2, rstd2 = normalised(y1)
    n2 = (u2 * gain2 + shift2).astype(BF16)
    g = cotangent.astype(F32)
    dm = layer_mlp * g
    d_fc2_bias = jnp.sum(dm, axis=0)
    dml = dm.astype(BF16)
    if by_axes:
        bias_hidden = bias_fc1.reshape(devices, blocks, shard_rows).transpose(1, 0, 2).reshape(-1)
        mlp, dn2, d_fc1_bias, keep1, send1, keep2, send2 = mlp_all(n2, dml, big, bias_hidden, me, shard_rows)
        d_fc1_bias = d_fc1_bias.reshape(blocks, devices, shard_rows).transpose(1, 0, 2).reshape(-1)
    else:
        act, slope = gelu_parts(mm(n2, big) + bias_fc1)
        act = act.astype(BF16)
        mlp = mm(act, w_fc2)
        dz = mm_t(dml, w_fc2) * slope
        d_fc1_bias = jnp.sum(dz, axis=0)
        dz = dz.astype(BF16)
        dn2 = mm_t(dz, big)
        d_fc1, d_fc2 = scattered(t_mm(n2, dz)), scattered(t_mm(act, dml))
    if by_axes:
        vec = jnp.stack([layer_attn, gain2, layer_mlp, bias_fc2])
        block_out, dy1, totals, do, keep3, send3 = after_mlp(
            mlp, dn2, tokens, branch, cotangent, o, big, vec, me, shard_rows
        )
        d_scale_mlp, d_fc2_bias, d_gain2, d_shift2, d_scale_attn, d_proj_bias = (totals[i] for i in range(6))
        got1, got2, got3 = (swapped(s, 1, devices) for s in (send1, send2, send3))
        do, got1, got2, got3 = lax.optimization_barrier((do, got1, got2, got3))
        view = (devices // GROUP, 2, 2, shard_rows)
        halves = [
            tuple(s.reshape(*view, -1) for s in pair) for pair in ((keep1, got1), (keep2, got2), (keep3, got3))
        ]
        out_a, out_b = first_sends(halves, me)
    else:
        mlp = mlp + bias_fc2
        block_out = (y1 + layer_mlp * mlp).astype(BF16)
        d_scale_mlp = jnp.sum(g * mlp, axis=0)
        d_gain2 = jnp.sum(dn2 * u2, axis=0)
        d_shift2 = jnp.sum(dn2, axis=0)
        dy1 = g + norm_back(u2, rstd2, dn2 * gain2)
        d_scale_attn = jnp.sum(dy1 * branch, axis=0)
        db = layer_attn * dy1
        d_proj_bias = jnp.sum(db, axis=0)
        dbl = db.astype(BF16)
        d_proj = scattered(t_mm(o, dbl))
        do = mm_t(dbl, w_proj).astype(BF16).reshape(rows, GROUP, -1).transpose(1, 0, 2)

    do_heads = in_plane(do, devices).reshape(span, -1)
    if by_axes:
        do_heads, out_a, out_b = lax.optimization_barrier((do_heads, out_a, out_b))
        in_a, in_b = swapped(out_a, 2, devices), swapped(out_b, 4, devices)
    part_dq, mid0, edge = backward_first(prefetch, seg, q, kv, left, right, o_heads, do_heads, lse)
    if by_axes:
        part_dq, in_a, in_b, w_qkv = lax.optimization_barrier((part_dq, in_a, in_b, w_qkv))
        out_a, sum_a, out_b, sum_b = second_sums(halves, in_a, in_b, me)
        part_dq, out_a, out_b = lax.optimization_barrier((part_dq, out_a, out_b))
        in_a, in_b = swapped(out_a, 4, devices), swapped(out_b, 2, devices)
    from_right = shifted(edge[0], -GROUP, devices)
    from_left = shifted(edge[1], GROUP, devices)
    dq, mid1 = backward_second(prefetch, seg, q, kv, o_heads, do_heads, lse, part_dq, edge_blocks)
    dq, mid1, from_left, from_right = lax.optimization_barrier((dq, mid1, from_left, from_right))
    if by_axes:
        dq, in_a, in_b = lax.optimization_barrier((dq, in_a, in_b))
    rest = span - halo
    mid = mid0 + mid1 + jnp.pad(from_left.astype(F32), ((0, rest), (0, 0)))
    mid = mid + jnp.pad(from_right.astype(F32), ((rest, 0), (0, 0)))
    mid = mid.astype(BF16)
    d_heads = jnp.concatenate([dq, mid], axis=1)
    if by_axes:
        third = [(s.astype(F32) + i.astype(F32)).astype(BF16) for s, i in ((sum_a, in_a), (sum_b, in_b))]
        d_heads, third = lax.optimization_barrier((d_heads, jnp.concatenate(third, axis=-1)))
        own_sums, sums = from_planes(third, me, devices)
    dqkv = in_plane(d_heads.reshape(GROUP, rows, -1), devices)
    if by_axes:
        dqkv, n1, sums[:2] = lax.optimization_barrier((dqkv, n1, sums[:2]))
    d_qkv = t_mm(n1, d_heads).astype(BF16).reshape(devices // GROUP, GROUP, shard_rows, -1)
    dqkv, d_qkv = lax.optimization_barrier((dqkv, d_qkv))
    own_qkv, got_qkv = from_planes(d_qkv, me, devices)
    per_head = jnp.sum(dqkv.astype(F32), axis=1)
    half = width // GROUP
    d_qv_bias = jnp.concatenate([per_head[:, :half].reshape(-1), per_head[:, 2 * half :].reshape(-1)])
    dn1 = mm_t(dqkv.transpose(1, 0, 2).reshape(rows, 3 * width), w_qkv)
    if by_axes:
        dn1, sums[2:], got_qkv = lax.optimization_barrier((dn1, sums[2:], got_qkv))
    d_qkv = in_plane(total_of(own_qkv, got_qkv), devices).reshape(GROUP, shard_rows, 3, -1)
    d_qkv = d_qkv.transpose(1, 2, 0, 3).reshape(shard_rows, 3 * width)
    if by_axes:
        sums = total_of(own_sums, sums)
        d_fc1 = sums[:, :hidden].reshape(shard_rows, blocks, devices, shard_rows).transpose(0, 2, 1, 3)
        d_fc1 = d_fc1.reshape(shard_rows, hidden)
        cut = width // 2
        at = hidden + cut
        d_fc2 = sums[:, at : at + hidden].reshape(shard_rows, blocks, width).transpose(1, 0, 2)
        d_fc2 = d_fc2.reshape(blocks * shard_rows, width)
        d_proj = jnp.concatenate([sums[:, hidden:at], sums[:, at + hidden :]], axis=1)
    d_gain1 = jnp.sum(dn1 * u1, axis=0)
    d_shift1 = jnp.sum(dn1, axis=0)
    grad_tokens = (dy1 + norm_back(u1, rstd1, dn1 * gain1)).astype(BF16)

    small = (
        d_gain1, d_shift1, d_qv_bias, d_proj_bias, d_scale_attn, d_gain2, d_shift2, d_fc1_bias, d_fc2_bias, d_scale_mlp,
    )
    small = lax.all_to_all(pack(small, devices), "dev", 0, 0, tiled=True)
    small = jnp.sum(small, axis=0, keepdims=True)
    s_gain1, s_shift1, s_qv, s_proj, s_attn, s_gain2, s_shift2, s_fc1, s_fc2, s_mlp = unpack(small, sizes)
    return (
        block_out,
        grad_tokens,
        s_gain1,
        s_shift1,
        d_qkv,
        s_qv,
        d_proj,
        s_proj,
        s_attn,
        s_gain2,
        s_shift2,
        d_fc1,
        s_fc1,
        d_fc2,
        s_fc2,
        s_mlp,
    )


def solution(mesh):
    matrix, vector = P("dev", None), P("dev")
    return jax.shard_map(
        body,
        mesh=mesh,
        in_specs=(
            matrix, matrix, P(), vector, vector, matrix, vector, matrix, vector, vector, vector, vector, matrix,
            vector, matrix, vector, vector,
        ),
        out_specs=(
            matrix, matrix, vector, vector, matrix, vector, matrix, vector, vector, vector, vector, matrix, vector,
            matrix, vector, vector,
        ),
        check_vma=False,
    )
```

```python
import functools

import jax
import jax.numpy as jnp
from jax import lax
from jax.experimental import pallas as pl
from jax.experimental.pallas import tpu as pltpu
from jax.sharding import PartitionSpec as P

BQ = 256
BK = 256
SLAB = 2 * BK
HD = 64
LOG2E = 1.4426950408889634
SCALE = 0.125
MASKED = -1e30
NT = (((1,), (1,)), ((), ()))


def head_halves(block):
    first = lax.broadcasted_iota(jnp.int32, block.shape, 1) < HD
    zero = jnp.zeros_like(block)
    return jnp.where(first, block, zero), jnp.where(first, zero, block)


def transpose_into(target, source, column):
    width = target.shape[0]
    for j in range(source.shape[0] // BK):
        part = source[j * BK : (j + 1) * BK, column : column + width].astype(jnp.float32)
        target[:, j * BK : (j + 1) * BK] = part.T.astype(target.dtype)


def slabs(low, high, first, last):
    low = jnp.clip(low, first, last) - first
    count = (jnp.clip(high, first, last) - first - low + 1) // 2
    return jnp.minimum(low, last - first - 2 * count), count


def slab_rows(start, t):
    return pl.ds(pl.multiple_of((start + 2 * t) * BK, BK), SLAB)


def forward_over(span, kv_ref, v_t, offset, q_heads, seg, carry):
    start, count = span
    width = q_heads[0].shape[1]
    begin, end = seg[0:1, :], seg[1:2, :]
    place = lax.broadcasted_iota(jnp.int32, (SLAB, BQ), 0) + offset

    def one_slab(t, carry):
        rows = slab_rows(start, t)
        keys = kv_ref[rows, :width]
        at = place + (start + 2 * t) * BK
        valid = (at >= begin) & (at < end)
        out = []
        for h in range(2):
            top, total, acc = carry[h]
            s = lax.dot_general(keys, q_heads[h], NT, preferred_element_type=jnp.float32)
            s = jnp.where(valid, s * (SCALE * LOG2E), MASKED)
            new_top = jnp.maximum(top, jnp.max(s, axis=0, keepdims=True))
            p = jnp.exp2(s - new_top)
            fade = jnp.exp2(top - new_top)
            total = total * fade + jnp.sum(p, axis=0, keepdims=True)
            v_part = v_t[h * HD : (h + 1) * HD, rows]
            acc = acc * fade + jnp.dot(v_part, p.astype(jnp.bfloat16), preferred_element_type=jnp.float32)
            out.append((new_top, total, acc))
        return tuple(out)

    return lax.fori_loop(0, count, one_slab, carry)


def forward_mid_kernel(low, high, seg, q_ref, kv_ref, acc_ref, stat_ref, v_t, *, edge):
    step = pl.program_id(0)

    @pl.when(step == 0)
    def _():
        transpose_into(v_t, kv_ref, q_ref.shape[1])

    start = (
        jnp.full((1, BQ), MASKED, jnp.float32),
        jnp.zeros((1, BQ), jnp.float32),
        jnp.zeros((HD, BQ), jnp.float32),
    )
    blocks = kv_ref.shape[0] // BK
    span = slabs(low[step], high[step], edge, edge + blocks)
    done = forward_over(span, kv_ref, v_t, edge * BK, head_halves(q_ref[...]), seg, (start, start))
    for h, (top, total, acc) in enumerate(done):
        stat_ref[2 * h : 2 * h + 1, :] = top
        stat_ref[2 * h + 1 : 2 * h + 2, :] = total
        acc_ref[h * HD : (h + 1) * HD, :] = acc


def forward_edge_kernel(
    low, high, seg, q_ref, left_ref, right_ref, acc_ref, stat_ref, o_ref, lse_ref, left_t, right_t, *, last
):
    step = pl.program_id(0)
    width = q_ref.shape[1]
    edge = left_ref.shape[0] // BK

    @pl.when(step == 0)
    def _():
        transpose_into(left_t, left_ref, width)
        transpose_into(right_t, right_ref, width)

    carry = tuple(
        (stat_ref[2 * h : 2 * h + 1, :], stat_ref[2 * h + 1 : 2 * h + 2, :], acc_ref[h * HD : (h + 1) * HD, :])
        for h in range(2)
    )
    q_heads = head_halves(q_ref[...])
    span = slabs(low[step], high[step], 0, edge)
    carry = forward_over(span, left_ref, left_t, 0, q_heads, seg, carry)
    span = slabs(low[step], high[step], last, last + edge)
    carry = forward_over(span, right_ref, right_t, last * BK, q_heads, seg, carry)
    o_ref[...] = jnp.concatenate([acc / total for _, total, acc in carry], axis=0).T.astype(o_ref.dtype)
    for h, (top, total, _) in enumerate(carry):
        lse_ref[h : h + 1, :] = top + jnp.log2(total)


def backward_setup(q_ref, do_ref, o_ref, lse_ref, heads):
    prod = (do_ref[...].astype(jnp.float32) * o_ref[...].astype(jnp.float32)).T
    q_heads, do_heads = head_halves(q_ref[...]), head_halves(do_ref[...])
    return [
        (
            h,
            q_heads[h],
            do_heads[h],
            jnp.sum(prod[h * HD : (h + 1) * HD], axis=0, keepdims=True),
            lse_ref[h : h + 1, :],
        )
        for h in heads
    ]


def backward_over(span, kv_ref, k_t, dkv, dq_t, offset, heads, seg):
    start, count = span
    width = dq_t.shape[0]
    begin, end = seg[0:1, :], seg[1:2, :]
    place = lax.broadcasted_iota(jnp.int32, (SLAB, BQ), 0) + offset
    q_all = jnp.concatenate([q for _, q, _, _, _ in heads], axis=0)
    do_all = jnp.concatenate([d for _, _, d, _, _ in heads], axis=0)

    @pl.loop(0, count)
    def _(t):
        rows = slab_rows(start, t)
        keys, values = kv_ref[rows, :width], kv_ref[rows, width:]
        at = place + (start + 2 * t) * BK
        valid = (at >= begin) & (at < end)
        ps, dss = [], []
        for h, q, do, centre, lse in heads:
            s = lax.dot_general(keys, q, NT, preferred_element_type=jnp.float32)
            p = jnp.where(valid, jnp.exp2(s * (SCALE * LOG2E) - lse), 0.0)
            dp = lax.dot_general(values, do, NT, preferred_element_type=jnp.float32)
            ds = (p * (dp - centre)).astype(jnp.bfloat16)
            ps.append(p.astype(jnp.bfloat16))
            dss.append(ds)
            part = slice(h * HD, (h + 1) * HD)
            dq_t[part, :] += jnp.dot(k_t[part, rows], ds, preferred_element_type=jnp.float32)
        dkv[rows, :width] += jnp.dot(jnp.concatenate(dss, axis=1), q_all, preferred_element_type=jnp.float32)
        dkv[rows, width:] += jnp.dot(jnp.concatenate(ps, axis=1), do_all, preferred_element_type=jnp.float32)


def backward_first_kernel(
    low, high, seg, q_ref, kv_ref, left_ref, right_ref, o_ref, do_ref, lse_ref, dq_t, mid_ref, out_left, out_right,
    left_t, right_t, k_t, dkv, *, last
):
    step = pl.program_id(0)
    width = q_ref.shape[1]
    edge = left_ref.shape[0] // BK

    @pl.when(step == 0)
    def _():
        transpose_into(left_t, left_ref, 0)
        transpose_into(right_t, right_ref, 0)
        transpose_into(k_t, kv_ref, 0)
        dkv[...] = jnp.zeros_like(dkv)
        mid_ref[...] = jnp.zeros_like(mid_ref)

    heads = backward_setup(q_ref, do_ref, o_ref, lse_ref, range(2))
    dq_t[...] = jnp.zeros_like(dq_t)
    span = slabs(low[step], high[step], 0, edge)
    backward_over(span, left_ref, left_t, dkv.at[0], dq_t, 0, heads, seg)
    span = slabs(low[step], high[step], last, last + edge)
    backward_over(span, right_ref, right_t, dkv.at[1], dq_t, last * BK, heads, seg)
    span = slabs(low[step], high[step], edge, last)
    backward_over(span, kv_ref, k_t, mid_ref, dq_t, edge * BK, heads[:1], seg)

    @pl.when(step == pl.num_programs(0) - 1)
    def _():
        mid_ref[:, :width] = mid_ref[:, :width] * SCALE
        for side, out in enumerate((out_left, out_right)):
            out[:, :width] = (dkv[side, :, :width] * SCALE).astype(out.dtype)
            out[:, width:] = dkv[side, :, width:].astype(out.dtype)


def backward_mid_kernel(
    low, high, seg, q_ref, kv_ref, o_ref, do_ref, lse_ref, part_ref, dq_ref, mid_ref, k_t, dq_t, *, edge
):
    step = pl.program_id(0)
    width = q_ref.shape[1]

    @pl.when(step == 0)
    def _():
        transpose_into(k_t, kv_ref, 0)
        mid_ref[...] = jnp.zeros_like(mid_ref)

    dq_t[...] = part_ref[...]
    blocks = kv_ref.shape[0] // BK
    span = slabs(low[step], high[step], edge, edge + blocks)
    heads = backward_setup(q_ref, do_ref, o_ref, lse_ref, [1])
    backward_over(span, kv_ref, k_t, mid_ref, dq_t, edge * BK, heads, seg)
    dq_ref[...] = (dq_t[...] * SCALE).T.astype(dq_ref.dtype)

    @pl.when(step == pl.num_programs(0) - 1)
    def _():
        mid_ref[:, :width] = mid_ref[:, :width] * SCALE


def whole_spec(array):
    return pl.BlockSpec(array.shape, lambda i, *_: (0,) * len(array.shape))


def attention_call(kernel, name, prefetch, inputs, in_kinds, outputs, out_kinds, scratch, work):
    span = prefetch[0].shape[0] * BQ

    def spec(array, kind):
        if kind == "r":
            return pl.BlockSpec((BQ, array.shape[1]), lambda i, *_: (i, 0))
        if kind == "c":
            return pl.BlockSpec((array.shape[0], BQ), lambda i, *_: (0, i))
        return whole_spec(array)

    return pl.pallas_call(
        kernel,
        out_shape=tuple(outputs),
        grid_spec=pltpu.PrefetchScalarGridSpec(
            num_scalar_prefetch=2,
            grid=(span // BQ,),
            in_specs=[spec(a, k) for a, k in zip(inputs, in_kinds)],
            out_specs=[spec(a, k) for a, k in zip(outputs, out_kinds)],
            scratch_shapes=scratch,
        ),
        compiler_params=pltpu.CompilerParams(vmem_limit_bytes=48 << 20),
        cost_estimate=pl.CostEstimate(flops=work << 30, bytes_accessed=8 << 20, transcendentals=span * 128),
        name=name,
    )(*prefetch, *inputs)


def shaped(*shape, dtype=jnp.float32):
    return jax.ShapeDtypeStruct(shape, dtype)


def forward_mid(prefetch, seg, q, kv, edge):
    span, width = q.shape
    return attention_call(
        functools.partial(forward_mid_kernel, edge=edge), "forward_mid", prefetch, [seg, q, kv], "crw",
        [shaped(width, span), shaped(8, span)], "cc", [pltpu.VMEM((width, span), jnp.bfloat16)], 3,
    )


def forward_edge(prefetch, seg, q, left, right, acc, stat):
    span, width = q.shape
    halo = pltpu.VMEM((width, left.shape[0]), jnp.bfloat16)
    return attention_call(
        functools.partial(forward_edge_kernel, last=(left.shape[0] + span) // BK), "forward_edge", prefetch,
        [seg, q, left, right, acc, stat], "crwwcc",
        [shaped(span, width, dtype=jnp.bfloat16), shaped(8, span)], "rc", [halo, halo], 3,
    )


def backward_first(prefetch, seg, q, kv, left, right, o, do, lse):
    span, width = q.shape
    halo = pltpu.VMEM((width, left.shape[0]), jnp.bfloat16)
    return attention_call(
        functools.partial(backward_first_kernel, last=(left.shape[0] + span) // BK), "backward_first", prefetch,
        [seg, q, kv, left, right, o, do, lse], "crwwwrrc",
        [shaped(width, span), shaped(*kv.shape)] + [shaped(*left.shape, dtype=jnp.bfloat16)] * 2, "cwww",
        [halo, halo, pltpu.VMEM((width, span), jnp.bfloat16), pltpu.VMEM((2, *left.shape), jnp.float32)], 3,
    )


def backward_second(prefetch, seg, q, kv, o, do, lse, part, edge):
    span, width = q.shape
    return attention_call(
        functools.partial(backward_mid_kernel, edge=edge), "backward_second", prefetch,
        [seg, q, kv, o, do, lse, part], "crwrrcc",
        [shaped(span, width, dtype=jnp.bfloat16), shaped(*kv.shape)], "rw",
        [pltpu.VMEM((width, span), jnp.bfloat16), pltpu.VMEM((width, BQ), jnp.float32)], 3,
    )


HEADS = 16
SEQ = 1370
GROUP = 8
EPS = 1e-06
F32, BF16 = jnp.float32, jnp.bfloat16


def mm(left, right):
    return jnp.dot(left, right, preferred_element_type=F32)


def mm_t(left, right):
    return jnp.einsum("tf,df->td", left, right, preferred_element_type=F32)


def t_mm(left, right):
    return jnp.einsum("td,tf->df", left, right, preferred_element_type=F32)


def normalised(value):
    centre = value - jnp.mean(value, axis=-1, keepdims=True)
    rstd = lax.rsqrt(jnp.mean(centre * centre, axis=-1, keepdims=True) + EPS)
    return centre * rstd, rstd


def norm_back(unit, rstd, grad):
    first = jnp.mean(grad, axis=-1, keepdims=True)
    second = jnp.mean(grad * unit, axis=-1, keepdims=True)
    return rstd * (grad - first - unit * second)


def gelu_parts(z):
    half = 0.5 * (1.0 + lax.erf(z * 0.7071067811865476))
    slope = half + z * (0.3989422804014327 * jnp.exp(-0.5 * z * z))
    return z * half, slope


def groups_of(count):
    return [list(range(first, first + GROUP)) for first in range(0, count, GROUP)]


def gathered(shard):
    return lax.all_gather(shard, "dev", axis=0, tiled=True)


def scattered(whole):
    return lax.psum_scatter(whole, "dev", scatter_dimension=0, tiled=True)


def pack(vectors, count):
    return jnp.concatenate([v.reshape(count, -1) for v in vectors], axis=1)


def unpack(packed, sizes):
    out, at = [], 0
    for size in sizes:
        out.append(packed[:, at : at + size].reshape(-1))
        at += size
    return out


def to_heads(parts, devices):
    rows = parts[0].shape[0]
    sent = jnp.stack([p.reshape(rows, GROUP, -1) for p in parts], axis=2)
    sent = sent.transpose(1, 0, 2, 3)
    back = lax.all_to_all(sent, "dev", 0, 0, axis_index_groups=groups_of(devices), tiled=True)
    return [back[:, :, i].reshape(GROUP * rows, -1) for i in range(len(parts))]


def to_tokens(parts, devices):
    rows = parts[0].shape[0] // GROUP
    sent = jnp.stack([p.reshape(GROUP, rows, -1) for p in parts], axis=2)
    back = lax.all_to_all(sent, "dev", 0, 0, axis_index_groups=groups_of(devices), tiled=True)
    return [back[:, :, i].transpose(1, 0, 2).reshape(rows, -1) for i in range(len(parts))]


def shifted(shard, by, devices):
    pairs = [(i, i + by) for i in range(devices) if 0 <= i + by < devices]
    return lax.ppermute(shard, "dev", pairs)


def take(stack, index, axis):
    return lax.dynamic_index_in_dim(stack, index, axis, keepdims=False)


def swapped(value, bit, devices):
    return lax.ppermute(value, "dev", [(i, i ^ bit) for i in range(devices)])


def join_kernel(dq, mid0, mid1, left, right, out):
    width = dq.shape[1]
    step, edge = pl.program_id(0), pl.num_programs(0) // 2
    halo = jnp.where(step < edge, left[...], right[...]).astype(F32)
    out[:, :width] = dq[...]
    out[:, width:] = (mid0[...] + mid1[...] + halo).astype(out.dtype)


def joined_heads(dq, mid0, mid1, left, right):
    span, width = dq.shape
    size = BQ
    half = span // (2 * size)
    rows = [pl.BlockSpec((size, columns), lambda i: (i, 0)) for columns in (width, 2 * width, 2 * width, 3 * width)]
    return pl.pallas_call(
        join_kernel,
        out_shape=shaped(span, 3 * width, dtype=BF16),
        grid=(span // size,),
        in_specs=rows[:3]
        + [
            pl.BlockSpec((size, 2 * width), lambda i: (jnp.minimum(i, half - 1), 0)),
            pl.BlockSpec((size, 2 * width), lambda i: (jnp.maximum(i - half, 0), 0)),
        ],
        out_specs=rows[3],
        cost_estimate=pl.CostEstimate(flops=0, bytes_accessed=10 << 20, transcendentals=0),
        name="joined_heads",
    )(dq, mid0, mid1, left, right)


def tail_kernel(dqkv, weight, dy1, x_ref, gain, grad, sums, heads):
    size = dqkv.shape[2]
    dn1 = jnp.zeros(dy1.shape, F32)
    for j in range(dqkv.shape[0]):
        dn1 += lax.dot_general(
            dqkv[j], weight[:, j * size : (j + 1) * size], NT, preferred_element_type=F32
        )
        heads[j : j + 1, :] = jnp.sum(dqkv[j].astype(F32), axis=0, keepdims=True)
    unit, rstd = normalised(x_ref[...].astype(F32))
    grad[...] = (dy1[...] + norm_back(unit, rstd, dn1 * gain[...])).astype(grad.dtype)
    sums[0:1, :] = jnp.sum(dn1 * unit, axis=0, keepdims=True)
    sums[1:2, :] = jnp.sum(dn1, axis=0, keepdims=True)


def input_gradient(dqkv, weight, dy1, tokens, gain):
    inputs = (dqkv, weight, dy1, tokens, gain[None])
    outs = (shaped(*tokens.shape, dtype=BF16), shaped(8, tokens.shape[1]), shaped(GROUP, dqkv.shape[2]))
    return pl.pallas_call(
        tail_kernel,
        out_shape=outs,
        grid=(1,),
        in_specs=[whole_spec(a) for a in inputs],
        out_specs=[whole_spec(a) for a in outs],
        compiler_params=pltpu.CompilerParams(vmem_limit_bytes=44 << 20),
        cost_estimate=pl.CostEstimate(flops=2 * weight.size * tokens.shape[0], bytes_accessed=12 << 20, transcendentals=0),
        name="input_gradient",
    )(*inputs)


def in_plane(stack, devices):
    return lax.all_to_all(stack, "dev", 0, 0, axis_index_groups=groups_of(devices), tiled=True)


def position(me):
    return (me // 4) % 2, (me // 2) % 2, me % 2


def qkv_kernel(bits, near_a, far_a, near_b, far_b, slab, n1_ref, q_ref, kv_ref, lines, bias, *, rows):
    step = pl.program_id(0)
    third = q_ref.shape[1]
    width = slab.shape[0]

    @pl.when(step == 0)
    def _():
        lines[...] = slab[:, 3 * third :].astype(F32).T
        group = bits[3]
        unit = lax.broadcasted_iota(jnp.int32, (width, third), 0)
        place = lax.broadcasted_iota(jnp.int32, (width, third), 1)
        some = lines[0:16, :].astype(BF16)
        bias[...] = jnp.zeros_like(bias)
        for part, first in ((0, 0), (2, width // 2)):
            total = jnp.zeros((1, third), F32)
            for column in range(2):
                at = first + group * (third // 2) + (place // (2 * rows)) * rows + place % rows
                chosen = (unit == at) & ((place // rows) % 2 == column)
                total = total + mm(some, jnp.where(chosen, 1.0, 0.0).astype(BF16))[2 + column : 3 + column]
            bias[0:1, part * third : (part + 1) * third] = total

    far = step >= 4
    left = jnp.where(far, far_a[0, 0], near_a[0, 0])
    right = jnp.where(far, far_b[0, 0], near_b[0, 0])
    unit, _ = normalised(jnp.concatenate([left, right], axis=1).astype(F32))
    n1 = (unit * lines[0:1, :] + lines[1:2, :]).astype(BF16)
    n1_ref[...] = n1
    out = (mm(n1, slab[:, : 3 * third]) + bias[0:1, :]).astype(BF16)
    q_ref[...] = out[:, :third]
    kv_ref[...] = out[:, third:]


def plane_qkv(tokens, slab, me, devices):
    rows, width = tokens.shape
    half, third = width // 2, (slab.shape[1] - 128) // 3
    a, b = tokens[:, :half], tokens[:, half:]
    a = jnp.stack([a, swapped(a, 4, devices)])
    b = jnp.stack([b, swapped(b, 2, devices)])
    a = jnp.stack([a, swapped(a, 2, devices)])
    b = jnp.stack([b, swapped(b, 4, devices)])
    a, b, slab = lax.optimization_barrier((a, b, slab))
    far_a, far_b = swapped(a, 1, devices), swapped(b, 1, devices)

    def near_at(s, swap):
        i, j = (s // 2) % 2, s % 2
        i, j = jnp.where(s < 4, i, 1), jnp.where(s < 4, j, 1)
        return (j, i, 0, 0) if swap else (i, j, 0, 0)

    def far_at(s, swap):
        i, j = (s // 2) % 2, s % 2
        i, j = jnp.where(s < 4, 0, i), jnp.where(s < 4, 0, j)
        return (j, i, 0, 0) if swap else (i, j, 0, 0)

    def place(s, bits):
        return ((bits[0] ^ (s % 2)) * 4 + (bits[1] ^ ((s // 2) % 2)) * 2 + (bits[2] ^ (s // 4)), 0)

    piece = (1, 1, rows, half)
    span = GROUP * rows
    return pl.pallas_call(
        functools.partial(qkv_kernel, rows=width // devices),
        out_shape=(
            jax.ShapeDtypeStruct((span, width), BF16),
            jax.ShapeDtypeStruct((span, third), BF16),
            jax.ShapeDtypeStruct((span, 2 * third), BF16),
        ),
        grid_spec=pltpu.PrefetchScalarGridSpec(
            num_scalar_prefetch=1,
            grid=(GROUP,),
            in_specs=[
                pl.BlockSpec(piece, lambda s, bits: near_at(s, False)),
                pl.BlockSpec(piece, lambda s, bits: far_at(s, False)),
                pl.BlockSpec(piece, lambda s, bits: near_at(s, True)),
                pl.BlockSpec(piece, lambda s, bits: far_at(s, True)),
                pl.BlockSpec(slab.shape, lambda s, bits: (0, 0)),
            ],
            out_specs=[pl.BlockSpec((rows, columns), place) for columns in (width, third, 2 * third)],
            scratch_shapes=[pltpu.VMEM((128, width), F32), pltpu.VMEM((8, 3 * third), F32)],
        ),
        compiler_params=pltpu.CompilerParams(vmem_limit_bytes=40 << 20),
        cost_estimate=pl.CostEstimate(flops=5 << 30, bytes_accessed=16 << 20, transcendentals=0),
        name="plane_qkv",
    )(
        jnp.stack([*position(me), me % GROUP]).astype(jnp.int32), a, far_a, b, far_b, slab,
    )


def from_planes(stack, me, devices):
    planes, mine = devices // GROUP, me // GROUP
    got = []
    for k in range(1, planes):
        piece = take(stack, (mine + k) % planes, 0)
        got.append(lax.ppermute(piece, "dev", [(i, (i + k * GROUP) % devices) for i in range(devices)]))
    return take(stack, mine, 0), got


def total_of(own, others):
    total = own.astype(F32)
    for other in others:
        total = total + other.astype(F32)
    return total


def pack_columns(vectors, rows):
    columns = jnp.concatenate([v.reshape(-1, rows).T for v in vectors], axis=1)
    return jnp.pad(columns, ((0, 0), (0, 128 - columns.shape[1])))


def unpack_columns(packed, sizes, rows):
    lines, out, at = packed[:, :16].T, [], 0
    for size in sizes:
        count = size // rows
        part = lines[at : at + count].reshape(count, -1, rows)
        out.append(part.transpose(1, 0, 2).reshape(-1))
        at += count
    return out


def by_parity(transposed, parity, rows):
    blocks = transposed.reshape(-1, 2, rows, transposed.shape[1])
    even, odd = (blocks[:, s].reshape(-1, transposed.shape[1]) for s in range(2))
    return jnp.where(parity == 0, even, odd), jnp.where(parity == 0, odd, even)


def turned(value):
    return value.astype(F32).T.astype(BF16)


def mlp_kernel(
    bits, n2_ref, dml_ref, f1_ref, f2_ref, bias, mlp_ref, dn2_ref, db_ref, keep1, send1, keep2, send2, n2_t
):
    step = pl.program_id(0)
    rows = keep1.shape[1]

    @pl.when(step == 0)
    def _():
        mlp_ref[...] = jnp.zeros_like(mlp_ref)
        dn2_ref[...] = jnp.zeros_like(dn2_ref)
        n2_t[0], n2_t[1] = by_parity(turned(n2_ref[...]), bits[2], rows)

    n2, dml, f1, f2 = n2_ref[...], dml_ref[...], f1_ref[...], f2_ref[...]
    act, slope = gelu_parts(mm(n2, f1) + bias[...])
    act = act.astype(BF16)
    mlp_ref[...] += mm(act, f2)
    dz = lax.dot_general(dml, f2, NT, preferred_element_type=F32) * slope
    db_ref[...] = jnp.sum(dz, axis=0, keepdims=True)
    dz = dz.astype(BF16)
    dn2_ref[...] += lax.dot_general(dz, f1, NT, preferred_element_type=F32)
    for side, out in enumerate((keep1, send1)):
        out[...] = mm(n2_t[side], dz).astype(BF16).reshape(out.shape)
    width = n2.shape[1]
    parts = keep2.shape[2] // width
    for part, out in zip(by_parity(turned(act), bits[2], parts * rows), (keep2, send2)):
        grad = mm(part, dml).astype(BF16).reshape(out.shape[0], parts, rows, width)
        for i in range(parts):
            out[:, :, i * width : (i + 1) * width] = grad[:, i]


def mlp_all(n2, dml, big, fc2, bias, me, shard_rows):
    tokens, width = n2.shape
    hidden, owners = bias.shape[0], width // shard_rows
    size = width // 2
    steps = hidden // size
    whole = pl.BlockSpec((tokens, width), lambda s, bits: (0, 0))
    first = pl.BlockSpec((owners // 2, shard_rows, size), lambda s, bits: (0, 0, s))
    second = pl.BlockSpec((owners // (2 * steps), shard_rows, hidden), lambda s, bits: (s, 0, 0))
    line = pl.BlockSpec((1, size), lambda s, bits: (0, s))
    grads = jax.ShapeDtypeStruct((owners // 2, shard_rows, hidden), BF16)
    total = jax.ShapeDtypeStruct((tokens, width), F32)
    return pl.pallas_call(
        mlp_kernel,
        out_shape=(total, total, jax.ShapeDtypeStruct((1, hidden), F32), grads, grads, grads, grads),
        grid_spec=pltpu.PrefetchScalarGridSpec(
            num_scalar_prefetch=1,
            grid=(steps,),
            in_specs=[
                whole,
                whole,
                pl.BlockSpec((width, size), lambda s, bits: (0, s)),
                pl.BlockSpec((size, width), lambda s, bits: (s, 0)),
                line,
            ],
            out_specs=[whole, whole, line, first, first, second, second],
            scratch_shapes=[pltpu.VMEM((2, width // 2, tokens), BF16)],
        ),
        compiler_params=pltpu.CompilerParams(vmem_limit_bytes=52 << 20),
        cost_estimate=pl.CostEstimate(
            flops=4 * tokens * width * hidden, bytes_accessed=8 * width * hidden, transcendentals=2 * tokens * hidden
        ),
        name="mlp_all",
    )(jnp.stack(position(me)).astype(jnp.int32), n2, dml, big, fc2, bias[None])


def grad_kernel(bits, a_ref, b_ref, keep_ref, send_ref):
    for part, out in zip(by_parity(turned(a_ref[...]), bits[2], keep_ref.shape[1]), (keep_ref, send_ref)):
        out[...] = mm(part, b_ref[...]).astype(BF16).reshape(out.shape)


def weight_grad(a, b, rows, me):
    out = jax.ShapeDtypeStruct((a.shape[1] // (2 * rows), rows, b.shape[1]), BF16)
    return pl.pallas_call(
        grad_kernel,
        out_shape=(out, out),
        grid_spec=pltpu.PrefetchScalarGridSpec(num_scalar_prefetch=1, grid=(1,)),
        compiler_params=pltpu.CompilerParams(vmem_limit_bytes=40 << 20),
        cost_estimate=pl.CostEstimate(
            flops=2 * a.size * b.shape[1], bytes_accessed=2 * (a.size + b.size + 2 * out.size), transcendentals=0
        ),
        name="weight_grad",
    )(jnp.stack(position(me)).astype(jnp.int32), a, b)


def after_mlp_kernel(
    bits, mlp, dn2, x_ref, branch, g_ref, o_ref, w_proj, vec, block_out, dy1_ref, sums, do_ref, keep, send
):
    layer_attn, gain2, layer_mlp, bias = (vec[i : i + 1, :] for i in range(4))
    g, out = g_ref[...].astype(F32), mlp[...] + bias
    y1 = x_ref[...].astype(F32) + layer_attn * branch[...]
    unit, rstd = normalised(y1)
    block_out[...] = (y1 + layer_mlp * out).astype(BF16)
    dy1 = g + norm_back(unit, rstd, dn2[...] * gain2)
    dy1_ref[...] = dy1
    db = layer_attn * dy1
    totals = (g * out, layer_mlp * g, dn2[...] * unit, dn2[...], dy1 * branch[...], db)
    for i, total in enumerate(totals):
        sums[i : i + 1, :] = jnp.sum(total, axis=0, keepdims=True)
    dbl = db.astype(BF16)
    do = lax.dot_general(dbl, w_proj[...], NT, preferred_element_type=F32).astype(BF16)
    columns = do_ref.shape[2]
    for j in range(do_ref.shape[0]):
        do_ref[j] = do[:, j * columns : (j + 1) * columns]
    for part, to in zip(by_parity(turned(o_ref[...]), bits[2], keep.shape[1]), (keep, send)):
        to[...] = mm(part, dbl).astype(BF16).reshape(to.shape)


def after_mlp(mlp, dn2, x, branch, g, o, big, vec, me, shard_rows):
    tokens, width = mlp.shape
    owners = width // shard_rows
    grads = shaped(owners // 2, shard_rows, width, dtype=BF16)
    outs = (
        shaped(tokens, width, dtype=BF16), shaped(tokens, width), shaped(8, width),
        shaped(GROUP, tokens, width // GROUP, dtype=BF16), grads, grads,
    )
    last = big.shape[1] // width - 1
    return pl.pallas_call(
        after_mlp_kernel,
        out_shape=outs,
        grid_spec=pltpu.PrefetchScalarGridSpec(
            num_scalar_prefetch=1,
            grid=(1,),
            in_specs=[whole_spec(a) for a in (mlp, dn2, x, branch, g, o)]
            + [pl.BlockSpec((width, width), lambda i, *_: (0, last)), whole_spec(vec)],
            out_specs=[whole_spec(a) for a in outs],
        ),
        compiler_params=pltpu.CompilerParams(vmem_limit_bytes=52 << 20),
        cost_estimate=pl.CostEstimate(flops=4 * tokens * width * width, bytes_accessed=20 << 20, transcendentals=0),
        name="after_mlp",
    )(jnp.stack(position(me)).astype(jnp.int32), mlp, dn2, x, branch, g, o, big, vec)


def add_kernel(bits, *refs, terms):
    outs = refs[terms * 2 * (len(refs) // (2 * terms + 1)) :]
    refs = refs[: terms * 2 * len(outs)]
    for n, out in enumerate(outs):
        wide, narrow = (
            [r[...].astype(F32).reshape(r.shape[-2:]) for r in refs[(2 * n + i) * terms : (2 * n + i + 1) * terms]]
            for i in range(2)
        )
        out[...] = jnp.concatenate([sum(wide), sum(narrow)], axis=1).astype(BF16).reshape(out.shape)


def added(operands, indices, grid, out_shape, out_index, me, name):
    flat, specs = [], []
    for sides, places in zip(operands, indices):
        for arrays, at in zip(sides, places):
            for (array, block), index in zip(arrays, at):
                flat.append(array)
                specs.append(pl.BlockSpec(block, index))
    terms = len(operands[0][0])
    outs = [shaped(*out_shape, dtype=BF16)] * len(operands)
    block = (1,) * (len(out_shape) - 2) + out_shape[-2:]
    return pl.pallas_call(
        functools.partial(add_kernel, terms=terms),
        out_shape=tuple(outs),
        grid_spec=pltpu.PrefetchScalarGridSpec(
            num_scalar_prefetch=1,
            grid=grid,
            in_specs=specs,
            out_specs=[pl.BlockSpec(block, out_index)] * len(outs),
        ),
        compiler_params=pltpu.CompilerParams(vmem_limit_bytes=40 << 20),
        cost_estimate=pl.CostEstimate(flops=0, bytes_accessed=16 << 20, transcendentals=0),
        name=name,
    )(jnp.stack(position(me)).astype(jnp.int32), *flat)


def first_sends(pairs, me):
    (one, two, small) = pairs
    planes, _, _, rows, width = one[0].shape
    cut = small[0].shape[-1] // 2
    wide, narrow = (1, 1, 1, rows, width), (1, 1, 1, rows, cut)

    def at_a(column):
        return lambda z, t, bits: (z, t, 1 - bits[1], 0, column)

    def at_b(column):
        return lambda z, t, bits: (z, 1 - bits[0], t, 0, column)

    operands = [
        ([(m, wide) for m in one], [(m, narrow) for m in small]),
        ([(m, wide) for m in two], [(m, narrow) for m in small]),
    ]
    indices = [([at_a(0)] * 2, [at_a(0)] * 2), ([at_b(0)] * 2, [at_b(1)] * 2)]
    shape = (planes, 2, rows, width + cut)
    return added(operands, indices, (planes, 2), shape, lambda z, t, bits: (z, t, 0, 0), me, "first_sends")


def second_sums(pairs, in_a, in_b, me):
    (one, two, small) = pairs
    planes, _, _, rows, width = one[0].shape
    cut = small[0].shape[-1] // 2
    wide, narrow = (1, 1, 1, rows, width), (1, 1, 1, rows, cut)
    wide_in, narrow_in = (1, 1, rows, width), (1, 1, rows, cut)
    operands, indices = [], []
    for sides, got, axis in ((one, in_a, 0), (two, in_b, 1)):
        for keep in (0, 1):
            def other(bits, axis=axis, keep=keep):
                return bits[axis] if keep else 1 - bits[axis]

            def at(column, axis=axis, other=other):
                if axis == 0:
                    return lambda z, bits: (z, other(bits), bits[1], 0, column)
                return lambda z, bits: (z, bits[0], other(bits), 0, column)

            def arrived(column, other=other):
                return lambda z, bits: (z, other(bits), 0, column)

            operands.append(
                ([(m, wide) for m in sides] + [(got, wide_in)], [(m, narrow) for m in small] + [(got, narrow_in)])
            )
            indices.append(
                ([at(0)] * 2 + [arrived(0)], [at(axis)] * 2 + [arrived(width // cut)])
            )
    shape = (planes, rows, width + cut)
    return added(operands, indices, (planes,), shape, lambda z, bits: (z, 0, 0), me, "second_sums")


def body(
    tokens,
    cotangent,
    image_lengths,
    ln1_gain,
    ln1_bias,
    qkv_weight,
    qv_bias,
    proj_weight,
    proj_bias,
    scale_attn,
    ln2_gain,
    ln2_bias,
    fc1_weight,
    fc1_bias,
    fc2_weight,
    fc2_bias,
    scale_mlp,
):
    devices = lax.axis_size("dev")
    me = lax.axis_index("dev")
    rows, width = tokens.shape
    vectors = (
        ln1_gain, ln1_bias, qv_bias, proj_bias, scale_attn, ln2_gain, ln2_bias, fc1_bias, fc2_bias, scale_mlp,
    )
    sizes = [v.shape[0] for v in vectors]
    shard_rows, hidden = qkv_weight.shape[0], fc1_weight.shape[1]
    by_axes = shard_rows % 32 == 0
    blocks = hidden // width
    slab = qkv_weight.reshape(shard_rows, 3, GROUP, -1).transpose(2, 0, 1, 3).reshape(GROUP, shard_rows, -1)
    packed = jnp.broadcast_to(pack_columns(vectors, shard_rows), (GROUP, shard_rows, 128))
    slab = jnp.concatenate([slab, packed], axis=2)
    slab = jnp.broadcast_to(slab[None], (devices // GROUP, *slab.shape)).reshape(devices, shard_rows, -1)
    slab = lax.all_to_all(slab, "dev", 0, 0, tiled=True).reshape(width, -1)
    packed = slab[:, -128:]
    spread = unpack_columns(packed.astype(F32), sizes, shard_rows)
    gain1, shift1, bias_qv, bias_proj, layer_attn, gain2, shift2, bias_fc1, bias_fc2, layer_mlp = spread
    if by_axes:
        big = gathered(jnp.concatenate([fc1_weight, proj_weight], axis=1))
        w_fc2 = gathered(fc2_weight)
        w_proj = big[:, hidden:]
    else:
        w_proj, big = gathered(proj_weight), gathered(fc1_weight)
        w_fc2 = gathered(fc2_weight)
    qkv_late = qkv_weight.reshape(shard_rows, 3, GROUP, -1).transpose(0, 2, 1, 3).reshape(shard_rows, -1)
    qkv_late, packed = lax.optimization_barrier((qkv_late, packed))
    w_qkv = gathered(qkv_late)

    span = GROUP * rows
    halo = -(-(SEQ - 1) // BK) * BK
    base = (me // GROUP) * span - halo
    places = base + halo + jnp.arange(span, dtype=jnp.int32)
    ends = jnp.cumsum(image_lengths)
    before = ends[None, :] <= places[:, None]
    begin = jnp.max(jnp.where(before, ends[None, :], 0), axis=1)
    finish = jnp.min(jnp.where(before, devices * rows, ends[None, :]), axis=1)
    seg = jnp.stack([begin - base, finish - base]).astype(jnp.int32)
    low = seg[0, ::BQ] // BK
    high = -(-seg[1, BQ - 1 :: BQ] // BK)

    x = tokens.astype(F32)
    u1, rstd1 = normalised(x)
    n1, q, kv = plane_qkv(tokens, slab, me, devices)
    prefetch, edge_blocks = (low, high), halo // BK
    left = shifted(kv[span - halo :], GROUP, devices)
    right = shifted(kv[:halo], -GROUP, devices)
    acc, stat = forward_mid(prefetch, seg, q, kv, edge_blocks)
    acc, stat, left, right = lax.optimization_barrier((acc, stat, left, right))
    o_heads, lse = forward_edge(prefetch, seg, q, left, right, acc, stat)
    (o,) = to_tokens([o_heads], devices)

    branch = mm(o, w_proj) + bias_proj
    y1 = x + layer_attn * branch
    u2, rstd2 = normalised(y1)
    n2 = (u2 * gain2 + shift2).astype(BF16)
    g = cotangent.astype(F32)
    dm = layer_mlp * g
    d_fc2_bias = jnp.sum(dm, axis=0)
    dml = dm.astype(BF16)
    if by_axes:
        mlp, dn2, d_fc1_bias, keep1, send1, keep2, send2 = mlp_all(n2, dml, big, w_fc2, bias_fc1, me, shard_rows)
        d_fc1_bias = d_fc1_bias.reshape(-1)
    else:
        act, slope = gelu_parts(mm(n2, big) + bias_fc1)
        act = act.astype(BF16)
        mlp = mm(act, w_fc2)
        dz = mm_t(dml, w_fc2) * slope
        d_fc1_bias = jnp.sum(dz, axis=0)
        dz = dz.astype(BF16)
        dn2 = mm_t(dz, big)
        d_fc1, d_fc2 = scattered(t_mm(n2, dz)), scattered(t_mm(act, dml))
    if by_axes:
        vec = jnp.stack([layer_attn, gain2, layer_mlp, bias_fc2])
        block_out, dy1, totals, do, keep3, send3 = after_mlp(
            mlp, dn2, tokens, branch, cotangent, o, big, vec, me, shard_rows
        )
        d_scale_mlp, d_fc2_bias, d_gain2, d_shift2, d_scale_attn, d_proj_bias = (totals[i] for i in range(6))
        got1, got2, got3 = (swapped(s, 1, devices) for s in (send1, send2, send3))
        view = (devices // GROUP, 2, 2, shard_rows)
        halves = [
            tuple(s.reshape(*view, -1) for s in pair) for pair in ((keep1, got1), (keep2, got2), (keep3, got3))
        ]
        out_a, out_b = first_sends(halves, me)
    else:
        mlp = mlp + bias_fc2
        block_out = (y1 + layer_mlp * mlp).astype(BF16)
        d_scale_mlp = jnp.sum(g * mlp, axis=0)
        d_gain2 = jnp.sum(dn2 * u2, axis=0)
        d_shift2 = jnp.sum(dn2, axis=0)
        dy1 = g + norm_back(u2, rstd2, dn2 * gain2)
        d_scale_attn = jnp.sum(dy1 * branch, axis=0)
        db = layer_attn * dy1
        d_proj_bias = jnp.sum(db, axis=0)
        dbl = db.astype(BF16)
        d_proj = scattered(t_mm(o, dbl))
        do = mm_t(dbl, w_proj).astype(BF16).reshape(rows, GROUP, -1).transpose(1, 0, 2)

    do_heads = in_plane(do, devices).reshape(span, -1)
    if by_axes:
        do_heads, out_a, out_b = lax.optimization_barrier((do_heads, out_a, out_b))
        in_a, in_b = swapped(out_a, 2, devices), swapped(out_b, 4, devices)
    part_dq, mid0, out_left, out_right = backward_first(prefetch, seg, q, kv, left, right, o_heads, do_heads, lse)
    if by_axes:
        part_dq, in_a, in_b, w_qkv = lax.optimization_barrier((part_dq, in_a, in_b, w_qkv))
        out_a, sum_a, out_b, sum_b = second_sums(halves, in_a, in_b, me)
        part_dq, out_a, out_b = lax.optimization_barrier((part_dq, out_a, out_b))
        in_a, in_b = swapped(out_a, 4, devices), swapped(out_b, 2, devices)
    from_right = shifted(out_left, -GROUP, devices)
    from_left = shifted(out_right, GROUP, devices)
    dq, mid1 = backward_second(prefetch, seg, q, kv, o_heads, do_heads, lse, part_dq, edge_blocks)
    dq, mid1, from_left, from_right = lax.optimization_barrier((dq, mid1, from_left, from_right))
    if by_axes:
        dq, in_a, in_b = lax.optimization_barrier((dq, in_a, in_b))
    d_heads = joined_heads(dq, mid0, mid1, from_left, from_right)
    if by_axes:
        third = [(s.astype(F32) + i.astype(F32)).astype(BF16) for s, i in ((sum_a, in_a), (sum_b, in_b))]
        d_heads, third = lax.optimization_barrier((d_heads, jnp.concatenate(third, axis=-1)))
        own_sums, sums = from_planes(third, me, devices)
    dqkv = in_plane(d_heads.reshape(GROUP, rows, -1), devices)
    if by_axes:
        dqkv, n1, sums[0] = lax.optimization_barrier((dqkv, n1, sums[0]))
    d_qkv = t_mm(n1, d_heads).astype(BF16).reshape(devices // GROUP, GROUP, shard_rows, -1)
    dqkv, d_qkv = lax.optimization_barrier((dqkv, d_qkv))
    own_qkv, got_qkv = from_planes(d_qkv, me, devices)
    grad_tokens, totals, per_head = input_gradient(dqkv, w_qkv, dy1, tokens, gain1)
    d_gain1, d_shift1, half = totals[0], totals[1], width // GROUP
    d_qv_bias = jnp.concatenate([per_head[:, :half].reshape(-1), per_head[:, 2 * half :].reshape(-1)])
    if by_axes:
        d_gain1, sums[1:], got_qkv = lax.optimization_barrier((d_gain1, sums[1:], got_qkv))
    d_qkv = in_plane(total_of(own_qkv, got_qkv), devices).reshape(GROUP, shard_rows, 3, -1)
    d_qkv = d_qkv.transpose(1, 2, 0, 3).reshape(shard_rows, 3 * width)
    if by_axes:
        sums = total_of(own_sums, sums)
        d_fc1 = sums[:, :hidden]
        cut = width // 2
        at = hidden + cut
        d_fc2 = sums[:, at : at + hidden].reshape(shard_rows, blocks, width).transpose(1, 0, 2)
        d_fc2 = d_fc2.reshape(blocks * shard_rows, width)
        d_proj = jnp.concatenate([sums[:, hidden:at], sums[:, at + hidden :]], axis=1)
    small = (
        d_gain1, d_shift1, d_qv_bias, d_proj_bias, d_scale_attn, d_gain2, d_shift2, d_fc1_bias, d_fc2_bias, d_scale_mlp,
    )
    small = lax.all_to_all(pack(small, devices), "dev", 0, 0, tiled=True)
    small = jnp.sum(small, axis=0, keepdims=True)
    s_gain1, s_shift1, s_qv, s_proj, s_attn, s_gain2, s_shift2, s_fc1, s_fc2, s_mlp = unpack(small, sizes)
    return (
        block_out,
        grad_tokens,
        s_gain1,
        s_shift1,
        d_qkv,
        s_qv,
        d_proj,
        s_proj,
        s_attn,
        s_gain2,
        s_shift2,
        d_fc1,
        s_fc1,
        d_fc2,
        s_fc2,
        s_mlp,
    )


def solution(mesh):
    matrix, vector = P("dev", None), P("dev")
    return jax.shard_map(
        body,
        mesh=mesh,
        in_specs=(
            matrix, matrix, P(), vector, vector, matrix, vector, matrix, vector, vector, vector, vector, matrix,
            vector, matrix, vector, vector,
        ),
        out_specs=(
            matrix, matrix, vector, vector, matrix, vector, matrix, vector, vector, vector, vector, matrix, vector,
            matrix, vector, vector,
        ),
        check_vma=False,
    )
```

```python
import functools

import jax
import jax.numpy as jnp
from jax import lax
from jax.experimental import pallas as pl
from jax.experimental.pallas import tpu as pltpu
from jax.sharding import PartitionSpec as P

BQ = 256
BK = 256
SLAB = 2 * BK
HD = 64
LOG2E = 1.4426950408889634
SCALE = 0.125
MASKED = -1e30
NT = (((1,), (1,)), ((), ()))


def head_halves(block):
    first = lax.broadcasted_iota(jnp.int32, block.shape, 1) < HD
    zero = jnp.zeros_like(block)
    return jnp.where(first, block, zero), jnp.where(first, zero, block)


def transpose_into(target, source, column):
    width = target.shape[0]
    for j in range(source.shape[0] // BK):
        part = source[j * BK : (j + 1) * BK, column : column + width].astype(jnp.float32)
        target[:, j * BK : (j + 1) * BK] = part.T.astype(target.dtype)


def slabs(low, high, first, last):
    low = jnp.clip(low, first, last) - first
    count = (jnp.clip(high, first, last) - first - low + 1) // 2
    return jnp.minimum(low, last - first - 2 * count), count


def slab_rows(start, t):
    return pl.ds(pl.multiple_of((start + 2 * t) * BK, BK), SLAB)


def forward_over(span, kv_ref, v_t, offset, q_heads, seg, carry):
    start, count = span
    width = q_heads[0].shape[1]
    begin, end = seg[0:1, :], seg[1:2, :]
    place = lax.broadcasted_iota(jnp.int32, (SLAB, BQ), 0) + offset

    def one_slab(t, carry):
        rows = slab_rows(start, t)
        keys = kv_ref[rows, :width]
        at = place + (start + 2 * t) * BK
        valid = (at >= begin) & (at < end)
        out = []
        for h in range(2):
            top, total, acc = carry[h]
            s = lax.dot_general(keys, q_heads[h], NT, preferred_element_type=jnp.float32)
            s = jnp.where(valid, s * (SCALE * LOG2E), MASKED)
            new_top = jnp.maximum(top, jnp.max(s, axis=0, keepdims=True))
            p = jnp.exp2(s - new_top)
            fade = jnp.exp2(top - new_top)
            total = total * fade + jnp.sum(p, axis=0, keepdims=True)
            v_part = v_t[h * HD : (h + 1) * HD, rows]
            acc = acc * fade + jnp.dot(v_part, p.astype(jnp.bfloat16), preferred_element_type=jnp.float32)
            out.append((new_top, total, acc))
        return tuple(out)

    return lax.fori_loop(0, count, one_slab, carry)


def forward_mid_kernel(low, high, seg, q_ref, kv_ref, acc_ref, stat_ref, v_t, *, edge):
    step = pl.program_id(0)

    @pl.when(step == 0)
    def _():
        transpose_into(v_t, kv_ref, q_ref.shape[1])

    start = (
        jnp.full((1, BQ), MASKED, jnp.float32),
        jnp.zeros((1, BQ), jnp.float32),
        jnp.zeros((HD, BQ), jnp.float32),
    )
    blocks = kv_ref.shape[0] // BK
    span = slabs(low[step], high[step], edge, edge + blocks)
    done = forward_over(span, kv_ref, v_t, edge * BK, head_halves(q_ref[...]), seg, (start, start))
    for h, (top, total, acc) in enumerate(done):
        stat_ref[2 * h : 2 * h + 1, :] = top
        stat_ref[2 * h + 1 : 2 * h + 2, :] = total
        acc_ref[h * HD : (h + 1) * HD, :] = acc


def forward_edge_kernel(
    low, high, seg, q_ref, left_ref, right_ref, acc_ref, stat_ref, o_ref, lse_ref, left_t, right_t, *, last
):
    step = pl.program_id(0)
    width = q_ref.shape[1]
    edge = left_ref.shape[0] // BK

    @pl.when(step == 0)
    def _():
        transpose_into(left_t, left_ref, width)
        transpose_into(right_t, right_ref, width)

    carry = tuple(
        (stat_ref[2 * h : 2 * h + 1, :], stat_ref[2 * h + 1 : 2 * h + 2, :], acc_ref[h * HD : (h + 1) * HD, :])
        for h in range(2)
    )
    q_heads = head_halves(q_ref[...])
    span = slabs(low[step], high[step], 0, edge)
    carry = forward_over(span, left_ref, left_t, 0, q_heads, seg, carry)
    span = slabs(low[step], high[step], last, last + edge)
    carry = forward_over(span, right_ref, right_t, last * BK, q_heads, seg, carry)
    o_ref[...] = jnp.concatenate([acc / total for _, total, acc in carry], axis=0).T.astype(o_ref.dtype)
    for h, (top, total, _) in enumerate(carry):
        lse_ref[h : h + 1, :] = top + jnp.log2(total)


def backward_setup(q_ref, do_ref, o_ref, lse_ref, heads):
    prod = (do_ref[...].astype(jnp.float32) * o_ref[...].astype(jnp.float32)).T
    q_heads, do_heads = head_halves(q_ref[...]), head_halves(do_ref[...])
    return [
        (
            h,
            q_heads[h],
            do_heads[h],
            jnp.sum(prod[h * HD : (h + 1) * HD], axis=0, keepdims=True),
            lse_ref[h : h + 1, :],
        )
        for h in heads
    ]


def backward_over(span, kv_ref, k_t, dkv, dq_t, offset, heads, seg):
    start, count = span
    width = dq_t.shape[0]
    begin, end = seg[0:1, :], seg[1:2, :]
    place = lax.broadcasted_iota(jnp.int32, (SLAB, BQ), 0) + offset
    q_all = jnp.concatenate([q for _, q, _, _, _ in heads], axis=0)
    do_all = jnp.concatenate([d for _, _, d, _, _ in heads], axis=0)

    @pl.loop(0, count)
    def _(t):
        rows = slab_rows(start, t)
        keys, values = kv_ref[rows, :width], kv_ref[rows, width:]
        at = place + (start + 2 * t) * BK
        valid = (at >= begin) & (at < end)
        ps, dss = [], []
        for h, q, do, centre, lse in heads:
            s = lax.dot_general(keys, q, NT, preferred_element_type=jnp.float32)
            p = jnp.where(valid, jnp.exp2(s * (SCALE * LOG2E) - lse), 0.0)
            dp = lax.dot_general(values, do, NT, preferred_element_type=jnp.float32)
            ds = (p * (dp - centre)).astype(jnp.bfloat16)
            ps.append(p.astype(jnp.bfloat16))
            dss.append(ds)
            part = slice(h * HD, (h + 1) * HD)
            dq_t[part, :] += jnp.dot(k_t[part, rows], ds, preferred_element_type=jnp.float32)
        dkv[rows, :width] += jnp.dot(jnp.concatenate(dss, axis=1), q_all, preferred_element_type=jnp.float32)
        dkv[rows, width:] += jnp.dot(jnp.concatenate(ps, axis=1), do_all, preferred_element_type=jnp.float32)


def backward_first_kernel(
    low, high, seg, q_ref, kv_ref, left_ref, right_ref, o_ref, do_ref, lse_ref, dq_t, mid_ref, out_left, out_right,
    left_t, right_t, k_t, dkv, *, last
):
    step = pl.program_id(0)
    width = q_ref.shape[1]
    edge = left_ref.shape[0] // BK

    @pl.when(step == 0)
    def _():
        transpose_into(left_t, left_ref, 0)
        transpose_into(right_t, right_ref, 0)
        transpose_into(k_t, kv_ref, 0)
        dkv[...] = jnp.zeros_like(dkv)
        mid_ref[...] = jnp.zeros_like(mid_ref)

    heads = backward_setup(q_ref, do_ref, o_ref, lse_ref, range(2))
    dq_t[...] = jnp.zeros_like(dq_t)
    span = slabs(low[step], high[step], 0, edge)
    backward_over(span, left_ref, left_t, dkv.at[0], dq_t, 0, heads, seg)
    span = slabs(low[step], high[step], last, last + edge)
    backward_over(span, right_ref, right_t, dkv.at[1], dq_t, last * BK, heads, seg)
    span = slabs(low[step], high[step], edge, last)
    backward_over(span, kv_ref, k_t, mid_ref, dq_t, edge * BK, heads[:1], seg)

    @pl.when(step == pl.num_programs(0) - 1)
    def _():
        for side, out in enumerate((out_left, out_right)):
            out[:, :width] = (dkv[side, :, :width] * SCALE).astype(out.dtype)
            out[:, width:] = dkv[side, :, width:].astype(out.dtype)


def backward_mid_kernel(
    low, high, seg, q_ref, kv_ref, o_ref, do_ref, lse_ref, part_ref, first_ref, dq_ref, mid_ref, k_t, dq_t, *, edge
):
    step = pl.program_id(0)
    width = q_ref.shape[1]

    @pl.when(step == 0)
    def _():
        transpose_into(k_t, kv_ref, 0)
        mid_ref[...] = first_ref[...]

    dq_t[...] = part_ref[...]
    blocks = kv_ref.shape[0] // BK
    span = slabs(low[step], high[step], edge, edge + blocks)
    heads = backward_setup(q_ref, do_ref, o_ref, lse_ref, [1])
    backward_over(span, kv_ref, k_t, mid_ref, dq_t, edge * BK, heads, seg)
    dq_ref[...] = (dq_t[...] * SCALE).T.astype(dq_ref.dtype)

    @pl.when(step == pl.num_programs(0) - 1)
    def _():
        mid_ref[:, :width] = mid_ref[:, :width] * SCALE


def whole_spec(array):
    return pl.BlockSpec(array.shape, lambda i, *_: (0,) * len(array.shape))


def attention_call(kernel, name, prefetch, inputs, in_kinds, outputs, out_kinds, scratch, work):
    span = prefetch[0].shape[0] * BQ

    def spec(array, kind):
        if kind == "r":
            return pl.BlockSpec((BQ, array.shape[1]), lambda i, *_: (i, 0))
        if kind == "c":
            return pl.BlockSpec((array.shape[0], BQ), lambda i, *_: (0, i))
        return whole_spec(array)

    return pl.pallas_call(
        kernel,
        out_shape=tuple(outputs),
        grid_spec=pltpu.PrefetchScalarGridSpec(
            num_scalar_prefetch=2,
            grid=(span // BQ,),
            in_specs=[spec(a, k) for a, k in zip(inputs, in_kinds)],
            out_specs=[spec(a, k) for a, k in zip(outputs, out_kinds)],
            scratch_shapes=scratch,
        ),
        compiler_params=pltpu.CompilerParams(vmem_limit_bytes=48 << 20),
        cost_estimate=pl.CostEstimate(flops=work << 30, bytes_accessed=8 << 20, transcendentals=span * 128),
        name=name,
    )(*prefetch, *inputs)


def shaped(*shape, dtype=jnp.float32):
    return jax.ShapeDtypeStruct(shape, dtype)


def forward_mid(prefetch, seg, q, kv, edge):
    span, width = q.shape
    return attention_call(
        functools.partial(forward_mid_kernel, edge=edge), "forward_mid", prefetch, [seg, q, kv], "crw",
        [shaped(width, span), shaped(8, span)], "cc", [pltpu.VMEM((width, span), jnp.bfloat16)], 3,
    )


def forward_edge(prefetch, seg, q, left, right, acc, stat):
    span, width = q.shape
    halo = pltpu.VMEM((width, left.shape[0]), jnp.bfloat16)
    return attention_call(
        functools.partial(forward_edge_kernel, last=(left.shape[0] + span) // BK), "forward_edge", prefetch,
        [seg, q, left, right, acc, stat], "crwwcc",
        [shaped(span, width, dtype=jnp.bfloat16), shaped(8, span)], "rc", [halo, halo], 3,
    )


def backward_first(prefetch, seg, q, kv, left, right, o, do, lse):
    span, width = q.shape
    halo = pltpu.VMEM((width, left.shape[0]), jnp.bfloat16)
    return attention_call(
        functools.partial(backward_first_kernel, last=(left.shape[0] + span) // BK), "backward_first", prefetch,
        [seg, q, kv, left, right, o, do, lse], "crwwwrrc",
        [shaped(width, span), shaped(*kv.shape)] + [shaped(*left.shape, dtype=jnp.bfloat16)] * 2, "cwww",
        [halo, halo, pltpu.VMEM((width, span), jnp.bfloat16), pltpu.VMEM((2, *left.shape), jnp.float32)], 3,
    )


def backward_second(prefetch, seg, q, kv, o, do, lse, part, first, edge):
    span, width = q.shape
    return attention_call(
        functools.partial(backward_mid_kernel, edge=edge), "backward_second", prefetch,
        [seg, q, kv, o, do, lse, part, first], "crwrrccw",
        [shaped(span, width, dtype=jnp.bfloat16), shaped(*kv.shape)], "rw",
        [pltpu.VMEM((width, span), jnp.bfloat16), pltpu.VMEM((width, BQ), jnp.float32)], 3,
    )


HEADS = 16
SEQ = 1370
GROUP = 8
EPS = 1e-06
F32, BF16 = jnp.float32, jnp.bfloat16


def mm(left, right):
    return jnp.dot(left, right, preferred_element_type=F32)


def mm_t(left, right):
    return jnp.einsum("tf,df->td", left, right, preferred_element_type=F32)


def t_mm(left, right):
    return jnp.einsum("td,tf->df", left, right, preferred_element_type=F32)


def normalised(value):
    centre = value - jnp.mean(value, axis=-1, keepdims=True)
    rstd = lax.rsqrt(jnp.mean(centre * centre, axis=-1, keepdims=True) + EPS)
    return centre * rstd, rstd


def norm_back(unit, rstd, grad):
    first = jnp.mean(grad, axis=-1, keepdims=True)
    second = jnp.mean(grad * unit, axis=-1, keepdims=True)
    return rstd * (grad - first - unit * second)


def gelu_parts(z):
    half = 0.5 * (1.0 + lax.erf(z * 0.7071067811865476))
    slope = half + z * (0.3989422804014327 * jnp.exp(-0.5 * z * z))
    return z * half, slope


def groups_of(count):
    return [list(range(first, first + GROUP)) for first in range(0, count, GROUP)]


def gathered(shard):
    return lax.all_gather(shard, "dev", axis=0, tiled=True)


def scattered(whole):
    return lax.psum_scatter(whole, "dev", scatter_dimension=0, tiled=True)


def pack(vectors, count):
    return jnp.concatenate([v.reshape(count, -1) for v in vectors], axis=1)


def unpack(packed, sizes):
    out, at = [], 0
    for size in sizes:
        out.append(packed[:, at : at + size].reshape(-1))
        at += size
    return out


def to_heads(parts, devices):
    rows = parts[0].shape[0]
    sent = jnp.stack([p.reshape(rows, GROUP, -1) for p in parts], axis=2)
    sent = sent.transpose(1, 0, 2, 3)
    back = lax.all_to_all(sent, "dev", 0, 0, axis_index_groups=groups_of(devices), tiled=True)
    return [back[:, :, i].reshape(GROUP * rows, -1) for i in range(len(parts))]


def to_tokens(parts, devices):
    rows = parts[0].shape[0] // GROUP
    sent = jnp.stack([p.reshape(GROUP, rows, -1) for p in parts], axis=2)
    back = lax.all_to_all(sent, "dev", 0, 0, axis_index_groups=groups_of(devices), tiled=True)
    return [back[:, :, i].transpose(1, 0, 2).reshape(rows, -1) for i in range(len(parts))]


def shifted(shard, by, devices):
    pairs = [(i, i + by) for i in range(devices) if 0 <= i + by < devices]
    return lax.ppermute(shard, "dev", pairs)


def take(stack, index, axis):
    return lax.dynamic_index_in_dim(stack, index, axis, keepdims=False)


def swapped(value, bit, devices):
    return lax.ppermute(value, "dev", [(i, i ^ bit) for i in range(devices)])


def join_kernel(dq, mid, left, right, out):
    width = dq.shape[1]
    step, edge = pl.program_id(0), pl.num_programs(0) // 2
    halo = jnp.where(step < edge, left[...], right[...]).astype(F32)
    out[:, :width] = dq[...]
    out[:, width:] = (mid[...] + halo).astype(out.dtype)


def joined_heads(dq, mid, left, right):
    span, width = dq.shape
    size = 3 * BQ
    half = span // (2 * size)
    rows = [pl.BlockSpec((size, columns), lambda i: (i, 0)) for columns in (width, 2 * width, 3 * width)]
    return pl.pallas_call(
        join_kernel,
        out_shape=shaped(span, 3 * width, dtype=BF16),
        grid=(span // size,),
        in_specs=rows[:2]
        + [
            pl.BlockSpec((size, 2 * width), lambda i: (jnp.minimum(i, half - 1), 0)),
            pl.BlockSpec((size, 2 * width), lambda i: (jnp.maximum(i - half, 0), 0)),
        ],
        out_specs=rows[2],
        cost_estimate=pl.CostEstimate(flops=0, bytes_accessed=10 << 20, transcendentals=0),
        name="joined_heads",
    )(dq, mid, left, right)


def tail_kernel(dqkv, weight, dy1, x_ref, gain, grad, sums, heads):
    size = dqkv.shape[2]
    dn1 = jnp.zeros(dy1.shape, F32)
    for j in range(dqkv.shape[0]):
        dn1 += lax.dot_general(
            dqkv[j], weight[:, j * size : (j + 1) * size], NT, preferred_element_type=F32
        )
        heads[j : j + 1, :] = jnp.sum(dqkv[j].astype(F32), axis=0, keepdims=True)
    unit, rstd = normalised(x_ref[...].astype(F32))
    grad[...] = (dy1[...] + norm_back(unit, rstd, dn1 * gain[...])).astype(grad.dtype)
    sums[0:1, :] = jnp.sum(dn1 * unit, axis=0, keepdims=True)
    sums[1:2, :] = jnp.sum(dn1, axis=0, keepdims=True)


def input_gradient(dqkv, weight, dy1, tokens, gain):
    inputs = (dqkv, weight, dy1, tokens, gain[None])
    outs = (shaped(*tokens.shape, dtype=BF16), shaped(8, tokens.shape[1]), shaped(GROUP, dqkv.shape[2]))
    return pl.pallas_call(
        tail_kernel,
        out_shape=outs,
        grid=(1,),
        in_specs=[whole_spec(a) for a in inputs],
        out_specs=[whole_spec(a) for a in outs],
        compiler_params=pltpu.CompilerParams(vmem_limit_bytes=44 << 20),
        cost_estimate=pl.CostEstimate(flops=2 * weight.size * tokens.shape[0], bytes_accessed=12 << 20, transcendentals=0),
        name="input_gradient",
    )(*inputs)


def in_plane(stack, devices):
    return lax.all_to_all(stack, "dev", 0, 0, axis_index_groups=groups_of(devices), tiled=True)


def position(me):
    return (me // 4) % 2, (me // 2) % 2, me % 2


def qkv_kernel(bits, near_a, far_a, near_b, far_b, slab, n1_ref, q_ref, kv_ref, lines, bias, *, rows):
    step = pl.program_id(0)
    third = q_ref.shape[1]
    width = slab.shape[0]

    @pl.when(step == 0)
    def _():
        lines[...] = slab[:, 3 * third :].astype(F32).T
        group = bits[3]
        unit = lax.broadcasted_iota(jnp.int32, (width, third), 0)
        place = lax.broadcasted_iota(jnp.int32, (width, third), 1)
        some = lines[0:16, :].astype(BF16)
        bias[...] = jnp.zeros_like(bias)
        for part, first in ((0, 0), (2, width // 2)):
            total = jnp.zeros((1, third), F32)
            for column in range(2):
                at = first + group * (third // 2) + (place // (2 * rows)) * rows + place % rows
                chosen = (unit == at) & ((place // rows) % 2 == column)
                total = total + mm(some, jnp.where(chosen, 1.0, 0.0).astype(BF16))[2 + column : 3 + column]
            bias[0:1, part * third : (part + 1) * third] = total

    far = step >= 4
    left = jnp.where(far, far_a[0, 0], near_a[0, 0])
    right = jnp.where(far, far_b[0, 0], near_b[0, 0])
    unit, _ = normalised(jnp.concatenate([left, right], axis=1).astype(F32))
    n1 = (unit * lines[0:1, :] + lines[1:2, :]).astype(BF16)
    n1_ref[...] = n1
    out = (mm(n1, slab[:, : 3 * third]) + bias[0:1, :]).astype(BF16)
    q_ref[...] = out[:, :third]
    kv_ref[...] = out[:, third:]


def plane_qkv(tokens, slab, me, devices):
    rows, width = tokens.shape
    half, third = width // 2, (slab.shape[2] - 128) // 3
    a, b = tokens[:, :half], tokens[:, half:]
    got_a, got_b, slab = lax.optimization_barrier((swapped(a, 4, devices), swapped(b, 2, devices), slab))
    slab = lax.all_to_all(slab, "dev", 0, 0, tiled=True).reshape(width, -1)
    packed = slab[:, -128:]
    a, b = jnp.stack([a, got_a]), jnp.stack([b, got_b])
    a = jnp.stack([a, swapped(a, 2, devices)])
    b = jnp.stack([b, swapped(b, 4, devices)])
    a, b, slab = lax.optimization_barrier((a, b, slab))
    far_a, far_b = swapped(a, 1, devices), swapped(b, 1, devices)

    def near_at(s, swap):
        i, j = (s // 2) % 2, s % 2
        i, j = jnp.where(s < 4, i, 1), jnp.where(s < 4, j, 1)
        return (j, i, 0, 0) if swap else (i, j, 0, 0)

    def far_at(s, swap):
        i, j = (s // 2) % 2, s % 2
        i, j = jnp.where(s < 4, 0, i), jnp.where(s < 4, 0, j)
        return (j, i, 0, 0) if swap else (i, j, 0, 0)

    def place(s, bits):
        return ((bits[0] ^ (s % 2)) * 4 + (bits[1] ^ ((s // 2) % 2)) * 2 + (bits[2] ^ (s // 4)), 0)

    piece = (1, 1, rows, half)
    span = GROUP * rows
    out = pl.pallas_call(
        functools.partial(qkv_kernel, rows=width // devices),
        out_shape=(
            jax.ShapeDtypeStruct((span, width), BF16),
            jax.ShapeDtypeStruct((span, third), BF16),
            jax.ShapeDtypeStruct((span, 2 * third), BF16),
        ),
        grid_spec=pltpu.PrefetchScalarGridSpec(
            num_scalar_prefetch=1,
            grid=(GROUP,),
            in_specs=[
                pl.BlockSpec(piece, lambda s, bits: near_at(s, False)),
                pl.BlockSpec(piece, lambda s, bits: far_at(s, False)),
                pl.BlockSpec(piece, lambda s, bits: near_at(s, True)),
                pl.BlockSpec(piece, lambda s, bits: far_at(s, True)),
                pl.BlockSpec(slab.shape, lambda s, bits: (0, 0)),
            ],
            out_specs=[pl.BlockSpec((rows, columns), place) for columns in (width, third, 2 * third)],
            scratch_shapes=[pltpu.VMEM((128, width), F32), pltpu.VMEM((8, 3 * third), F32)],
        ),
        compiler_params=pltpu.CompilerParams(vmem_limit_bytes=40 << 20),
        cost_estimate=pl.CostEstimate(flops=5 << 30, bytes_accessed=16 << 20, transcendentals=0),
        name="plane_qkv",
    )(
        jnp.stack([*position(me), me % GROUP]).astype(jnp.int32), a, far_a, b, far_b, slab,
    )
    return (*out, packed)


def plane_pieces(stack, me, devices):
    planes, mine = devices // GROUP, me // GROUP
    return take(stack, mine, 0), [take(stack, (mine + k) % planes, 0) for k in range(1, planes)]


def send_planes(pieces, devices):
    return [
        lax.ppermute(piece, "dev", [(i, (i + (k + 1) * GROUP) % devices) for i in range(devices)])
        for k, piece in enumerate(pieces)
    ]


def total_of(own, others):
    total = own.astype(F32)
    for other in others:
        total = total + other.astype(F32)
    return total


def pack_columns(vectors, rows):
    columns = jnp.concatenate([v.reshape(-1, rows).T for v in vectors], axis=1)
    return jnp.pad(columns, ((0, 0), (0, 128 - columns.shape[1])))


def unpack_columns(packed, sizes, rows):
    lines, out, at = packed[:, :16].T, [], 0
    for size in sizes:
        count = size // rows
        part = lines[at : at + count].reshape(count, -1, rows)
        out.append(part.transpose(1, 0, 2).reshape(-1))
        at += count
    return out


def by_parity(transposed, parity, rows):
    blocks = transposed.reshape(-1, 2, rows, transposed.shape[1])
    even, odd = (blocks[:, s].reshape(-1, transposed.shape[1]) for s in range(2))
    return jnp.where(parity == 0, even, odd), jnp.where(parity == 0, odd, even)


def turned(value):
    return value.astype(F32).T.astype(BF16)


def mlp_kernel(
    bits, n2_ref, dml_ref, f1_ref, f2_ref, bias, mlp_ref, dn2_ref, db_ref, keep1, send1, keep2, send2, n2_t
):
    step = pl.program_id(0)
    rows = keep1.shape[1]

    @pl.when(step == 0)
    def _():
        mlp_ref[...] = jnp.zeros_like(mlp_ref)
        dn2_ref[...] = jnp.zeros_like(dn2_ref)
        n2_t[0], n2_t[1] = by_parity(turned(n2_ref[...]), bits[2], rows)

    n2, dml = n2_ref[...], dml_ref[...]
    f1 = f1_ref[...].reshape(n2.shape[1], -1)
    f2 = f2_ref[...].reshape(-1, n2.shape[1])
    act, slope = gelu_parts(mm(n2, f1) + bias[...])
    act = act.astype(BF16)
    mlp_ref[...] += mm(act, f2)
    dz = lax.dot_general(dml, f2, NT, preferred_element_type=F32) * slope
    db_ref[...] = jnp.sum(dz, axis=0, keepdims=True)
    dz = dz.astype(BF16)
    dn2_ref[...] += lax.dot_general(dz, f1, NT, preferred_element_type=F32)
    for side, out in enumerate((keep1, send1)):
        out[...] = mm(n2_t[side], dz).astype(BF16).reshape(out.shape)
    width = n2.shape[1]
    parts = keep2.shape[2] // width
    for part, out in zip(by_parity(turned(act), bits[2], parts * rows), (keep2, send2)):
        grad = mm(part, dml).astype(BF16).reshape(out.shape[0], parts, rows, width)
        for i in range(parts):
            out[:, :, i * width : (i + 1) * width] = grad[:, i]


def mlp_all(n2, dml, big, bias, me, shard_rows):
    tokens, width = n2.shape
    hidden, owners = bias.shape[0], width // shard_rows
    size = width // 2
    steps = hidden // size
    whole = pl.BlockSpec((tokens, width), lambda s, bits: (0, 0))
    first = pl.BlockSpec((owners // 2, shard_rows, size), lambda s, bits: (0, 0, s))
    second = pl.BlockSpec((owners // (2 * steps), shard_rows, hidden), lambda s, bits: (s, 0, 0))
    line = pl.BlockSpec((1, size), lambda s, bits: (0, s))
    grads = jax.ShapeDtypeStruct((owners // 2, shard_rows, hidden), BF16)
    total = jax.ShapeDtypeStruct((tokens, width), F32)
    return pl.pallas_call(
        mlp_kernel,
        out_shape=(total, total, jax.ShapeDtypeStruct((1, hidden), F32), grads, grads, grads, grads),
        grid_spec=pltpu.PrefetchScalarGridSpec(
            num_scalar_prefetch=1,
            grid=(steps,),
            in_specs=[
                whole,
                whole,
                pl.BlockSpec((owners, shard_rows, size), lambda s, bits: (0, s // 2, s % 2)),
                pl.BlockSpec((owners // steps, hidden // owners, width), lambda s, bits: (s, 1, 0)),
                line,
            ],
            out_specs=[whole, whole, line, first, first, second, second],
            scratch_shapes=[pltpu.VMEM((2, width // 2, tokens), BF16)],
        ),
        compiler_params=pltpu.CompilerParams(vmem_limit_bytes=52 << 20),
        cost_estimate=pl.CostEstimate(
            flops=4 * tokens * width * hidden, bytes_accessed=8 * width * hidden, transcendentals=2 * tokens * hidden
        ),
        name="mlp_all",
    )(jnp.stack(position(me)).astype(jnp.int32), n2, dml, big, big, bias[None])


def grad_kernel(bits, a_ref, b_ref, keep_ref, send_ref):
    for part, out in zip(by_parity(turned(a_ref[...]), bits[2], keep_ref.shape[1]), (keep_ref, send_ref)):
        out[...] = mm(part, b_ref[...]).astype(BF16).reshape(out.shape)


def weight_grad(a, b, rows, me):
    out = jax.ShapeDtypeStruct((a.shape[1] // (2 * rows), rows, b.shape[1]), BF16)
    return pl.pallas_call(
        grad_kernel,
        out_shape=(out, out),
        grid_spec=pltpu.PrefetchScalarGridSpec(num_scalar_prefetch=1, grid=(1,)),
        compiler_params=pltpu.CompilerParams(vmem_limit_bytes=40 << 20),
        cost_estimate=pl.CostEstimate(
            flops=2 * a.size * b.shape[1], bytes_accessed=2 * (a.size + b.size + 2 * out.size), transcendentals=0
        ),
        name="weight_grad",
    )(jnp.stack(position(me)).astype(jnp.int32), a, b)


def after_mlp_kernel(
    bits, mlp, dn2, x_ref, branch, g_ref, o_ref, w_proj, vec, block_out, dy1_ref, sums, do_ref, keep, send
):
    layer_attn, gain2, layer_mlp, bias = (vec[i : i + 1, :] for i in range(4))
    g, out = g_ref[...].astype(F32), mlp[...] + bias
    y1 = x_ref[...].astype(F32) + layer_attn * branch[...]
    unit, rstd = normalised(y1)
    block_out[...] = (y1 + layer_mlp * out).astype(BF16)
    dy1 = g + norm_back(unit, rstd, dn2[...] * gain2)
    dy1_ref[...] = dy1
    db = layer_attn * dy1
    totals = (g * out, layer_mlp * g, dn2[...] * unit, dn2[...], dy1 * branch[...], db)
    for i, total in enumerate(totals):
        sums[i : i + 1, :] = jnp.sum(total, axis=0, keepdims=True)
    dbl = db.astype(BF16)
    weight = w_proj[...].reshape(dbl.shape[1], -1)
    do = lax.dot_general(dbl, weight, NT, preferred_element_type=F32).astype(BF16)
    columns = do_ref.shape[2]
    for j in range(do_ref.shape[0]):
        do_ref[j] = do[:, j * columns : (j + 1) * columns]
    for part, to in zip(by_parity(turned(o_ref[...]), bits[2], keep.shape[1]), (keep, send)):
        to[...] = mm(part, dbl).astype(BF16).reshape(to.shape)


def after_mlp(mlp, dn2, x, branch, g, o, big, vec, me, shard_rows):
    tokens, width = mlp.shape
    owners = width // shard_rows
    grads = shaped(owners // 2, shard_rows, width, dtype=BF16)
    outs = (
        shaped(tokens, width, dtype=BF16), shaped(tokens, width), shaped(8, width),
        shaped(GROUP, tokens, width // GROUP, dtype=BF16), grads, grads,
    )
    last = big.shape[1] // shard_rows - 1
    return pl.pallas_call(
        after_mlp_kernel,
        out_shape=outs,
        grid_spec=pltpu.PrefetchScalarGridSpec(
            num_scalar_prefetch=1,
            grid=(1,),
            in_specs=[whole_spec(a) for a in (mlp, dn2, x, branch, g, o)]
            + [pl.BlockSpec((owners, shard_rows, width), lambda i, *_: (0, last, 0)), whole_spec(vec)],
            out_specs=[whole_spec(a) for a in outs],
        ),
        compiler_params=pltpu.CompilerParams(vmem_limit_bytes=52 << 20),
        cost_estimate=pl.CostEstimate(flops=4 * tokens * width * width, bytes_accessed=20 << 20, transcendentals=0),
        name="after_mlp",
    )(jnp.stack(position(me)).astype(jnp.int32), mlp, dn2, x, branch, g, o, big, vec)


def add_kernel(bits, *refs, terms):
    outs = refs[terms * 2 * (len(refs) // (2 * terms + 1)) :]
    refs = refs[: terms * 2 * len(outs)]
    for n, out in enumerate(outs):
        wide, narrow = (
            [r[...].astype(F32).reshape(r.shape[-2:]) for r in refs[(2 * n + i) * terms : (2 * n + i + 1) * terms]]
            for i in range(2)
        )
        out[...] = jnp.concatenate([sum(wide), sum(narrow)], axis=1).astype(BF16).reshape(out.shape)


def added(operands, indices, grid, out_shape, out_index, me, name):
    flat, specs = [], []
    for sides, places in zip(operands, indices):
        for arrays, at in zip(sides, places):
            for (array, block), index in zip(arrays, at):
                flat.append(array)
                specs.append(pl.BlockSpec(block, index))
    terms = len(operands[0][0])
    outs = [shaped(*out_shape, dtype=BF16)] * len(operands)
    block = (1,) * (len(out_shape) - 2) + out_shape[-2:]
    return pl.pallas_call(
        functools.partial(add_kernel, terms=terms),
        out_shape=tuple(outs),
        grid_spec=pltpu.PrefetchScalarGridSpec(
            num_scalar_prefetch=1,
            grid=grid,
            in_specs=specs,
            out_specs=[pl.BlockSpec(block, out_index)] * len(outs),
        ),
        compiler_params=pltpu.CompilerParams(vmem_limit_bytes=40 << 20),
        cost_estimate=pl.CostEstimate(flops=0, bytes_accessed=16 << 20, transcendentals=0),
        name=name,
    )(jnp.stack(position(me)).astype(jnp.int32), *flat)


def first_sends(pairs, me):
    (one, two, small) = pairs
    planes, _, _, rows, width = one[0].shape
    cut = small[0].shape[-1] // 2
    wide, narrow = (1, 1, 1, rows, width), (1, 1, 1, rows, cut)

    def at_a(column):
        return lambda z, t, bits: (z, t, 1 - bits[1], 0, column)

    def at_b(column):
        return lambda z, t, bits: (z, 1 - bits[0], t, 0, column)

    operands = [
        ([(m, wide) for m in one], [(m, narrow) for m in small]),
        ([(m, wide) for m in two], [(m, narrow) for m in small]),
    ]
    indices = [([at_a(0)] * 2, [at_a(0)] * 2), ([at_b(0)] * 2, [at_b(1)] * 2)]
    shape = (planes, 2, rows, width + cut)
    return added(operands, indices, (planes, 2), shape, lambda z, t, bits: (z, t, 0, 0), me, "first_sends")


def second_sums(pairs, in_a, in_b, me):
    (one, two, small) = pairs
    planes, _, _, rows, width = one[0].shape
    cut = small[0].shape[-1] // 2
    wide, narrow = (1, 1, 1, rows, width), (1, 1, 1, rows, cut)
    wide_in, narrow_in = (1, 1, rows, width), (1, 1, rows, cut)
    operands, indices = [], []
    for sides, got, axis in ((one, in_a, 0), (two, in_b, 1)):
        for keep in (0, 1):
            def other(bits, axis=axis, keep=keep):
                return bits[axis] if keep else 1 - bits[axis]

            def at(column, axis=axis, other=other):
                if axis == 0:
                    return lambda z, bits: (z, other(bits), bits[1], 0, column)
                return lambda z, bits: (z, bits[0], other(bits), 0, column)

            def arrived(column, other=other):
                return lambda z, bits: (z, other(bits), 0, column)

            operands.append(
                ([(m, wide) for m in sides] + [(got, wide_in)], [(m, narrow) for m in small] + [(got, narrow_in)])
            )
            indices.append(
                ([at(0)] * 2 + [arrived(0)], [at(axis)] * 2 + [arrived(width // cut)])
            )
    shape = (planes, rows, width + cut)
    return added(operands, indices, (planes,), shape, lambda z, bits: (z, 0, 0), me, "second_sums")


def body(
    tokens,
    cotangent,
    image_lengths,
    ln1_gain,
    ln1_bias,
    qkv_weight,
    qv_bias,
    proj_weight,
    proj_bias,
    scale_attn,
    ln2_gain,
    ln2_bias,
    fc1_weight,
    fc1_bias,
    fc2_weight,
    fc2_bias,
    scale_mlp,
):
    devices = lax.axis_size("dev")
    me = lax.axis_index("dev")
    rows, width = tokens.shape
    vectors = (
        ln1_gain, ln1_bias, qv_bias, proj_bias, scale_attn, ln2_gain, ln2_bias, fc1_bias, fc2_bias, scale_mlp,
    )
    sizes = [v.shape[0] for v in vectors]
    shard_rows, hidden = qkv_weight.shape[0], fc1_weight.shape[1]
    by_axes = shard_rows % 32 == 0
    blocks = hidden // width
    slab = qkv_weight.reshape(shard_rows, 3, GROUP, -1).transpose(2, 0, 1, 3).reshape(GROUP, shard_rows, -1)
    packed = jnp.broadcast_to(pack_columns(vectors, shard_rows), (GROUP, shard_rows, 128))
    slab = jnp.concatenate([slab, packed], axis=2)
    slab = jnp.broadcast_to(slab[None], (devices // GROUP, *slab.shape)).reshape(devices, shard_rows, -1)
    n1, q, kv, packed = plane_qkv(tokens, slab, me, devices)
    spread = unpack_columns(packed.astype(F32), sizes, shard_rows)
    gain1, shift1, bias_qv, bias_proj, layer_attn, gain2, shift2, bias_fc1, bias_fc2, layer_mlp = spread
    if by_axes:
        first = fc1_weight.reshape(shard_rows, blocks, width).transpose(1, 0, 2).reshape(-1, width)
        big = gathered(jnp.concatenate([first, fc2_weight, proj_weight])).reshape(devices, -1, width)
        w_proj = big[:, 2 * blocks * shard_rows :].reshape(width, width)
    else:
        w_proj, big = gathered(proj_weight), gathered(fc1_weight)
        w_fc2 = gathered(fc2_weight)
    qkv_late = qkv_weight.reshape(shard_rows, 3, GROUP, -1).transpose(0, 2, 1, 3).reshape(shard_rows, -1)
    qkv_late, packed = lax.optimization_barrier((qkv_late, packed))
    w_qkv = gathered(qkv_late)

    span = GROUP * rows
    halo = -(-(SEQ - 1) // BK) * BK
    base = (me // GROUP) * span - halo
    places = base + halo + jnp.arange(span, dtype=jnp.int32)
    ends = jnp.cumsum(image_lengths)
    before = ends[None, :] <= places[:, None]
    begin = jnp.max(jnp.where(before, ends[None, :], 0), axis=1)
    finish = jnp.min(jnp.where(before, devices * rows, ends[None, :]), axis=1)
    seg = jnp.stack([begin - base, finish - base]).astype(jnp.int32)
    low = seg[0, ::BQ] // BK
    high = -(-seg[1, BQ - 1 :: BQ] // BK)

    x = tokens.astype(F32)
    u1, rstd1 = normalised(x)
    prefetch, edge_blocks = (low, high), halo // BK
    left = shifted(kv[span - halo :], GROUP, devices)
    right = shifted(kv[:halo], -GROUP, devices)
    acc, stat = forward_mid(prefetch, seg, q, kv, edge_blocks)
    acc, stat, left, right = lax.optimization_barrier((acc, stat, left, right))
    o_heads, lse = forward_edge(prefetch, seg, q, left, right, acc, stat)
    (o,) = to_tokens([o_heads], devices)

    branch = mm(o, w_proj) + bias_proj
    y1 = x + layer_attn * branch
    u2, rstd2 = normalised(y1)
    n2 = (u2 * gain2 + shift2).astype(BF16)
    g = cotangent.astype(F32)
    dm = layer_mlp * g
    d_fc2_bias = jnp.sum(dm, axis=0)
    dml = dm.astype(BF16)
    if by_axes:
        mlp, dn2, d_fc1_bias, keep1, send1, keep2, send2 = mlp_all(n2, dml, big, bias_fc1, me, shard_rows)
        d_fc1_bias = d_fc1_bias.reshape(-1)
    else:
        act, slope = gelu_parts(mm(n2, big) + bias_fc1)
        act = act.astype(BF16)
        mlp = mm(act, w_fc2)
        dz = mm_t(dml, w_fc2) * slope
        d_fc1_bias = jnp.sum(dz, axis=0)
        dz = dz.astype(BF16)
        dn2 = mm_t(dz, big)
        d_fc1, d_fc2 = scattered(t_mm(n2, dz)), scattered(t_mm(act, dml))
    if by_axes:
        vec = jnp.stack([layer_attn, gain2, layer_mlp, bias_fc2])
        block_out, dy1, totals, do, keep3, send3 = after_mlp(
            mlp, dn2, tokens, branch, cotangent, o, big, vec, me, shard_rows
        )
        d_scale_mlp, d_fc2_bias, d_gain2, d_shift2, d_scale_attn, d_proj_bias = (totals[i] for i in range(6))
        got1, got2, got3 = (swapped(s, 1, devices) for s in (send1, send2, send3))
        view = (devices // GROUP, 2, 2, shard_rows)
        halves = [
            tuple(s.reshape(*view, -1) for s in pair) for pair in ((keep1, got1), (keep2, got2), (keep3, got3))
        ]
        out_a, out_b = first_sends(halves, me)
    else:
        mlp = mlp + bias_fc2
        block_out = (y1 + layer_mlp * mlp).astype(BF16)
        d_scale_mlp = jnp.sum(g * mlp, axis=0)
        d_gain2 = jnp.sum(dn2 * u2, axis=0)
        d_shift2 = jnp.sum(dn2, axis=0)
        dy1 = g + norm_back(u2, rstd2, dn2 * gain2)
        d_scale_attn = jnp.sum(dy1 * branch, axis=0)
        db = layer_attn * dy1
        d_proj_bias = jnp.sum(db, axis=0)
        dbl = db.astype(BF16)
        d_proj = scattered(t_mm(o, dbl))
        do = mm_t(dbl, w_proj).astype(BF16).reshape(rows, GROUP, -1).transpose(1, 0, 2)

    do_heads = in_plane(do, devices).reshape(span, -1)
    if by_axes:
        in_a, in_b = swapped(out_a, 2, devices), swapped(out_b, 4, devices)
    part_dq, mid0, out_left, out_right = backward_first(prefetch, seg, q, kv, left, right, o_heads, do_heads, lse)
    if by_axes:
        part_dq, in_a, in_b, w_qkv = lax.optimization_barrier((part_dq, in_a, in_b, w_qkv))
        out_a, sum_a, out_b, sum_b = second_sums(halves, in_a, in_b, me)
        part_dq, out_a, out_b = lax.optimization_barrier((part_dq, out_a, out_b))
        in_a, in_b = swapped(out_a, 4, devices), swapped(out_b, 2, devices)
    from_right = shifted(out_left, -GROUP, devices)
    from_left = shifted(out_right, GROUP, devices)
    dq, mid = backward_second(prefetch, seg, q, kv, o_heads, do_heads, lse, part_dq, mid0, edge_blocks)
    dq, mid, from_left, from_right = lax.optimization_barrier((dq, mid, from_left, from_right))
    if by_axes:
        dq, in_a, in_b = lax.optimization_barrier((dq, in_a, in_b))
    if by_axes:
        third = [(s.astype(F32) + i.astype(F32)).astype(BF16) for s, i in ((sum_a, in_a), (sum_b, in_b))]
        own_sums, pieces = plane_pieces(jnp.concatenate(third, axis=-1), me, devices)
        dq, pieces = lax.optimization_barrier((dq, pieces))
        sums = send_planes(pieces, devices)
    d_heads = joined_heads(dq, mid, from_left, from_right)
    dqkv = in_plane(d_heads.reshape(GROUP, rows, -1), devices)
    if by_axes:
        dqkv, n1 = lax.optimization_barrier((dqkv, n1))
    d_qkv = t_mm(n1, d_heads).astype(BF16).reshape(devices // GROUP, GROUP, shard_rows, -1)
    if by_axes:
        dqkv, d_qkv, sums = lax.optimization_barrier((dqkv, d_qkv, sums))
    own_qkv, pieces = plane_pieces(d_qkv, me, devices)
    got_qkv = send_planes(pieces, devices)
    grad_tokens, totals, per_head = input_gradient(dqkv, w_qkv, dy1, tokens, gain1)
    d_gain1, d_shift1, half = totals[0], totals[1], width // GROUP
    d_qv_bias = jnp.concatenate([per_head[:, :half].reshape(-1), per_head[:, 2 * half :].reshape(-1)])
    if by_axes:
        d_gain1, got_qkv = lax.optimization_barrier((d_gain1, got_qkv))
    d_qkv = in_plane(total_of(own_qkv, got_qkv), devices).reshape(GROUP, shard_rows, 3, -1)
    d_qkv = d_qkv.transpose(1, 2, 0, 3).reshape(shard_rows, 3 * width)
    if by_axes:
        sums = total_of(own_sums, sums)
        d_fc1 = sums[:, :hidden]
        cut = width // 2
        at = hidden + cut
        d_fc2 = sums[:, at : at + hidden].reshape(shard_rows, blocks, width).transpose(1, 0, 2)
        d_fc2 = d_fc2.reshape(blocks * shard_rows, width)
        d_proj = jnp.concatenate([sums[:, hidden:at], sums[:, at + hidden :]], axis=1)
    small = (
        d_gain1, d_shift1, d_qv_bias, d_proj_bias, d_scale_attn, d_gain2, d_shift2, d_fc1_bias, d_fc2_bias, d_scale_mlp,
    )
    small = lax.all_to_all(pack(small, devices), "dev", 0, 0, tiled=True)
    small = jnp.sum(small, axis=0, keepdims=True)
    s_gain1, s_shift1, s_qv, s_proj, s_attn, s_gain2, s_shift2, s_fc1, s_fc2, s_mlp = unpack(small, sizes)
    return (
        block_out,
        grad_tokens,
        s_gain1,
        s_shift1,
        d_qkv,
        s_qv,
        d_proj,
        s_proj,
        s_attn,
        s_gain2,
        s_shift2,
        d_fc1,
        s_fc1,
        d_fc2,
        s_fc2,
        s_mlp,
    )


def solution(mesh):
    matrix, vector = P("dev", None), P("dev")
    return jax.shard_map(
        body,
        mesh=mesh,
        in_specs=(
            matrix, matrix, P(), vector, vector, matrix, vector, matrix, vector, vector, vector, vector, matrix,
            vector, matrix, vector, vector,
        ),
        out_specs=(
            matrix, matrix, vector, vector, matrix, vector, matrix, vector, vector, vector, vector, matrix, vector,
            matrix, vector, vector,
        ),
        check_vma=False,
    )
```

```python
import functools

import jax
import jax.numpy as jnp
from jax import lax
from jax.experimental import pallas as pl
from jax.experimental.pallas import tpu as pltpu
from jax.sharding import PartitionSpec as P

BQ = 256
BK = 256
SLAB = 2 * BK
HD = 64
LOG2E = 1.4426950408889634
SCALE = 0.125
MASKED = -1e30
NT = (((1,), (1,)), ((), ()))


def head_halves(block):
    first = lax.broadcasted_iota(jnp.int32, block.shape, 1) < HD
    zero = jnp.zeros_like(block)
    return jnp.where(first, block, zero), jnp.where(first, zero, block)


def transpose_into(target, source, column):
    width = target.shape[0]
    for j in range(source.shape[0] // BK):
        part = source[j * BK : (j + 1) * BK, column : column + width].astype(jnp.float32)
        target[:, j * BK : (j + 1) * BK] = part.T.astype(target.dtype)


def slabs(low, high, first, last):
    low = jnp.clip(low, first, last) - first
    count = (jnp.clip(high, first, last) - first - low + 1) // 2
    return jnp.minimum(low, last - first - 2 * count), count


def slab_rows(start, t):
    return pl.ds(pl.multiple_of((start + 2 * t) * BK, BK), SLAB)


def forward_over(span, kv_ref, v_t, offset, q_heads, seg, carry):
    start, count = span
    width = q_heads[0].shape[1]
    begin, end = seg[0:1, :], seg[1:2, :]
    place = lax.broadcasted_iota(jnp.int32, (SLAB, BQ), 0) + offset

    def one_slab(t, carry):
        rows = slab_rows(start, t)
        keys = kv_ref[rows, :width]
        at = place + (start + 2 * t) * BK
        valid = (at >= begin) & (at < end)
        out = []
        for h in range(2):
            top, total, acc = carry[h]
            s = lax.dot_general(keys, q_heads[h], NT, preferred_element_type=jnp.float32)
            s = jnp.where(valid, s * (SCALE * LOG2E), MASKED)
            new_top = jnp.maximum(top, jnp.max(s, axis=0, keepdims=True))
            p = jnp.exp2(s - new_top)
            fade = jnp.exp2(top - new_top)
            total = total * fade + jnp.sum(p, axis=0, keepdims=True)
            v_part = v_t[h * HD : (h + 1) * HD, rows]
            acc = acc * fade + jnp.dot(v_part, p.astype(jnp.bfloat16), preferred_element_type=jnp.float32)
            out.append((new_top, total, acc))
        return tuple(out)

    return lax.fori_loop(0, count, one_slab, carry)


def forward_mid_kernel(low, high, seg, q_ref, kv_ref, acc_ref, stat_ref, v_t, *, edge):
    step = pl.program_id(0)

    @pl.when(step == 0)
    def _():
        transpose_into(v_t, kv_ref, q_ref.shape[1])

    start = (
        jnp.full((1, BQ), MASKED, jnp.float32),
        jnp.zeros((1, BQ), jnp.float32),
        jnp.zeros((HD, BQ), jnp.float32),
    )
    blocks = kv_ref.shape[0] // BK
    span = slabs(low[step], high[step], edge, edge + blocks)
    done = forward_over(span, kv_ref, v_t, edge * BK, head_halves(q_ref[...]), seg, (start, start))
    for h, (top, total, acc) in enumerate(done):
        stat_ref[2 * h : 2 * h + 1, :] = top
        stat_ref[2 * h + 1 : 2 * h + 2, :] = total
        acc_ref[h * HD : (h + 1) * HD, :] = acc


def forward_edge_kernel(
    low, high, seg, q_ref, left_ref, right_ref, acc_ref, stat_ref, o_ref, lse_ref, left_t, right_t, *, last
):
    step = pl.program_id(0)
    width = q_ref.shape[1]
    edge = left_ref.shape[0] // BK

    @pl.when(step == 0)
    def _():
        transpose_into(left_t, left_ref, width)
        transpose_into(right_t, right_ref, width)

    carry = tuple(
        (stat_ref[2 * h : 2 * h + 1, :], stat_ref[2 * h + 1 : 2 * h + 2, :], acc_ref[h * HD : (h + 1) * HD, :])
        for h in range(2)
    )
    q_heads = head_halves(q_ref[...])
    span = slabs(low[step], high[step], 0, edge)
    carry = forward_over(span, left_ref, left_t, 0, q_heads, seg, carry)
    span = slabs(low[step], high[step], last, last + edge)
    carry = forward_over(span, right_ref, right_t, last * BK, q_heads, seg, carry)
    o_ref[...] = jnp.concatenate([acc / total for _, total, acc in carry], axis=0).T.astype(o_ref.dtype)
    for h, (top, total, _) in enumerate(carry):
        lse_ref[h : h + 1, :] = top + jnp.log2(total)


def backward_setup(q_ref, do_ref, o_ref, lse_ref, heads):
    prod = (do_ref[...].astype(jnp.float32) * o_ref[...].astype(jnp.float32)).T
    q_heads, do_heads = head_halves(q_ref[...]), head_halves(do_ref[...])
    return [
        (
            h,
            q_heads[h],
            do_heads[h],
            jnp.sum(prod[h * HD : (h + 1) * HD], axis=0, keepdims=True),
            lse_ref[h : h + 1, :],
        )
        for h in heads
    ]


def backward_over(span, kv_ref, k_t, dkv, dq_t, offset, heads, seg):
    start, count = span
    width = dq_t.shape[0]
    begin, end = seg[0:1, :], seg[1:2, :]
    place = lax.broadcasted_iota(jnp.int32, (SLAB, BQ), 0) + offset
    q_all = jnp.concatenate([q for _, q, _, _, _ in heads], axis=0)
    do_all = jnp.concatenate([d for _, _, d, _, _ in heads], axis=0)

    @pl.loop(0, count)
    def _(t):
        rows = slab_rows(start, t)
        keys, values = kv_ref[rows, :width], kv_ref[rows, width:]
        at = place + (start + 2 * t) * BK
        valid = (at >= begin) & (at < end)
        ps, dss = [], []
        for h, q, do, centre, lse in heads:
            s = lax.dot_general(keys, q, NT, preferred_element_type=jnp.float32)
            p = jnp.where(valid, jnp.exp2(s * (SCALE * LOG2E) - lse), 0.0)
            dp = lax.dot_general(values, do, NT, preferred_element_type=jnp.float32)
            ds = (p * (dp - centre)).astype(jnp.bfloat16)
            ps.append(p.astype(jnp.bfloat16))
            dss.append(ds)
            part = slice(h * HD, (h + 1) * HD)
            dq_t[part, :] += jnp.dot(k_t[part, rows], ds, preferred_element_type=jnp.float32)
        dkv[rows, :width] += jnp.dot(jnp.concatenate(dss, axis=1), q_all, preferred_element_type=jnp.float32)
        dkv[rows, width:] += jnp.dot(jnp.concatenate(ps, axis=1), do_all, preferred_element_type=jnp.float32)


def backward_first_kernel(
    low, high, seg, q_ref, kv_ref, left_ref, right_ref, o_ref, do_ref, lse_ref, dq_t, mid_ref, out_left, out_right,
    left_t, right_t, k_t, dkv, *, last
):
    step = pl.program_id(0)
    width = q_ref.shape[1]
    edge = left_ref.shape[0] // BK

    @pl.when(step == 0)
    def _():
        transpose_into(left_t, left_ref, 0)
        transpose_into(right_t, right_ref, 0)
        transpose_into(k_t, kv_ref, 0)
        dkv[...] = jnp.zeros_like(dkv)
        mid_ref[...] = jnp.zeros_like(mid_ref)

    heads = backward_setup(q_ref, do_ref, o_ref, lse_ref, range(2))
    dq_t[...] = jnp.zeros_like(dq_t)
    span = slabs(low[step], high[step], 0, edge)
    backward_over(span, left_ref, left_t, dkv.at[0], dq_t, 0, heads, seg)
    span = slabs(low[step], high[step], last, last + edge)
    backward_over(span, right_ref, right_t, dkv.at[1], dq_t, last * BK, heads, seg)
    span = slabs(low[step], high[step], edge, last)
    backward_over(span, kv_ref, k_t, mid_ref, dq_t, edge * BK, heads[:1], seg)

    @pl.when(step == pl.num_programs(0) - 1)
    def _():
        for side, out in enumerate((out_left, out_right)):
            out[:, :width] = (dkv[side, :, :width] * SCALE).astype(out.dtype)
            out[:, width:] = dkv[side, :, width:].astype(out.dtype)


def backward_mid_kernel(
    low, high, seg, q_ref, kv_ref, o_ref, do_ref, lse_ref, part_ref, first_ref, dq_ref, mid_ref, k_t, dq_t, *, edge
):
    step = pl.program_id(0)
    width = q_ref.shape[1]

    @pl.when(step == 0)
    def _():
        transpose_into(k_t, kv_ref, 0)
        mid_ref[...] = first_ref[...]

    dq_t[...] = part_ref[...]
    blocks = kv_ref.shape[0] // BK
    span = slabs(low[step], high[step], edge, edge + blocks)
    heads = backward_setup(q_ref, do_ref, o_ref, lse_ref, [1])
    backward_over(span, kv_ref, k_t, mid_ref, dq_t, edge * BK, heads, seg)
    dq_ref[...] = (dq_t[...] * SCALE).T.astype(dq_ref.dtype)

    @pl.when(step == pl.num_programs(0) - 1)
    def _():
        mid_ref[:, :width] = mid_ref[:, :width] * SCALE


def whole_spec(array):
    return pl.BlockSpec(array.shape, lambda i, *_: (0,) * len(array.shape))


def attention_call(kernel, name, prefetch, inputs, in_kinds, outputs, out_kinds, scratch, work):
    span = prefetch[0].shape[0] * BQ

    def spec(array, kind):
        if kind == "r":
            return pl.BlockSpec((BQ, array.shape[1]), lambda i, *_: (i, 0))
        if kind == "c":
            return pl.BlockSpec((array.shape[0], BQ), lambda i, *_: (0, i))
        return whole_spec(array)

    return pl.pallas_call(
        kernel,
        out_shape=tuple(outputs),
        grid_spec=pltpu.PrefetchScalarGridSpec(
            num_scalar_prefetch=2,
            grid=(span // BQ,),
            in_specs=[spec(a, k) for a, k in zip(inputs, in_kinds)],
            out_specs=[spec(a, k) for a, k in zip(outputs, out_kinds)],
            scratch_shapes=scratch,
        ),
        compiler_params=pltpu.CompilerParams(vmem_limit_bytes=48 << 20),
        cost_estimate=pl.CostEstimate(flops=work << 30, bytes_accessed=8 << 20, transcendentals=span * 128),
        name=name,
    )(*prefetch, *inputs)


def shaped(*shape, dtype=jnp.float32):
    return jax.ShapeDtypeStruct(shape, dtype)


def forward_mid(prefetch, seg, q, kv, edge):
    span, width = q.shape
    return attention_call(
        functools.partial(forward_mid_kernel, edge=edge), "forward_mid", prefetch, [seg, q, kv], "crw",
        [shaped(width, span), shaped(8, span)], "cc", [pltpu.VMEM((width, span), jnp.bfloat16)], 3,
    )


def forward_edge(prefetch, seg, q, left, right, acc, stat):
    span, width = q.shape
    halo = pltpu.VMEM((width, left.shape[0]), jnp.bfloat16)
    return attention_call(
        functools.partial(forward_edge_kernel, last=(left.shape[0] + span) // BK), "forward_edge", prefetch,
        [seg, q, left, right, acc, stat], "crwwcc",
        [shaped(span, width, dtype=jnp.bfloat16), shaped(8, span)], "rc", [halo, halo], 3,
    )


def backward_first(prefetch, seg, q, kv, left, right, o, do, lse):
    span, width = q.shape
    halo = pltpu.VMEM((width, left.shape[0]), jnp.bfloat16)
    return attention_call(
        functools.partial(backward_first_kernel, last=(left.shape[0] + span) // BK), "backward_first", prefetch,
        [seg, q, kv, left, right, o, do, lse], "crwwwrrc",
        [shaped(width, span), shaped(*kv.shape)] + [shaped(*left.shape, dtype=jnp.bfloat16)] * 2, "cwww",
        [halo, halo, pltpu.VMEM((width, span), jnp.bfloat16), pltpu.VMEM((2, *left.shape), jnp.float32)], 3,
    )


def backward_second(prefetch, seg, q, kv, o, do, lse, part, first, edge):
    span, width = q.shape
    return attention_call(
        functools.partial(backward_mid_kernel, edge=edge), "backward_second", prefetch,
        [seg, q, kv, o, do, lse, part, first], "crwrrccw",
        [shaped(span, width, dtype=jnp.bfloat16), shaped(*kv.shape)], "rw",
        [pltpu.VMEM((width, span), jnp.bfloat16), pltpu.VMEM((width, BQ), jnp.float32)], 3,
    )


HEADS = 16
SEQ = 1370
GROUP = 8
EPS = 1e-06
F32, BF16 = jnp.float32, jnp.bfloat16


def mm(left, right):
    return jnp.dot(left, right, preferred_element_type=F32)


def mm_t(left, right):
    return jnp.einsum("tf,df->td", left, right, preferred_element_type=F32)


def t_mm(left, right):
    return jnp.einsum("td,tf->df", left, right, preferred_element_type=F32)


def normalised(value):
    centre = value - jnp.mean(value, axis=-1, keepdims=True)
    rstd = lax.rsqrt(jnp.mean(centre * centre, axis=-1, keepdims=True) + EPS)
    return centre * rstd, rstd


def norm_back(unit, rstd, grad):
    first = jnp.mean(grad, axis=-1, keepdims=True)
    second = jnp.mean(grad * unit, axis=-1, keepdims=True)
    return rstd * (grad - first - unit * second)


def gelu_parts(z):
    half = 0.5 * (1.0 + lax.erf(z * 0.7071067811865476))
    slope = half + z * (0.3989422804014327 * jnp.exp(-0.5 * z * z))
    return z * half, slope


def groups_of(count):
    return [list(range(first, first + GROUP)) for first in range(0, count, GROUP)]


def gathered(shard):
    return lax.all_gather(shard, "dev", axis=0, tiled=True)


def scattered(whole):
    return lax.psum_scatter(whole, "dev", scatter_dimension=0, tiled=True)


def pack(vectors, count):
    return jnp.concatenate([v.reshape(count, -1) for v in vectors], axis=1)


def unpack(packed, sizes):
    out, at = [], 0
    for size in sizes:
        out.append(packed[:, at : at + size].reshape(-1))
        at += size
    return out


def to_heads(parts, devices):
    rows = parts[0].shape[0]
    sent = jnp.stack([p.reshape(rows, GROUP, -1) for p in parts], axis=2)
    sent = sent.transpose(1, 0, 2, 3)
    back = lax.all_to_all(sent, "dev", 0, 0, axis_index_groups=groups_of(devices), tiled=True)
    return [back[:, :, i].reshape(GROUP * rows, -1) for i in range(len(parts))]


def to_tokens(parts, devices):
    rows = parts[0].shape[0] // GROUP
    sent = jnp.stack([p.reshape(GROUP, rows, -1) for p in parts], axis=2)
    back = lax.all_to_all(sent, "dev", 0, 0, axis_index_groups=groups_of(devices), tiled=True)
    return [back[:, :, i].transpose(1, 0, 2).reshape(rows, -1) for i in range(len(parts))]


def shifted(shard, by, devices):
    pairs = [(i, i + by) for i in range(devices) if 0 <= i + by < devices]
    return lax.ppermute(shard, "dev", pairs)


def take(stack, index, axis):
    return lax.dynamic_index_in_dim(stack, index, axis, keepdims=False)


def swapped(value, bit, devices):
    return lax.ppermute(value, "dev", [(i, i ^ bit) for i in range(devices)])


def join_kernel(dq, mid, left, right, out):
    width = dq.shape[1]
    step, edge = pl.program_id(0), pl.num_programs(0) // 2
    halo = jnp.where(step < edge, left[...], right[...]).astype(F32)
    out[:, :width] = dq[...]
    out[:, width:] = (mid[...] + halo).astype(out.dtype)


def joined_heads(dq, mid, left, right):
    span, width = dq.shape
    size = 3 * BQ
    half = span // (2 * size)
    rows = [pl.BlockSpec((size, columns), lambda i: (i, 0)) for columns in (width, 2 * width, 3 * width)]
    return pl.pallas_call(
        join_kernel,
        out_shape=shaped(span, 3 * width, dtype=BF16),
        grid=(span // size,),
        in_specs=rows[:2]
        + [
            pl.BlockSpec((size, 2 * width), lambda i: (jnp.minimum(i, half - 1), 0)),
            pl.BlockSpec((size, 2 * width), lambda i: (jnp.maximum(i - half, 0), 0)),
        ],
        out_specs=rows[2],
        cost_estimate=pl.CostEstimate(flops=0, bytes_accessed=10 << 20, transcendentals=0),
        name="joined_heads",
    )(dq, mid, left, right)


def tail_kernel(dqkv, weight, dy1, x_ref, gain, grad, sums, heads):
    size = dqkv.shape[2]
    dn1 = jnp.zeros(dy1.shape, F32)
    for j in range(dqkv.shape[0]):
        dn1 += lax.dot_general(
            dqkv[j], weight[:, j * size : (j + 1) * size], NT, preferred_element_type=F32
        )
        heads[j : j + 1, :] = jnp.sum(dqkv[j].astype(F32), axis=0, keepdims=True)
    unit, rstd = normalised(x_ref[...].astype(F32))
    grad[...] = (dy1[...] + norm_back(unit, rstd, dn1 * gain[...])).astype(grad.dtype)
    sums[0:1, :] = jnp.sum(dn1 * unit, axis=0, keepdims=True)
    sums[1:2, :] = jnp.sum(dn1, axis=0, keepdims=True)


def input_gradient(dqkv, weight, dy1, tokens, gain):
    inputs = (dqkv, weight, dy1, tokens, gain[None])
    outs = (shaped(*tokens.shape, dtype=BF16), shaped(8, tokens.shape[1]), shaped(GROUP, dqkv.shape[2]))
    return pl.pallas_call(
        tail_kernel,
        out_shape=outs,
        grid=(1,),
        in_specs=[whole_spec(a) for a in inputs],
        out_specs=[whole_spec(a) for a in outs],
        compiler_params=pltpu.CompilerParams(vmem_limit_bytes=44 << 20),
        cost_estimate=pl.CostEstimate(flops=2 * weight.size * tokens.shape[0], bytes_accessed=12 << 20, transcendentals=0),
        name="input_gradient",
    )(*inputs)


def in_plane(stack, devices):
    return lax.all_to_all(stack, "dev", 0, 0, axis_index_groups=groups_of(devices), tiled=True)


def position(me):
    return (me // 4) % 2, (me // 2) % 2, me % 2


def qkv_kernel(bits, near_a, far_a, near_b, far_b, slab, n1_ref, q_ref, kv_ref, lines, bias, *, rows):
    step = pl.program_id(0)
    third = q_ref.shape[1]
    width = slab.shape[0]

    @pl.when(step == 0)
    def _():
        lines[...] = slab[:, 3 * third :].astype(F32).T
        group = bits[3]
        unit = lax.broadcasted_iota(jnp.int32, (width, third), 0)
        place = lax.broadcasted_iota(jnp.int32, (width, third), 1)
        some = lines[0:16, :].astype(BF16)
        bias[...] = jnp.zeros_like(bias)
        for part, first in ((0, 0), (2, width // 2)):
            total = jnp.zeros((1, third), F32)
            for column in range(2):
                at = first + group * (third // 2) + (place // (2 * rows)) * rows + place % rows
                chosen = (unit == at) & ((place // rows) % 2 == column)
                total = total + mm(some, jnp.where(chosen, 1.0, 0.0).astype(BF16))[2 + column : 3 + column]
            bias[0:1, part * third : (part + 1) * third] = total

    far = step >= 4
    left = jnp.where(far, far_a[0, 0], near_a[0, 0])
    right = jnp.where(far, far_b[0, 0], near_b[0, 0])
    unit, _ = normalised(jnp.concatenate([left, right], axis=1).astype(F32))
    n1 = (unit * lines[0:1, :] + lines[1:2, :]).astype(BF16)
    n1_ref[...] = n1
    out = (mm(n1, slab[:, : 3 * third]) + bias[0:1, :]).astype(BF16)
    q_ref[...] = out[:, :third]
    kv_ref[...] = out[:, third:]


def plane_qkv(tokens, slab, me, devices):
    rows, width = tokens.shape
    half, third = width // 2, (slab.shape[2] - 128) // 3
    a, b = tokens[:, :half], tokens[:, half:]
    got_a, got_b, slab = lax.optimization_barrier((swapped(a, 4, devices), swapped(b, 2, devices), slab))
    slab = lax.all_to_all(slab, "dev", 0, 0, tiled=True).reshape(width, -1)
    packed = slab[:, -128:]
    a, b = jnp.stack([a, got_a]), jnp.stack([b, got_b])
    a = jnp.stack([a, swapped(a, 2, devices)])
    b = jnp.stack([b, swapped(b, 4, devices)])
    a, b, slab = lax.optimization_barrier((a, b, slab))
    far_a, far_b = swapped(a, 1, devices), swapped(b, 1, devices)

    def near_at(s, swap):
        i, j = (s // 2) % 2, s % 2
        i, j = jnp.where(s < 4, i, 1), jnp.where(s < 4, j, 1)
        return (j, i, 0, 0) if swap else (i, j, 0, 0)

    def far_at(s, swap):
        i, j = (s // 2) % 2, s % 2
        i, j = jnp.where(s < 4, 0, i), jnp.where(s < 4, 0, j)
        return (j, i, 0, 0) if swap else (i, j, 0, 0)

    def place(s, bits):
        return ((bits[0] ^ (s % 2)) * 4 + (bits[1] ^ ((s // 2) % 2)) * 2 + (bits[2] ^ (s // 4)), 0)

    piece = (1, 1, rows, half)
    span = GROUP * rows
    out = pl.pallas_call(
        functools.partial(qkv_kernel, rows=width // devices),
        out_shape=(
            jax.ShapeDtypeStruct((span, width), BF16),
            jax.ShapeDtypeStruct((span, third), BF16),
            jax.ShapeDtypeStruct((span, 2 * third), BF16),
        ),
        grid_spec=pltpu.PrefetchScalarGridSpec(
            num_scalar_prefetch=1,
            grid=(GROUP,),
            in_specs=[
                pl.BlockSpec(piece, lambda s, bits: near_at(s, False)),
                pl.BlockSpec(piece, lambda s, bits: far_at(s, False)),
                pl.BlockSpec(piece, lambda s, bits: near_at(s, True)),
                pl.BlockSpec(piece, lambda s, bits: far_at(s, True)),
                pl.BlockSpec(slab.shape, lambda s, bits: (0, 0)),
            ],
            out_specs=[pl.BlockSpec((rows, columns), place) for columns in (width, third, 2 * third)],
            scratch_shapes=[pltpu.VMEM((128, width), F32), pltpu.VMEM((8, 3 * third), F32)],
        ),
        compiler_params=pltpu.CompilerParams(vmem_limit_bytes=40 << 20),
        cost_estimate=pl.CostEstimate(flops=5 << 30, bytes_accessed=16 << 20, transcendentals=0),
        name="plane_qkv",
    )(
        jnp.stack([*position(me), me % GROUP]).astype(jnp.int32), a, far_a, b, far_b, slab,
    )
    return (*out, packed)


def plane_pieces(stack, me, devices):
    planes, mine = devices // GROUP, me // GROUP
    return take(stack, mine, 0), [take(stack, (mine + k) % planes, 0) for k in range(1, planes)]


def send_planes(pieces, devices):
    return [
        lax.ppermute(piece, "dev", [(i, (i + (k + 1) * GROUP) % devices) for i in range(devices)])
        for k, piece in enumerate(pieces)
    ]


def total_of(own, others):
    total = own.astype(F32)
    for other in others:
        total = total + other.astype(F32)
    return total


def pack_columns(vectors, rows):
    columns = jnp.concatenate([v.reshape(-1, rows).T for v in vectors], axis=1)
    return jnp.pad(columns, ((0, 0), (0, 128 - columns.shape[1])))


def unpack_columns(packed, sizes, rows):
    lines, out, at = packed[:, :16].T, [], 0
    for size in sizes:
        count = size // rows
        part = lines[at : at + count].reshape(count, -1, rows)
        out.append(part.transpose(1, 0, 2).reshape(-1))
        at += count
    return out


def by_parity(transposed, parity, rows):
    blocks = transposed.reshape(-1, 2, rows, transposed.shape[1])
    even, odd = (blocks[:, s].reshape(-1, transposed.shape[1]) for s in range(2))
    return jnp.where(parity == 0, even, odd), jnp.where(parity == 0, odd, even)


def turned(value):
    return value.astype(F32).T.astype(BF16)


def mlp_kernel(
    bits, n2_ref, dml_ref, f1_ref, f2_ref, bias, mlp_ref, dn2_ref, db_ref, keep1, send1, keep2, send2, n2_t
):
    step = pl.program_id(0)
    rows = keep1.shape[1]

    @pl.when(step == 0)
    def _():
        mlp_ref[...] = jnp.zeros_like(mlp_ref)
        dn2_ref[...] = jnp.zeros_like(dn2_ref)
        n2_t[0], n2_t[1] = by_parity(turned(n2_ref[...]), bits[2], rows)

    n2, dml = n2_ref[...], dml_ref[...]
    f1 = f1_ref[...].reshape(n2.shape[1], -1)
    f2 = f2_ref[...].reshape(-1, n2.shape[1])
    act, slope = gelu_parts(mm(n2, f1) + bias[...])
    act = act.astype(BF16)
    mlp_ref[...] += mm(act, f2)
    dz = lax.dot_general(dml, f2, NT, preferred_element_type=F32) * slope
    db_ref[...] = jnp.sum(dz, axis=0, keepdims=True)
    dz = dz.astype(BF16)
    dn2_ref[...] += lax.dot_general(dz, f1, NT, preferred_element_type=F32)
    for side, out in enumerate((keep1, send1)):
        out[...] = mm(n2_t[side], dz).astype(BF16).reshape(out.shape)
    width = n2.shape[1]
    parts = keep2.shape[2] // width
    for part, out in zip(by_parity(turned(act), bits[2], parts * rows), (keep2, send2)):
        grad = mm(part, dml).astype(BF16).reshape(out.shape[0], parts, rows, width)
        for i in range(parts):
            out[:, :, i * width : (i + 1) * width] = grad[:, i]


def mlp_all(n2, dml, big, bias, me, shard_rows):
    tokens, width = n2.shape
    hidden, owners = bias.shape[0], width // shard_rows
    size = width // 2
    steps = hidden // size
    whole = pl.BlockSpec((tokens, width), lambda s, bits: (0, 0))
    first = pl.BlockSpec((owners // 2, shard_rows, size), lambda s, bits: (0, 0, s))
    second = pl.BlockSpec((owners // (2 * steps), shard_rows, hidden), lambda s, bits: (s, 0, 0))
    line = pl.BlockSpec((1, size), lambda s, bits: (0, s))
    grads = jax.ShapeDtypeStruct((owners // 2, shard_rows, hidden), BF16)
    total = jax.ShapeDtypeStruct((tokens, width), F32)
    return pl.pallas_call(
        mlp_kernel,
        out_shape=(total, total, jax.ShapeDtypeStruct((1, hidden), F32), grads, grads, grads, grads),
        grid_spec=pltpu.PrefetchScalarGridSpec(
            num_scalar_prefetch=1,
            grid=(steps,),
            in_specs=[
                whole,
                whole,
                pl.BlockSpec((owners, shard_rows, size), lambda s, bits: (0, s // 2, s % 2)),
                pl.BlockSpec((owners // steps, hidden // owners, width), lambda s, bits: (s, 1, 0)),
                line,
            ],
            out_specs=[whole, whole, line, first, first, second, second],
            scratch_shapes=[pltpu.VMEM((2, width // 2, tokens), BF16)],
        ),
        compiler_params=pltpu.CompilerParams(vmem_limit_bytes=52 << 20),
        cost_estimate=pl.CostEstimate(
            flops=4 * tokens * width * hidden, bytes_accessed=8 * width * hidden, transcendentals=2 * tokens * hidden
        ),
        name="mlp_all",
    )(jnp.stack(position(me)).astype(jnp.int32), n2, dml, big, big, bias[None])


def grad_kernel(bits, a_ref, b_ref, keep_ref, send_ref):
    for part, out in zip(by_parity(turned(a_ref[...]), bits[2], keep_ref.shape[1]), (keep_ref, send_ref)):
        out[...] = mm(part, b_ref[...]).astype(BF16).reshape(out.shape)


def weight_grad(a, b, rows, me):
    out = jax.ShapeDtypeStruct((a.shape[1] // (2 * rows), rows, b.shape[1]), BF16)
    return pl.pallas_call(
        grad_kernel,
        out_shape=(out, out),
        grid_spec=pltpu.PrefetchScalarGridSpec(num_scalar_prefetch=1, grid=(1,)),
        compiler_params=pltpu.CompilerParams(vmem_limit_bytes=40 << 20),
        cost_estimate=pl.CostEstimate(
            flops=2 * a.size * b.shape[1], bytes_accessed=2 * (a.size + b.size + 2 * out.size), transcendentals=0
        ),
        name="weight_grad",
    )(jnp.stack(position(me)).astype(jnp.int32), a, b)


def after_mlp_kernel(
    bits, mlp, dn2, x_ref, branch, g_ref, o_ref, w_proj, vec, block_out, dy1_ref, sums, do_ref, keep, send
):
    layer_attn, gain2, layer_mlp, bias = (vec[i : i + 1, :] for i in range(4))
    g, out = g_ref[...].astype(F32), mlp[...] + bias
    y1 = x_ref[...].astype(F32) + layer_attn * branch[...]
    unit, rstd = normalised(y1)
    block_out[...] = (y1 + layer_mlp * out).astype(BF16)
    dy1 = g + norm_back(unit, rstd, dn2[...] * gain2)
    dy1_ref[...] = dy1
    db = layer_attn * dy1
    totals = (g * out, layer_mlp * g, dn2[...] * unit, dn2[...], dy1 * branch[...], db)
    for i, total in enumerate(totals):
        sums[i : i + 1, :] = jnp.sum(total, axis=0, keepdims=True)
    dbl = db.astype(BF16)
    weight = w_proj[...].reshape(dbl.shape[1], -1)
    do = lax.dot_general(dbl, weight, NT, preferred_element_type=F32).astype(BF16)
    columns = do_ref.shape[2]
    for j in range(do_ref.shape[0]):
        do_ref[j] = do[:, j * columns : (j + 1) * columns]
    for part, to in zip(by_parity(turned(o_ref[...]), bits[2], keep.shape[1]), (keep, send)):
        to[...] = mm(part, dbl).astype(BF16).reshape(to.shape)


def after_mlp(mlp, dn2, x, branch, g, o, big, vec, me, shard_rows):
    tokens, width = mlp.shape
    owners = width // shard_rows
    grads = shaped(owners // 2, shard_rows, width, dtype=BF16)
    outs = (
        shaped(tokens, width, dtype=BF16), shaped(tokens, width), shaped(8, width),
        shaped(GROUP, tokens, width // GROUP, dtype=BF16), grads, grads,
    )
    last = big.shape[1] // shard_rows - 1
    return pl.pallas_call(
        after_mlp_kernel,
        out_shape=outs,
        grid_spec=pltpu.PrefetchScalarGridSpec(
            num_scalar_prefetch=1,
            grid=(1,),
            in_specs=[whole_spec(a) for a in (mlp, dn2, x, branch, g, o)]
            + [pl.BlockSpec((owners, shard_rows, width), lambda i, *_: (0, last, 0)), whole_spec(vec)],
            out_specs=[whole_spec(a) for a in outs],
        ),
        compiler_params=pltpu.CompilerParams(vmem_limit_bytes=52 << 20),
        cost_estimate=pl.CostEstimate(flops=4 * tokens * width * width, bytes_accessed=20 << 20, transcendentals=0),
        name="after_mlp",
    )(jnp.stack(position(me)).astype(jnp.int32), mlp, dn2, x, branch, g, o, big, vec)


def add_kernel(bits, *refs, terms):
    outs = refs[terms * 2 * (len(refs) // (2 * terms + 1)) :]
    refs = refs[: terms * 2 * len(outs)]
    for n, out in enumerate(outs):
        wide, narrow = (
            [r[...].astype(F32).reshape(r.shape[-2:]) for r in refs[(2 * n + i) * terms : (2 * n + i + 1) * terms]]
            for i in range(2)
        )
        out[...] = jnp.concatenate([sum(wide), sum(narrow)], axis=1).astype(BF16).reshape(out.shape)


def added(operands, indices, grid, out_shape, out_index, me, name):
    flat, specs = [], []
    for sides, places in zip(operands, indices):
        for arrays, at in zip(sides, places):
            for (array, block), index in zip(arrays, at):
                flat.append(array)
                specs.append(pl.BlockSpec(block, index))
    terms = len(operands[0][0])
    outs = [shaped(*out_shape, dtype=BF16)] * len(operands)
    block = (1,) * (len(out_shape) - 2) + out_shape[-2:]
    return pl.pallas_call(
        functools.partial(add_kernel, terms=terms),
        out_shape=tuple(outs),
        grid_spec=pltpu.PrefetchScalarGridSpec(
            num_scalar_prefetch=1,
            grid=grid,
            in_specs=specs,
            out_specs=[pl.BlockSpec(block, out_index)] * len(outs),
        ),
        compiler_params=pltpu.CompilerParams(vmem_limit_bytes=40 << 20),
        cost_estimate=pl.CostEstimate(flops=0, bytes_accessed=16 << 20, transcendentals=0),
        name=name,
    )(jnp.stack(position(me)).astype(jnp.int32), *flat)


def first_sends(pairs, me):
    (one, two, small) = pairs
    planes, _, _, rows, width = one[0].shape
    cut = small[0].shape[-1] // 2
    wide, narrow = (1, 1, 1, rows, width), (1, 1, 1, rows, cut)

    def at_a(column):
        return lambda z, t, bits: (z, t, 1 - bits[1], 0, column)

    def at_b(column):
        return lambda z, t, bits: (z, 1 - bits[0], t, 0, column)

    operands = [
        ([(m, wide) for m in one], [(m, narrow) for m in small]),
        ([(m, wide) for m in two], [(m, narrow) for m in small]),
    ]
    indices = [([at_a(0)] * 2, [at_a(0)] * 2), ([at_b(0)] * 2, [at_b(1)] * 2)]
    shape = (planes, 2, rows, width + cut)
    return added(operands, indices, (planes, 2), shape, lambda z, t, bits: (z, t, 0, 0), me, "first_sends")


def second_sums(pairs, in_a, in_b, me):
    (one, two, small) = pairs
    planes, _, _, rows, width = one[0].shape
    cut = small[0].shape[-1] // 2
    wide, narrow = (1, 1, 1, rows, width), (1, 1, 1, rows, cut)
    wide_in, narrow_in = (1, 1, rows, width), (1, 1, rows, cut)
    operands, indices = [], []
    for sides, got, axis in ((one, in_a, 0), (two, in_b, 1)):
        for keep in (0, 1):
            def other(bits, axis=axis, keep=keep):
                return bits[axis] if keep else 1 - bits[axis]

            def at(column, axis=axis, other=other):
                if axis == 0:
                    return lambda z, bits: (z, other(bits), bits[1], 0, column)
                return lambda z, bits: (z, bits[0], other(bits), 0, column)

            def arrived(column, other=other):
                return lambda z, bits: (z, other(bits), 0, column)

            operands.append(
                ([(m, wide) for m in sides] + [(got, wide_in)], [(m, narrow) for m in small] + [(got, narrow_in)])
            )
            indices.append(
                ([at(0)] * 2 + [arrived(0)], [at(axis)] * 2 + [arrived(width // cut)])
            )
    shape = (planes, rows, width + cut)
    return added(operands, indices, (planes,), shape, lambda z, bits: (z, 0, 0), me, "second_sums")


def body(
    tokens,
    cotangent,
    image_lengths,
    ln1_gain,
    ln1_bias,
    qkv_weight,
    qv_bias,
    proj_weight,
    proj_bias,
    scale_attn,
    ln2_gain,
    ln2_bias,
    fc1_weight,
    fc1_bias,
    fc2_weight,
    fc2_bias,
    scale_mlp,
):
    devices = lax.axis_size("dev")
    me = lax.axis_index("dev")
    rows, width = tokens.shape
    vectors = (
        ln1_gain, ln1_bias, qv_bias, proj_bias, scale_attn, ln2_gain, ln2_bias, fc1_bias, fc2_bias, scale_mlp,
    )
    sizes = [v.shape[0] for v in vectors]
    shard_rows, hidden = qkv_weight.shape[0], fc1_weight.shape[1]
    by_axes = shard_rows % 32 == 0
    blocks = hidden // width
    slab = qkv_weight.reshape(shard_rows, 3, GROUP, -1).transpose(2, 0, 1, 3).reshape(GROUP, shard_rows, -1)
    packed = jnp.broadcast_to(pack_columns(vectors, shard_rows), (GROUP, shard_rows, 128))
    slab = jnp.concatenate([slab, packed], axis=2)
    slab = jnp.broadcast_to(slab[None], (devices // GROUP, *slab.shape)).reshape(devices, shard_rows, -1)
    n1, q, kv, packed = plane_qkv(tokens, slab, me, devices)
    spread = unpack_columns(packed.astype(F32), sizes, shard_rows)
    gain1, shift1, bias_qv, bias_proj, layer_attn, gain2, shift2, bias_fc1, bias_fc2, layer_mlp = spread
    if by_axes:
        first = fc1_weight.reshape(shard_rows, blocks, width).transpose(1, 0, 2).reshape(-1, width)
        big = gathered(jnp.concatenate([first, fc2_weight, proj_weight])).reshape(devices, -1, width)
        w_proj = big[:, 2 * blocks * shard_rows :].reshape(width, width)
    else:
        w_proj, big = gathered(proj_weight), gathered(fc1_weight)
        w_fc2 = gathered(fc2_weight)
    qkv_late = qkv_weight.reshape(shard_rows, 3, GROUP, -1).transpose(0, 2, 1, 3).reshape(shard_rows, -1)
    qkv_late, packed = lax.optimization_barrier((qkv_late, packed))
    w_qkv = gathered(qkv_late)

    span = GROUP * rows
    halo = -(-(SEQ - 1) // BK) * BK
    base = (me // GROUP) * span - halo
    places = base + halo + jnp.arange(span, dtype=jnp.int32)
    ends = jnp.cumsum(image_lengths)
    before = ends[None, :] <= places[:, None]
    begin = jnp.max(jnp.where(before, ends[None, :], 0), axis=1)
    finish = jnp.min(jnp.where(before, devices * rows, ends[None, :]), axis=1)
    seg = jnp.stack([begin - base, finish - base]).astype(jnp.int32)
    low = seg[0, ::BQ] // BK
    high = -(-seg[1, BQ - 1 :: BQ] // BK)

    x = tokens.astype(F32)
    u1, rstd1 = normalised(x)
    prefetch, edge_blocks = (low, high), halo // BK
    left = shifted(kv[span - halo :], GROUP, devices)
    right = shifted(kv[:halo], -GROUP, devices)
    acc, stat = forward_mid(prefetch, seg, q, kv, edge_blocks)
    acc, stat, left, right = lax.optimization_barrier((acc, stat, left, right))
    o_heads, lse = forward_edge(prefetch, seg, q, left, right, acc, stat)
    (o,) = to_tokens([o_heads], devices)

    branch = mm(o, w_proj) + bias_proj
    y1 = x + layer_attn * branch
    u2, rstd2 = normalised(y1)
    n2 = (u2 * gain2 + shift2).astype(BF16)
    g = cotangent.astype(F32)
    dm = layer_mlp * g
    d_fc2_bias = jnp.sum(dm, axis=0)
    dml = dm.astype(BF16)
    if by_axes:
        mlp, dn2, d_fc1_bias, keep1, send1, keep2, send2 = mlp_all(n2, dml, big, bias_fc1, me, shard_rows)
        d_fc1_bias = d_fc1_bias.reshape(-1)
    else:
        act, slope = gelu_parts(mm(n2, big) + bias_fc1)
        act = act.astype(BF16)
        mlp = mm(act, w_fc2)
        dz = mm_t(dml, w_fc2) * slope
        d_fc1_bias = jnp.sum(dz, axis=0)
        dz = dz.astype(BF16)
        dn2 = mm_t(dz, big)
        d_fc1, d_fc2 = scattered(t_mm(n2, dz)), scattered(t_mm(act, dml))
    if by_axes:
        vec = jnp.stack([layer_attn, gain2, layer_mlp, bias_fc2])
        block_out, dy1, totals, do, keep3, send3 = after_mlp(
            mlp, dn2, tokens, branch, cotangent, o, big, vec, me, shard_rows
        )
        d_scale_mlp, d_fc2_bias, d_gain2, d_shift2, d_scale_attn, d_proj_bias = (totals[i] for i in range(6))
        got1, got2, got3 = (swapped(s, 1, devices) for s in (send1, send2, send3))
        view = (devices // GROUP, 2, 2, shard_rows)
        halves = [
            tuple(s.reshape(*view, -1) for s in pair) for pair in ((keep1, got1), (keep2, got2), (keep3, got3))
        ]
        out_a, out_b = first_sends(halves, me)
    else:
        mlp = mlp + bias_fc2
        block_out = (y1 + layer_mlp * mlp).astype(BF16)
        d_scale_mlp = jnp.sum(g * mlp, axis=0)
        d_gain2 = jnp.sum(dn2 * u2, axis=0)
        d_shift2 = jnp.sum(dn2, axis=0)
        dy1 = g + norm_back(u2, rstd2, dn2 * gain2)
        d_scale_attn = jnp.sum(dy1 * branch, axis=0)
        db = layer_attn * dy1
        d_proj_bias = jnp.sum(db, axis=0)
        dbl = db.astype(BF16)
        d_proj = scattered(t_mm(o, dbl))
        do = mm_t(dbl, w_proj).astype(BF16).reshape(rows, GROUP, -1).transpose(1, 0, 2)

    do_heads = in_plane(do, devices).reshape(span, -1)
    if by_axes:
        do_heads, out_a, out_b = lax.optimization_barrier((do_heads, out_a, out_b))
        in_a, in_b = swapped(out_a, 2, devices), swapped(out_b, 4, devices)
    part_dq, mid0, out_left, out_right = backward_first(prefetch, seg, q, kv, left, right, o_heads, do_heads, lse)
    if by_axes:
        part_dq, in_a, in_b, w_qkv = lax.optimization_barrier((part_dq, in_a, in_b, w_qkv))
        out_a, sum_a, out_b, sum_b = second_sums(halves, in_a, in_b, me)
        part_dq, out_a, out_b = lax.optimization_barrier((part_dq, out_a, out_b))
        in_a, in_b = swapped(out_a, 4, devices), swapped(out_b, 2, devices)
    from_right = shifted(out_left, -GROUP, devices)
    from_left = shifted(out_right, GROUP, devices)
    dq, mid = backward_second(prefetch, seg, q, kv, o_heads, do_heads, lse, part_dq, mid0, edge_blocks)
    dq, mid, from_left, from_right = lax.optimization_barrier((dq, mid, from_left, from_right))
    if by_axes:
        dq, in_a, in_b = lax.optimization_barrier((dq, in_a, in_b))
    if by_axes:
        third = [(s.astype(F32) + i.astype(F32)).astype(BF16) for s, i in ((sum_a, in_a), (sum_b, in_b))]
        own_sums, pieces = plane_pieces(jnp.concatenate(third, axis=-1), me, devices)
        dq, pieces = lax.optimization_barrier((dq, pieces))
        sums = send_planes(pieces, devices)
    d_heads = joined_heads(dq, mid, from_left, from_right)
    dqkv = in_plane(d_heads.reshape(GROUP, rows, -1), devices)
    if by_axes:
        dqkv, n1 = lax.optimization_barrier((dqkv, n1))
    d_qkv = t_mm(n1, d_heads).astype(BF16).reshape(devices // GROUP, GROUP, shard_rows, -1)
    if by_axes:
        dqkv, d_qkv, sums = lax.optimization_barrier((dqkv, d_qkv, sums))
    own_qkv, pieces = plane_pieces(d_qkv, me, devices)
    got_qkv = send_planes(pieces, devices)
    grad_tokens, totals, per_head = input_gradient(dqkv, w_qkv, dy1, tokens, gain1)
    d_gain1, d_shift1, half = totals[0], totals[1], width // GROUP
    d_qv_bias = jnp.concatenate([per_head[:, :half].reshape(-1), per_head[:, 2 * half :].reshape(-1)])
    if by_axes:
        d_gain1, got_qkv = lax.optimization_barrier((d_gain1, got_qkv))
    d_qkv = in_plane(total_of(own_qkv, got_qkv), devices).reshape(GROUP, shard_rows, 3, -1)
    d_qkv = d_qkv.transpose(1, 2, 0, 3).reshape(shard_rows, 3 * width)
    if by_axes:
        sums = total_of(own_sums, sums)
        d_fc1 = sums[:, :hidden]
        cut = width // 2
        at = hidden + cut
        d_fc2 = sums[:, at : at + hidden].reshape(shard_rows, blocks, width).transpose(1, 0, 2)
        d_fc2 = d_fc2.reshape(blocks * shard_rows, width)
        d_proj = jnp.concatenate([sums[:, hidden:at], sums[:, at + hidden :]], axis=1)
    small = (
        d_gain1, d_shift1, d_qv_bias, d_proj_bias, d_scale_attn, d_gain2, d_shift2, d_fc1_bias, d_fc2_bias, d_scale_mlp,
    )
    small = lax.all_to_all(pack(small, devices), "dev", 0, 0, tiled=True)
    small = jnp.sum(small, axis=0, keepdims=True)
    s_gain1, s_shift1, s_qv, s_proj, s_attn, s_gain2, s_shift2, s_fc1, s_fc2, s_mlp = unpack(small, sizes)
    return (
        block_out,
        grad_tokens,
        s_gain1,
        s_shift1,
        d_qkv,
        s_qv,
        d_proj,
        s_proj,
        s_attn,
        s_gain2,
        s_shift2,
        d_fc1,
        s_fc1,
        d_fc2,
        s_fc2,
        s_mlp,
    )


def solution(mesh):
    matrix, vector = P("dev", None), P("dev")
    return jax.shard_map(
        body,
        mesh=mesh,
        in_specs=(
            matrix, matrix, P(), vector, vector, matrix, vector, matrix, vector, vector, vector, vector, matrix,
            vector, matrix, vector, vector,
        ),
        out_specs=(
            matrix, matrix, vector, vector, matrix, vector, matrix, vector, vector, vector, vector, matrix, vector,
            matrix, vector, vector,
        ),
        check_vma=False,
    )
```
